512 devices in a mesh: rows: 32 (over z_lo, y, core), gz: 16 (over z_hi, x).
Axes of the slice: x: 4, y: 4, z: 16 (z_hi: 4, z_lo: 4; z = z_hi * 4 + z_lo), core: 2. Of those that a mesh axis runs over, the one named last changes fastest.
Arguments:
- plane_colour_samples: int32 [32, 3, 1024, 2048], P('gz', None, 'rows'), may hold values from 0 to 255
- clarity_gain: float32 [32], P('gz'), may hold values from 0.01 to 4
Outputs:
- joined: float32 [3, 1024, 2048], P(None, 'rows')
The draws below stay inside these ranges and needn't reach their ends.
All inputs are finite; a program needn't handle non-finite values.
Results may differ from the reference program's by a relative error of at most 0.000067.
Values sent between devices are 32-bit elements; how exact they have to be, the bound alone decides.
No kernel may reach another device: no remote copies, remote signals or barrier semaphores. Data moves between devices by JAX's collectives and lax.ppermute only.
A program may use at most 64 MiB of HBM per device.

```python
import jax
import jax.numpy as jnp
from jax import lax

COLOURS = 3
COLS = 2048
PLANES = 32
HEIGHT = 1024


def draw_clarity_gain(key, part):
    key = jax.random.fold_in(key, 7)
    spread = jax.random.uniform(key, (PLANES,), jnp.float32)
    return jnp.exp(jnp.log(0.01) + spread * (jnp.log(0.1) - jnp.log(0.01)))


def touch_ends(result, stream_key, low, high):
    longest = result.shape.index(max(result.shape))
    spots = []
    for shift in (0, 1):
        where = [jax.random.randint(jax.random.fold_in(stream_key, axis), (), 0, length) for axis, length in enumerate(result.shape)]
        where[longest] = (where[longest] + shift) % result.shape[longest]
        spots.append(tuple(where))
    return result.at[spots[0]].set(low).at[spots[1]].set(high)


def setup_inputs(seed: int = 0) -> dict:
    streams_of = jax.random.split(jax.random.key(seed), 3)
    return {
        "plane_colour_samples": touch_ends(jax.random.randint(streams_of[0], (PLANES, COLOURS, HEIGHT, COLS), 0, 256), jax.random.fold_in(streams_of[0], 1), 0, 255).astype(jnp.int32),
        "clarity_gain": draw_clarity_gain(jax.random.fold_in(streams_of[2], 71), 0),
    }


def pad_rows(field, width):
    return jnp.pad(field, [(0, 0)] * (field.ndim - 2) + [(width, width), (0, 0)])


def blur_rows(padded_image, count):
    return (padded_image[..., 0:count, :] + 4.0 * padded_image[..., 1:count + 1, :] + 6.0 * padded_image[..., 2:count + 2, :]
            + 4.0 * padded_image[..., 3:count + 3, :] + padded_image[..., 4:count + 4, :]) / 16.0


def blur_cols(field):
    count = field.shape[-1]
    padded_image = jnp.pad(field, [(0, 0)] * (field.ndim - 1) + [(2, 2)])
    return (padded_image[..., 0:count] + 4.0 * padded_image[..., 1:count + 1] + 6.0 * padded_image[..., 2:count + 2]
            + 4.0 * padded_image[..., 3:count + 3] + padded_image[..., 4:count + 4]) / 16.0


def upsampled_rows(padded_image, count):
    even = (padded_image[..., 0:count, :] + 6.0 * padded_image[..., 1:count + 1, :] + padded_image[..., 2:count + 2, :]) / 8.0
    odd = (padded_image[..., 1:count + 1, :] + padded_image[..., 2:count + 2, :]) / 2.0
    shape = even.shape[:-2] + (2 * count, even.shape[-1])
    return jnp.stack([even, odd], axis=-2).reshape(shape)


def up_cols(field):
    count = field.shape[-1]
    padded_image = jnp.pad(field, [(0, 0)] * (field.ndim - 1) + [(1, 1)])
    even = (padded_image[..., 0:count] + 6.0 * padded_image[..., 1:count + 1] + padded_image[..., 2:count + 2]) / 8.0
    odd = (padded_image[..., 1:count + 1] + padded_image[..., 2:count + 2]) / 2.0
    shape = field.shape[:-1] + (2 * count,)
    return jnp.stack([even, odd], axis=-1).reshape(shape)


def reduce_level(padded_image, count):
    return blur_cols(blur_rows(padded_image, count))[..., ::2, ::2]


def expand_level(padded_image, count):
    return up_cols(upsampled_rows(padded_image, count))


def plane_energy(plane):
    image = plane.astype(jnp.float32) / 255.0
    grey = 0.299 * image[0] + 0.587 * image[1] + 0.114 * image[2]
    side = jnp.pad(grey, ((1, 1), (1, 1)))
    lap = 4.0 * grey - side[:-2, 1:-1] - side[2:, 1:-1] - side[1:-1, :-2] - side[1:-1, 2:]
    squared = lap * lap
    rows_pad = jnp.pad(squared, ((4, 4), (0, 0)))
    count = squared.shape[0]
    summed = rows_pad[0:count]
    for shift in range(1, 9):
        summed = summed + rows_pad[shift:shift + count]
    cols_pad = jnp.pad(summed, ((0, 0), (4, 4)))
    width = squared.shape[1]
    sharpness_measure_field = cols_pad[:, 0:width]
    for shift in range(1, 9):
        sharpness_measure_field = sharpness_measure_field + cols_pad[:, shift:shift + width]
    return sharpness_measure_field


def reference(plane_colour_samples, clarity_gain):
    height = plane_colour_samples.shape[2]
    sharpness_measure_field = lax.map(plane_energy, plane_colour_samples)
    clarity_ratings = clarity_gain[:, None, None] * sharpness_measure_field
    weights0 = jax.nn.softmax(clarity_ratings, axis=0)

    def accumulate(carry, item):
        plane, weight = item
        image = plane.astype(jnp.float32) / 255.0
        level1 = reduce_level(pad_rows(image, 2), height)
        level2 = reduce_level(pad_rows(level1, 2), height // 2)
        detail0 = image - expand_level(pad_rows(level1, 1), height // 2)
        detail1 = level1 - expand_level(pad_rows(level2, 1), height // 4)
        weight0 = weight[None]
        weight1 = reduce_level(pad_rows(weight0, 2), height)
        weight_level2 = reduce_level(pad_rows(weight1, 2), height // 2)
        return (carry[0] + weight0 * detail0, carry[1] + weight1 * detail1, carry[2] + weight_level2 * level2), None

    start = (jnp.zeros((COLOURS, height, COLS), jnp.float32),
             jnp.zeros((COLOURS, height // 2, COLS // 2), jnp.float32),
             jnp.zeros((COLOURS, height // 4, COLS // 4), jnp.float32))
    blends, unused = lax.scan(accumulate, start, (plane_colour_samples, weights0))
    mixed_finest_band, mixed_coarse_band, blend2 = blends
    central_rows = mixed_coarse_band + expand_level(pad_rows(blend2, 1), height // 4)
    return mixed_finest_band + expand_level(pad_rows(central_rows, 1), height // 2)
```

```python
import jax
import jax.numpy as jnp
import numpy as np
from jax import lax
from jax.experimental import pallas as pl
from jax.experimental.pallas import tpu as pltpu
from jax.sharding import Mesh
from jax.sharding import PartitionSpec as P

ROWS = ("zl", "y", "c")
GZ = ("zh", "x")
BF = jnp.bfloat16
F32 = jnp.float32
HALO = 16
VMEM_BYTES = 56 * 1024 * 1024


def down_taps():
    taps = np.zeros((768, 256), np.float32)
    for n in range(256):
        for k, tap in enumerate((1, 4, 6, 4, 1)):
            taps[2 * n + 126 + k, n] = tap / 16.0
    return taps


def up_taps():
    taps = np.zeros((384, 256), np.float32)
    for n in range(256):
        half = n // 2
        if n % 2 == 0:
            taps[half + 127, n] = 0.125
            taps[half + 128, n] = 0.75
            taps[half + 129, n] = 0.125
        else:
            taps[half + 128, n] = 0.5
            taps[half + 129, n] = 0.5
    return taps


def energy_kernel(strip_ref, main_ref, top_ref, bot_ref, gain_ref, logit_ref, lse_ref, grey_ref):
    rows, wide = grey_ref.shape
    width = main_ref.shape[3]
    first = strip_ref[0] * 32 - HALO
    row = lax.broadcasted_iota(jnp.int32, (rows, wide), 0) + first
    col = lax.broadcasted_iota(jnp.int32, (rows, wide), 1)
    keep = (row >= 0) & (row < 1024) & (col < width)
    grey_ref[:, width:] = jnp.zeros((rows, wide - width), F32)

    def grey_of(ref, p):
        return (
            ref[p, 0].astype(F32) * (0.299 / 255.0)
            + ref[p, 1].astype(F32) * (0.587 / 255.0)
            + ref[p, 2].astype(F32) * (0.114 / 255.0)
        )

    for p in range(2):
        grey_ref[0:16, 0:width] = grey_of(top_ref, p)
        grey_ref[16:48, 0:width] = grey_of(main_ref, p)
        grey_ref[48:64, 0:width] = grey_of(bot_ref, p)
        grey = grey_ref[...]
        lap = (
            4.0 * grey
            - pltpu.roll(grey, 1, 0)
            - pltpu.roll(grey, rows - 1, 0)
            - pltpu.roll(grey, 1, 1)
            - pltpu.roll(grey, wide - 1, 1)
        )
        field = jnp.where(keep, lap * lap, 0.0)
        for axis, size in ((0, rows), (1, wide)):
            two = field + pltpu.roll(field, size - 1, axis)
            four = two + pltpu.roll(two, size - 2, axis)
            eight = four + pltpu.roll(four, size - 4, axis)
            field = pltpu.roll(eight, 4, axis) + pltpu.roll(field, size - 4, axis)
        logit_ref[p] = gain_ref[p] * field[:, 0:width]
    a = logit_ref[0, 16:48]
    b = logit_ref[1, 16:48]
    lse_ref[...] = jnp.maximum(a, b) + jnp.log(1.0 + jnp.exp(-jnp.abs(a - b)))


def split2(value):
    high = value.astype(BF)
    low = (value - high.astype(F32)).astype(BF)
    return high, low


def stacked(value):
    return jnp.concatenate(split2(value), axis=0)


def dot(a, b):
    return jnp.dot(a, b, preferred_element_type=F32)


def iota2(shape):
    return lax.broadcasted_iota(jnp.int32, shape, 0), lax.broadcasted_iota(jnp.int32, shape, 1)


def down_rows(count, inputs, copies, first, limit):
    q, e = iota2((count, inputs * copies))
    for c in range(1, copies):
        e = jnp.where(e >= inputs, e - inputs, e)
    gap = jnp.abs(e - 2 * q)
    taps = jnp.where(gap == 0, 0.375, jnp.where(gap == 1, 0.25, jnp.where(gap == 2, 0.0625, 0.0)))
    inside = (q + first >= 0) & (q + first < limit)
    return jnp.where(inside, taps, 0.0).astype(BF)


def up_rows(count, inputs, offset, first, limit):
    r, q = iota2((count, 2 * inputs))
    q = jnp.where(q >= inputs, q - inputs, q)
    gap = jnp.abs(2 * q - (r + offset))
    even = (r & 1) == 0
    taps = jnp.where(
        even,
        jnp.where(gap == 0, 0.75, jnp.where(gap == 2, 0.125, 0.0)),
        jnp.where(gap == 1, 0.5, 0.0),
    )
    inside = (r + first >= 0) & (r + first < limit)
    return jnp.where(inside, taps, 0.0).astype(BF)


def blend_kernel(
    strip_ref, main_ref, top_ref, bot_ref, logit_ref, lse_ref, lse_top_ref, lse_bot_ref, down_ref, up_ref,
    out_ref, w0_ref, x_ref, s1_ref, l1_ref, s2_ref, l2_ref, s3_ref, c1_ref, s4_ref,
):
    strip = strip_ref[0]
    for ref in (s1_ref, s2_ref, s3_ref, s4_ref):
        edge = jnp.zeros((ref.shape[0], 128), BF)
        ref[:, 0:128] = edge
        ref[:, ref.shape[1] - 128 :] = edge
    v1 = down_rows(32, 64, 1, strip * 16 - 8, 512)
    v1w = down_rows(32, 64, 2, strip * 16 - 8, 512)
    v2 = down_rows(16, 32, 2, strip * 8 - 4, 256)
    p2 = up_rows(32, 16, 0, strip * 16 - 8, 512)
    p1 = up_rows(32, 32, 16, 0, 32)

    def put(ref, n, a, count, value):
        high, low = split2(value)
        width = value.shape[1]
        ref[a * count : (a + 1) * count, 128 : 128 + width] = high
        ref[(n + a) * count : (n + a + 1) * count, 128 : 128 + width] = low

    def row_mask(rows, offset):
        r = lax.broadcasted_iota(jnp.int32, (rows, 2048), 0) + offset
        g = r + strip * 32
        return (r >= -10) & (r <= 42) & (g >= 0) & (g < 1024)

    for p in range(2):
        for lo, count, ref in ((0, 16, lse_top_ref), (16, 32, lse_ref), (48, 16, lse_bot_ref)):
            w0_ref[lo : lo + count] = jnp.where(
                row_mask(count, lo - 16), jnp.exp(logit_ref[p, lo : lo + count] - ref[...]), 0.0
            )
        put(s1_ref, 8, 6 + p, 32, dot(v1w, stacked(w0_ref[...])))
        for c in range(3):
            a = p * 3 + c
            x_ref[0:16] = top_ref[p, c].astype(F32).astype(BF)
            x_ref[16:48] = main_ref[p, c].astype(F32).astype(BF)
            x_ref[48:64] = bot_ref[p, c].astype(F32).astype(BF)
            put(s1_ref, 8, a, 32, dot(v1, x_ref[...]))
    for t in range(4):
        both = dot(s1_ref[:, 512 * t : 512 * t + 768], down_ref[...])
        l1_ref[:, 256 * t : 256 * t + 256] = both[0:256] + both[256:512]
    for a in range(8):
        put(s2_ref, 8, a, 16, dot(v2, stacked(l1_ref[a * 32 : a * 32 + 32])))
    for t in range(2):
        both = dot(s2_ref[:, 512 * t : 512 * t + 768], down_ref[...])
        l2_ref[:, 256 * t : 256 * t + 256] = both[0:128] + both[128:256]
    for a in range(6):
        put(s3_ref, 9, a, 32, dot(p2, stacked(l2_ref[a * 16 : a * 16 + 16])))
    for c in range(3):
        blend2 = l2_ref[96:112] * l2_ref[c * 16 : c * 16 + 16] + l2_ref[112:128] * l2_ref[(3 + c) * 16 : (4 + c) * 16]
        put(s3_ref, 9, 6 + c, 32, dot(p2, stacked(blend2)))
    for t in range(4):
        both = dot(s3_ref[:, 128 * t : 128 * t + 384], up_ref[...])
        part = both[0:288] + both[288:576]
        cols = slice(256 * t, 256 * t + 256)
        for c in range(3):
            total = part[(6 + c) * 32 : (7 + c) * 32]
            for p in range(2):
                a = p * 3 + c
                total = total + l1_ref[(6 + p) * 32 : (7 + p) * 32, cols] * (
                    l1_ref[a * 32 : a * 32 + 32, cols] - part[a * 32 : a * 32 + 32]
                )
            c1_ref[c * 32 : c * 32 + 32, cols] = total
    for a in range(9):
        source = l1_ref[a * 32 : a * 32 + 32] if a < 6 else c1_ref[(a - 6) * 32 : (a - 5) * 32]
        put(s4_ref, 9, a, 32, dot(p1, stacked(source)))
    for t in range(8):
        both = dot(s4_ref[:, 128 * t : 128 * t + 384], up_ref[...])
        part = both[0:288] + both[288:576]
        cols = slice(256 * t, 256 * t + 256)
        weight = [jnp.exp(logit_ref[p, 16:48, cols] - lse_ref[:, cols]) for p in range(2)]
        for c in range(3):
            total = part[(6 + c) * 32 : (7 + c) * 32]
            for p in range(2):
                a = p * 3 + c
                total = total + weight[p] * (main_ref[p, c, :, cols].astype(F32) - part[a * 32 : a * 32 + 32])
            total = total * (1.0 / 255.0)
            for k in range(4):
                out_ref[k, c, :, cols] = total[8 * k : 8 * k + 8]


def vmem(count):
    return [pl.BlockSpec(memory_space=pltpu.VMEM)] * count


def smem():
    return pl.BlockSpec(memory_space=pltpu.SMEM)


def neighbours(low_part, high_part):
    count = lax.axis_size(ROWS)
    forward = [(i, i + 1) for i in range(count - 1)]
    backward = [(i + 1, i) for i in range(count - 1)]
    return lax.ppermute(high_part, ROWS, forward), lax.ppermute(low_part, ROWS, backward)


def pairwise(value, combine):
    half = value.shape[-1] // 2
    left, right = value[..., :half], value[..., half:]
    one = [(i, i ^ 1) for i in range(4)]
    three = [(i, i ^ 3) for i in range(4)]
    for a, b in ((one, three), (three, one)):
        left_in = lax.ppermute(left, "zh", a)
        right_in = lax.ppermute(right, "zh", b)
        left, right = combine(left, left_in), combine(right, right_in)
    return jnp.concatenate([left, right], axis=-1)


def on_device(samples, gain):
    strip = lax.axis_index(ROWS).astype(jnp.int32).reshape(1)
    top, bot = neighbours(samples[:, :, :HALO], samples[:, :, 32 - HALO :])
    logits, lse = pl.pallas_call(
        energy_kernel,
        out_shape=(jax.ShapeDtypeStruct((2, 64, 2048), F32), jax.ShapeDtypeStruct((32, 2048), F32)),
        in_specs=[smem()] + vmem(3) + [smem()],
        out_specs=tuple(vmem(2)),
        scratch_shapes=[pltpu.VMEM((64, 2176), F32)],
        compiler_params=pltpu.CompilerParams(vmem_limit_bytes=VMEM_BYTES),
        name="energy",
    )(strip, samples, top, bot, gain)

    parts = lax.all_to_all(lse.reshape(4, 8, 2048), "x", 0, 0)
    peak = jnp.max(parts, axis=0)
    part = peak + jnp.log(jnp.sum(jnp.exp(parts - peak), axis=0))
    whole = pairwise(part, jnp.logaddexp)
    lse = lax.all_to_all(jnp.broadcast_to(whole, (4, 8, 2048)), "x", 0, 0).reshape(32, 2048)
    lse_top, lse_bot = neighbours(lse[:HALO], lse[32 - HALO :])

    mine = pl.pallas_call(
        blend_kernel,
        out_shape=jax.ShapeDtypeStruct((4, 3, 8, 2048), F32),
        in_specs=[smem()] + vmem(9),
        out_specs=vmem(1)[0],
        scratch_shapes=[
            pltpu.VMEM((64, 2048), F32),
            pltpu.VMEM((64, 2048), BF),
            pltpu.VMEM((512, 2304), BF),
            pltpu.VMEM((256, 1024), F32),
            pltpu.VMEM((256, 1280), BF),
            pltpu.VMEM((128, 512), F32),
            pltpu.VMEM((576, 768), BF),
            pltpu.VMEM((96, 1024), F32),
            pltpu.VMEM((576, 1280), BF),
        ],
        compiler_params=pltpu.CompilerParams(vmem_limit_bytes=VMEM_BYTES),
        name="blend",
    )(strip, samples, top, bot, logits, lse, lse_top, lse_bot, jnp.asarray(down_taps(), BF), jnp.asarray(up_taps(), BF))

    part = jnp.sum(lax.all_to_all(mine, "x", 0, 0), axis=0)
    whole = pairwise(part, jnp.add)
    joined = lax.all_to_all(jnp.broadcast_to(whole, (4, 3, 8, 2048)), "x", 0, 0)
    return joined.transpose(1, 0, 2, 3).reshape(3, 32, 2048)


def solution(mesh):
    fine = Mesh(mesh.devices.reshape(4, 4, 2, 4, 4), ROWS + GZ)
    return jax.shard_map(
        on_device,
        mesh=fine,
        in_specs=(P(GZ, None, ROWS, None), P(GZ)),
        out_specs=P(None, ROWS, None),
        check_vma=False,
    )
```

```python
import functools

import jax
import jax.numpy as jnp
import numpy as np
from jax import lax
from jax.experimental import pallas as pl
from jax.experimental.pallas import tpu as pltpu
from jax.sharding import Mesh
from jax.sharding import PartitionSpec as P

ROWS = ("zl", "y", "c")
GZ = ("zh", "x")
BF = jnp.bfloat16
F32 = jnp.float32
GREY = (0.299 / 255.0, 0.587 / 255.0, 0.114 / 255.0)
W0, W1, W2 = 640, 384, 256
M0, M1, M2 = 512, 256, 128
PARAMS = pltpu.CompilerParams(vmem_limit_bytes=56 * 1024 * 1024)


def lane_of(col, main, wide):
    if 0 <= col < main + 64:
        return col
    if -64 <= col < 0:
        return wide + col
    return None


def column_taps(kind, main_in, wide_in, main_out, wide_out):
    taps = np.zeros((wide_in, wide_out), np.float32)
    for lane in range(wide_out):
        col = lane if lane < main_out + 64 else lane - wide_out
        if kind == "down":
            picks = [(2 * col + d, t / 16.0) for d, t in zip(range(-2, 3), (1, 4, 6, 4, 1))]
        elif col % 2 == 0:
            picks = [(col // 2 - 1, 0.125), (col // 2, 0.75), (col // 2 + 1, 0.125)]
        else:
            picks = [(col // 2, 0.5), (col // 2 + 1, 0.5)]
        for source, tap in picks:
            at = lane_of(source, main_in, wide_in)
            if at is not None:
                taps[at, lane] += tap
    return taps


def pack_kernel(samples_ref, gain_ref, out_ref):
    lane = lax.broadcasted_iota(jnp.int32, (16, 128), 1)
    for j in range(4):
        for h in range(2):
            rows = slice(16 * h, 16 * h + 16)
            tiles = [
                jnp.zeros((16, 128), F32),
                jnp.where(lane < 64, 0.0, jnp.where(lane < 96, gain_ref[0], gain_ref[1])),
            ]
            for a in range(6):
                p, c = divmod(a, 3)
                out_ref[j, h, 16 * a : 16 * a + 16, :] = samples_ref[p, c, rows, 512 * j : 512 * j + 512].astype(F32)
                at, t = 32 * (a % 4), a // 4
                if j > 0:
                    piece = samples_ref[p, c, rows, 512 * j - 128 : 512 * j].astype(F32)
                    piece = pltpu.roll(piece, (at - 112) % 128, 1)
                    tiles[t] = jnp.where((lane >= at) & (lane < at + 16), piece, tiles[t])
                if j < 3:
                    piece = samples_ref[p, c, rows, 512 * j + 512 : 512 * j + 640].astype(F32)
                    piece = pltpu.roll(piece, (at + 16) % 128, 1)
                    tiles[t] = jnp.where((lane >= at + 16) & (lane < at + 32), piece, tiles[t])
            out_ref[j, h, 96:104, 0:128] = tiles[0][0:8]
            out_ref[j, h, 96:104, 128:256] = tiles[1][0:8]
            out_ref[j, h, 96:104, 256:384] = tiles[0][8:16]
            out_ref[j, h, 96:104, 384:512] = tiles[1][8:16]


def blocks_of(main_ref, top_ref, bot_ref, s):
    return (top_ref.at[s], main_ref.at[s, 0], main_ref.at[s, 1], bot_ref.at[s])


def halo_tile(block, a):
    base, at = 128 * (a // 4), 32 * (a % 4)
    tile = jnp.concatenate([block[96:104, base : base + 128], block[96:104, 256 + base : 384 + base]], axis=0)
    lane = lax.broadcasted_iota(jnp.int32, (16, 128), 1)
    return jnp.where((lane < 16) | (lane >= 112), pltpu.roll(tile, (112 - at) % 128, 1), 0.0)


def column_of(shape, main, wide):
    lane = lax.broadcasted_iota(jnp.int32, shape, len(shape) - 1)
    return jnp.where(lane < main + 64, lane, lane - wide)


def energy_kernel(place_ref, main_ref, top_ref, bot_ref, logit_ref, lse_ref, grey_ref):
    row = lax.broadcasted_iota(jnp.int32, (64, W0), 0) + (place_ref[0] * 32 - 16)
    col = column_of((64, W0), M0, W0) + place_ref[1] * M0
    keep = (row >= 0) & (row < 1024) & (col >= 0) & (col < 2048)

    @pl.loop(0, 4)
    def _(s):
        for p in range(2):
            for b, block in enumerate(blocks_of(main_ref, top_ref, bot_ref, s)):
                main = 0.0
                tile = 0.0
                for c in range(3):
                    a = 3 * p + c
                    main = main + block[16 * a : 16 * a + 16, :] * GREY[c]
                    tile = tile + halo_tile(block, a) * GREY[c]
                grey_ref[16 * b : 16 * b + 16, 0:M0] = main
                grey_ref[16 * b : 16 * b + 16, M0:W0] = tile
            grey = grey_ref[...]
            lap = (
                4.0 * grey
                - pltpu.roll(grey, 1, 0)
                - pltpu.roll(grey, 63, 0)
                - pltpu.roll(grey, 1, 1)
                - pltpu.roll(grey, W0 - 1, 1)
            )
            field = jnp.where(keep, lap * lap, 0.0)
            for axis, size in ((0, 64), (1, W0)):
                two = field + pltpu.roll(field, size - 1, axis)
                four = two + pltpu.roll(two, size - 2, axis)
                eight = four + pltpu.roll(four, size - 4, axis)
                field = pltpu.roll(eight, 4, axis) + pltpu.roll(field, size - 4, axis)
            gain = main_ref[s, 0, 96:97, 192 + 32 * p : 193 + 32 * p]
            logit_ref[2 * s + p] = gain * field

    peak = logit_ref[0, 16:48]
    for i in range(1, 8):
        peak = jnp.maximum(peak, logit_ref[i, 16:48])
    total = 0.0
    for i in range(8):
        total = total + jnp.exp(logit_ref[i, 16:48] - peak)
    lse_ref[...] = peak + jnp.log(total)


def split2(value):
    high = value.astype(BF)
    low = (value - high.astype(F32)).astype(BF)
    return high, low


def stacked(value):
    return jnp.concatenate(split2(value), axis=0)


def dot(a, b):
    return jnp.dot(a, b, preferred_element_type=F32)


def iota2(shape):
    return lax.broadcasted_iota(jnp.int32, shape, 0), lax.broadcasted_iota(jnp.int32, shape, 1)


def down_rows(count, inputs, copies, first, limit):
    q, e = iota2((count, inputs * copies))
    if copies == 2:
        e = jnp.where(e >= inputs, e - inputs, e)
    gap = jnp.abs(e - 2 * q)
    taps = jnp.where(gap == 0, 0.375, jnp.where(gap == 1, 0.25, jnp.where(gap == 2, 0.0625, 0.0)))
    inside = (q + first >= 0) & (q + first < limit)
    return jnp.where(inside, taps, 0.0).astype(BF)


def up_rows(count, inputs, offset, first, limit):
    r, q = iota2((count, 2 * inputs))
    q = jnp.where(q >= inputs, q - inputs, q)
    gap = jnp.abs(2 * q - (r + offset))
    even = (r & 1) == 0
    taps = jnp.where(
        even,
        jnp.where(gap == 0, 0.75, jnp.where(gap == 2, 0.125, 0.0)),
        jnp.where(gap == 1, 0.5, 0.0),
    )
    inside = (r + first >= 0) & (r + first < limit)
    return jnp.where(inside, taps, 0.0).astype(BF)


def row_matrices(strip):
    v2 = down_rows(16, 32, 2, strip * 8 - 4, 256)
    p2 = up_rows(32, 16, 0, strip * 16 - 8, 512)
    p1 = up_rows(32, 32, 16, 0, 32)
    return v2, p2, p1


def level_masks(rows1, rows2, k):
    col1 = column_of((rows1, W1), M1, W1) + k * M1
    col2 = column_of((rows2, W2), M2, W2) + k * M2
    return (col1 >= 0) & (col1 < 1024), (col2 >= 0) & (col2 < 512)


def put(ref, n, a, count, value):
    high, low = split2(value)
    ref[a * count : (a + 1) * count] = high
    ref[(n + a) * count : (n + a + 1) * count] = low


def resampled(source_ref, taps_ref):
    both = dot(source_ref[...], taps_ref[...])
    half = both.shape[0] // 2
    return both[:half] + both[half:]


def pyramid_kernel(
    sources, place_ref, main_ref, top_ref, bot_ref, d1_ref, d2_ref, u2_ref, u1_ref,
    detail0_ref, detail1_ref, l2_ref, x_ref, s1_ref, l1_ref, s2_ref, s3_ref, s4_ref,
):
    strip = place_ref[0]
    v1 = down_rows(32, 64, 1, strip * 16 - 8, 512)
    v2, p2, p1 = row_matrices(strip)
    inside1, inside2 = level_masks(192, 96, place_ref[1])
    for i, s in enumerate(sources):
        blocks = blocks_of(main_ref, top_ref, bot_ref, s)
        for a in range(6):
            for b, block in enumerate(blocks):
                x_ref[16 * b : 16 * b + 16, 0:M0] = block[16 * a : 16 * a + 16, :].astype(BF)
                x_ref[16 * b : 16 * b + 16, M0:W0] = halo_tile(block, a).astype(BF)
            put(s1_ref, 6, a, 32, dot(v1, x_ref[...]))
        l1_ref[...] = jnp.where(inside1, resampled(s1_ref, d1_ref), 0.0)
        for a in range(6):
            both = stacked(l1_ref[a * 32 : a * 32 + 32])
            put(s2_ref, 6, a, 16, dot(v2, both))
            put(s4_ref, 6, a, 32, dot(p1, both))
        l2 = jnp.where(inside2, resampled(s2_ref, d2_ref), 0.0)
        l2_ref[i * 96 : i * 96 + 96] = l2
        for a in range(6):
            put(s3_ref, 6, a, 32, dot(p2, stacked(l2[a * 16 : a * 16 + 16])))
        detail1_ref[i * 192 : i * 192 + 192] = l1_ref[...] - resampled(s3_ref, u2_ref)
        part = resampled(s4_ref, u1_ref)
        for a in range(6):
            for h in range(2):
                at = a * 32 + 16 * h
                detail0_ref[i * 192 + at : i * 192 + at + 16] = (
                    main_ref[s, h, 16 * a : 16 * a + 16, :] - part[at : at + 16]
                )


def mix_kernel(
    place_ref, logit_ref, lse_ref, lse_top_ref, lse_bot_ref,
    fine_a_ref, mid_a_ref, low_a_ref, fine_b_ref, mid_b_ref, low_b_ref,
    d1_ref, d2_ref, u2_ref, u1_ref,
    left_ref, right_ref, w0_ref, s1_ref, w1_ref, s2_ref, s3_ref, s4_ref,
):
    strip, k = place_ref[0], place_ref[1]
    v1 = down_rows(32, 64, 2, strip * 16 - 8, 512)
    v2, p2, p1 = row_matrices(strip)
    col = column_of((16, W0), M0, W0)
    inside_col = (col >= -10) & (col <= 522) & (col + k * M0 >= 0) & (col + k * M0 < 2048)
    row = lax.broadcasted_iota(jnp.int32, (16, W0), 0)
    lses = (lse_top_ref[...], lse_ref[0:16], lse_ref[16:32], lse_bot_ref[...])
    keeps = []
    for b in range(4):
        r = row + (16 * b - 16)
        g = r + strip * 32
        keeps.append(inside_col & (r >= -10) & (r <= 42) & (g >= 0) & (g < 1024))
    for i in range(8):
        for b in range(4):
            rows = slice(16 * b, 16 * b + 16)
            w0_ref[i, rows] = jnp.where(keeps[b], jnp.exp(logit_ref[i, rows] - lses[b]), 0.0)
        put(s1_ref, 8, i, 32, dot(v1, stacked(w0_ref[i])))
    inside1, inside2 = level_masks(32, 16, k)
    w1_ref[...] = resampled(s1_ref, d1_ref)
    for i in range(8):
        w1 = jnp.where(inside1, w1_ref[i * 32 : i * 32 + 32], 0.0)
        w1_ref[i * 32 : i * 32 + 32] = w1
        put(s2_ref, 8, i, 16, dot(v2, stacked(w1)))
    w2 = resampled(s2_ref, d2_ref)

    def piece(pair, i, c, rows):
        ref = pair[i // 4]
        at = ((i % 4) * 3 + c) * rows
        return ref[at : at + rows]

    for c in range(3):
        blend2 = 0.0
        for i in range(8):
            blend2 = blend2 + w2[i * 16 : i * 16 + 16] * piece((low_a_ref, low_b_ref), i, c, 16)
        put(s3_ref, 3, c, 32, dot(p2, stacked(blend2)))
    rise = resampled(s3_ref, u2_ref)
    for c in range(3):
        total = jnp.where(inside1, rise[c * 32 : c * 32 + 32], 0.0)
        for i in range(8):
            total = total + w1_ref[i * 32 : i * 32 + 32] * piece((mid_a_ref, mid_b_ref), i, c, 32)
        put(s4_ref, 3, c, 32, dot(p1, stacked(total)))
    rise = resampled(s4_ref, u1_ref)
    for c in range(3):
        total = rise[c * 32 : c * 32 + 32]
        for i in range(8):
            total = total + w0_ref[i, 16:48, 0:M0] * piece((fine_a_ref, fine_b_ref), i, c, 32)
        total = total * (1.0 / 255.0)
        left_ref[c] = total[:, :256]
        right_ref[c] = total[:, 256:]


def vmem(count):
    return [pl.BlockSpec(memory_space=pltpu.VMEM)] * count


def smem():
    return [pl.BlockSpec(memory_space=pltpu.SMEM)]


def neighbours(low_part, high_part):
    count = lax.axis_size(ROWS)
    forward = [(i, i + 1) for i in range(count - 1)]
    backward = [(i + 1, i) for i in range(count - 1)]
    return lax.ppermute(high_part, ROWS, forward), lax.ppermute(low_part, ROWS, backward)


def partner(value, flip):
    return lax.ppermute(value, "zh", [(i, i ^ flip) for i in range(4)])


def join_lse(a, b):
    return jnp.maximum(a, b) + jnp.log(1.0 + jnp.exp(-jnp.abs(a - b)))


def on_device(samples, gain):
    place = jnp.stack([lax.axis_index(ROWS), lax.axis_index("x")]).astype(jnp.int32)
    packed = pl.pallas_call(
        pack_kernel,
        out_shape=jax.ShapeDtypeStruct((4, 2, 104, 512), F32),
        in_specs=vmem(1) + smem(),
        out_specs=vmem(1)[0],
        compiler_params=PARAMS,
        name="pack",
    )(samples, gain)
    main = lax.all_to_all(packed, "x", 0, 0)
    top, bot = neighbours(main[:, 0], main[:, 1])
    logits, lse = pl.pallas_call(
        energy_kernel,
        out_shape=(jax.ShapeDtypeStruct((8, 64, W0), F32), jax.ShapeDtypeStruct((32, W0), F32)),
        in_specs=smem() + vmem(3),
        out_specs=tuple(vmem(2)),
        scratch_shapes=[pltpu.VMEM((64, W0), F32)],
        compiler_params=PARAMS,
        name="energy",
    )(place, main, top, bot)

    taps = [
        jnp.asarray(t, BF)
        for t in (
            column_taps("down", M0, W0, M1, W1),
            column_taps("down", M1, W1, M2, W2),
            column_taps("up", M2, W2, M1, W1),
            column_taps("up", M1, W1, M0, W0)[:, :M0],
        )
    ]
    details = []
    for step, flip in enumerate((1, 3)):
        other = partner(lse, flip)
        detail = pl.pallas_call(
            functools.partial(pyramid_kernel, (2 * step, 2 * step + 1)),
            out_shape=(
                jax.ShapeDtypeStruct((384, M0), F32),
                jax.ShapeDtypeStruct((384, W1), F32),
                jax.ShapeDtypeStruct((192, W2), F32),
            ),
            in_specs=smem() + vmem(7),
            out_specs=tuple(vmem(3)),
            scratch_shapes=[
                pltpu.VMEM((64, W0), BF),
                pltpu.VMEM((384, W0), BF),
                pltpu.VMEM((192, W1), F32),
                pltpu.VMEM((192, W1), BF),
                pltpu.VMEM((384, W2), BF),
                pltpu.VMEM((384, W1), BF),
            ],
            compiler_params=PARAMS,
            cost_estimate=pl.CostEstimate(flops=2_000_000_000, bytes_accessed=6_000_000, transcendentals=0),
            name="pyramid",
        )(place, main, top, bot, *taps)
        other, *detail = lax.optimization_barrier((other, *detail))
        details += detail
        lse = join_lse(lse, other)
    lse_top, lse_bot = neighbours(lse[:16], lse[16:])

    left, right = pl.pallas_call(
        mix_kernel,
        out_shape=(jax.ShapeDtypeStruct((3, 32, 256), F32),) * 2,
        in_specs=smem() + vmem(14),
        out_specs=tuple(vmem(2)),
        scratch_shapes=[
            pltpu.VMEM((8, 64, W0), F32),
            pltpu.VMEM((512, W0), BF),
            pltpu.VMEM((256, W1), F32),
            pltpu.VMEM((256, W1), BF),
            pltpu.VMEM((192, W2), BF),
            pltpu.VMEM((192, W1), BF),
        ],
        compiler_params=PARAMS,
        name="mix",
    )(place, logits, lse, lse_top, lse_bot, *details, *taps)

    for a, b in ((1, 3), (3, 1)):
        left_in, right_in = partner(left, a), partner(right, b)
        left, right = left + left_in, right + right_in
    whole = jnp.concatenate([left, right], axis=-1)
    joined = lax.all_to_all(jnp.broadcast_to(whole, (4, 3, 32, 512)), "x", 0, 0)
    return joined.transpose(1, 2, 0, 3).reshape(3, 32, 2048)


def solution(mesh):
    fine = Mesh(mesh.devices.reshape(4, 4, 2, 4, 4), ROWS + GZ)
    return jax.shard_map(
        on_device,
        mesh=fine,
        in_specs=(P(GZ, None, ROWS, None), P(GZ)),
        out_specs=P(None, ROWS, None),
        check_vma=False,
    )
```

```python
import functools

import jax
import jax.numpy as jnp
import numpy as np
from jax import lax
from jax.experimental import pallas as pl
from jax.experimental.pallas import tpu as pltpu
from jax.sharding import Mesh
from jax.sharding import PartitionSpec as P

ROWS = ("zl", "y", "c")
GZ = ("zh", "x")
BF = jnp.bfloat16
F32 = jnp.float32
GREY = (0.299 / 255.0, 0.587 / 255.0, 0.114 / 255.0)
W0, W1, W2 = 640, 384, 256
M0, M1, M2 = 512, 256, 128
PARAMS = pltpu.CompilerParams(vmem_limit_bytes=20 * 1024 * 1024)


def lane_of(col, main, wide):
    if 0 <= col < main + 64:
        return col
    if -64 <= col < 0:
        return wide + col
    return None


def column_taps(kind, main_in, wide_in, main_out, wide_out):
    taps = np.zeros((wide_in, wide_out), np.float32)
    for lane in range(wide_out):
        col = lane if lane < main_out + 64 else lane - wide_out
        if kind == "down":
            picks = [(2 * col + d, t / 16.0) for d, t in zip(range(-2, 3), (1, 4, 6, 4, 1))]
        elif col % 2 == 0:
            picks = [(col // 2 - 1, 0.125), (col // 2, 0.75), (col // 2 + 1, 0.125)]
        else:
            picks = [(col // 2, 0.5), (col // 2 + 1, 0.5)]
        for source, tap in picks:
            at = lane_of(source, main_in, wide_in)
            if at is not None:
                taps[at, lane] += tap
    return taps


def pack_kernel(samples_ref, gain_ref, out_ref):
    lane = lax.broadcasted_iota(jnp.int32, (16, 128), 1)
    for j in range(4):
        for h in range(2):
            rows = slice(16 * h, 16 * h + 16)
            tiles = [
                jnp.zeros((16, 128), F32),
                jnp.where(lane < 64, 0.0, jnp.where(lane < 96, gain_ref[0], gain_ref[1])),
            ]
            for a in range(6):
                p, c = divmod(a, 3)
                out_ref[j, h, 16 * a : 16 * a + 16, :] = samples_ref[p, c, rows, 512 * j : 512 * j + 512].astype(F32)
                at, t = 32 * (a % 4), a // 4
                if j > 0:
                    piece = samples_ref[p, c, rows, 512 * j - 128 : 512 * j].astype(F32)
                    piece = pltpu.roll(piece, (at - 112) % 128, 1)
                    tiles[t] = jnp.where((lane >= at) & (lane < at + 16), piece, tiles[t])
                if j < 3:
                    piece = samples_ref[p, c, rows, 512 * j + 512 : 512 * j + 640].astype(F32)
                    piece = pltpu.roll(piece, (at + 16) % 128, 1)
                    tiles[t] = jnp.where((lane >= at + 16) & (lane < at + 32), piece, tiles[t])
            out_ref[j, h, 96:104, 0:128] = tiles[0][0:8]
            out_ref[j, h, 96:104, 128:256] = tiles[1][0:8]
            out_ref[j, h, 96:104, 256:384] = tiles[0][8:16]
            out_ref[j, h, 96:104, 384:512] = tiles[1][8:16]


def blocks_of(main_ref, top_ref, bot_ref, s):
    return (top_ref.at[s], main_ref.at[s, 0], main_ref.at[s, 1], bot_ref.at[s])


def halo_tile(block, a):
    base, at = 128 * (a // 4), 32 * (a % 4)
    tile = jnp.concatenate([block[96:104, base : base + 128], block[96:104, 256 + base : 384 + base]], axis=0)
    lane = lax.broadcasted_iota(jnp.int32, (16, 128), 1)
    return jnp.where((lane < 16) | (lane >= 112), pltpu.roll(tile, (112 - at) % 128, 1), 0.0)


def column_of(shape, main, wide):
    lane = lax.broadcasted_iota(jnp.int32, shape, len(shape) - 1)
    return jnp.where(lane < main + 64, lane, lane - wide)


def energy_kernel(place_ref, main_ref, top_ref, bot_ref, logit_ref, lse_ref, grey_ref):
    row = lax.broadcasted_iota(jnp.int32, (64, W0), 0) + (place_ref[0] * 32 - 16)
    col = column_of((64, W0), M0, W0) + place_ref[1] * M0
    keep = (row >= 0) & (row < 1024) & (col >= 0) & (col < 2048)

    @pl.loop(0, 4)
    def _(s):
        for p in range(2):
            for b, block in enumerate(blocks_of(main_ref, top_ref, bot_ref, s)):
                main = 0.0
                tile = 0.0
                for c in range(3):
                    a = 3 * p + c
                    main = main + block[16 * a : 16 * a + 16, :] * GREY[c]
                    tile = tile + halo_tile(block, a) * GREY[c]
                grey_ref[16 * b : 16 * b + 16, 0:M0] = main
                grey_ref[16 * b : 16 * b + 16, M0:W0] = tile
            grey = grey_ref[...]
            lap = (
                4.0 * grey
                - pltpu.roll(grey, 1, 0)
                - pltpu.roll(grey, 63, 0)
                - pltpu.roll(grey, 1, 1)
                - pltpu.roll(grey, W0 - 1, 1)
            )
            field = jnp.where(keep, lap * lap, 0.0)
            for axis, size in ((0, 64), (1, W0)):
                two = field + pltpu.roll(field, size - 1, axis)
                four = two + pltpu.roll(two, size - 2, axis)
                eight = four + pltpu.roll(four, size - 4, axis)
                field = pltpu.roll(eight, 4, axis) + pltpu.roll(field, size - 4, axis)
            gain = main_ref[s, 0, 96:97, 192 + 32 * p : 193 + 32 * p]
            logit_ref[2 * s + p] = gain * field

    peak = logit_ref[0, 16:48]
    for i in range(1, 8):
        peak = jnp.maximum(peak, logit_ref[i, 16:48])
    total = 0.0
    for i in range(8):
        total = total + jnp.exp(logit_ref[i, 16:48] - peak)
    lse_ref[...] = peak + jnp.log(total)


def split2(value):
    high = value.astype(BF)
    low = (value - high.astype(F32)).astype(BF)
    return high, low


def stacked(value):
    return jnp.concatenate(split2(value), axis=0)


def dot(a, b):
    return jnp.dot(a, b, preferred_element_type=F32)


def iota2(shape):
    return lax.broadcasted_iota(jnp.int32, shape, 0), lax.broadcasted_iota(jnp.int32, shape, 1)


def down_rows(count, inputs, copies, first, limit):
    q, e = iota2((count, inputs * copies))
    if copies == 2:
        e = jnp.where(e >= inputs, e - inputs, e)
    gap = jnp.abs(e - 2 * q)
    taps = jnp.where(gap == 0, 0.375, jnp.where(gap == 1, 0.25, jnp.where(gap == 2, 0.0625, 0.0)))
    inside = (q + first >= 0) & (q + first < limit)
    return jnp.where(inside, taps, 0.0).astype(BF)


def up_rows(count, inputs, offset, first, limit):
    r, q = iota2((count, 2 * inputs))
    q = jnp.where(q >= inputs, q - inputs, q)
    gap = jnp.abs(2 * q - (r + offset))
    even = (r & 1) == 0
    taps = jnp.where(
        even,
        jnp.where(gap == 0, 0.75, jnp.where(gap == 2, 0.125, 0.0)),
        jnp.where(gap == 1, 0.5, 0.0),
    )
    inside = (r + first >= 0) & (r + first < limit)
    return jnp.where(inside, taps, 0.0).astype(BF)


def row_matrices(strip):
    v2 = down_rows(16, 32, 2, strip * 8 - 4, 256)
    p2 = up_rows(32, 16, 0, strip * 16 - 8, 512)
    p1 = up_rows(32, 32, 16, 0, 32)
    return v2, p2, p1


def level_masks(rows1, rows2, k):
    col1 = column_of((rows1, W1), M1, W1) + k * M1
    col2 = column_of((rows2, W2), M2, W2) + k * M2
    return (col1 >= 0) & (col1 < 1024), (col2 >= 0) & (col2 < 512)


def put(ref, n, a, count, value):
    high, low = split2(value)
    ref[a * count : (a + 1) * count] = high
    ref[(n + a) * count : (n + a + 1) * count] = low


def resampled(source_ref, taps_ref):
    both = dot(source_ref[...], taps_ref[...])
    half = both.shape[0] // 2
    return both[:half] + both[half:]


def pyramid_kernel(
    sources, place_ref, main_ref, top_ref, bot_ref, d1_ref, d2_ref, u2_ref, u1_ref,
    detail0_ref, detail1_ref, l2_ref, x_ref, s1_ref, l1_ref, s2_ref, s3_ref, s4_ref,
):
    strip = place_ref[0]
    v1 = down_rows(32, 64, 1, strip * 16 - 8, 512)
    v2, p2, p1 = row_matrices(strip)
    inside1, inside2 = level_masks(192, 96, place_ref[1])
    for i, s in enumerate(sources):
        blocks = blocks_of(main_ref, top_ref, bot_ref, s)
        for a in range(6):
            for b, block in enumerate(blocks):
                x_ref[16 * b : 16 * b + 16, 0:M0] = block[16 * a : 16 * a + 16, :].astype(BF)
                x_ref[16 * b : 16 * b + 16, M0:W0] = halo_tile(block, a).astype(BF)
            put(s1_ref, 6, a, 32, dot(v1, x_ref[...]))
        l1_ref[...] = jnp.where(inside1, resampled(s1_ref, d1_ref), 0.0)
        for a in range(6):
            both = stacked(l1_ref[a * 32 : a * 32 + 32])
            put(s2_ref, 6, a, 16, dot(v2, both))
            put(s4_ref, 6, a, 32, dot(p1, both))
        l2 = jnp.where(inside2, resampled(s2_ref, d2_ref), 0.0)
        l2_ref[i * 96 : i * 96 + 96] = l2
        for a in range(6):
            put(s3_ref, 6, a, 32, dot(p2, stacked(l2[a * 16 : a * 16 + 16])))
        detail1_ref[i * 192 : i * 192 + 192] = l1_ref[...] - resampled(s3_ref, u2_ref)
        part = resampled(s4_ref, u1_ref)
        for a in range(6):
            for h in range(2):
                at = a * 32 + 16 * h
                detail0_ref[i * 192 + at : i * 192 + at + 16] = (
                    main_ref[s, h, 16 * a : 16 * a + 16, :] - part[at : at + 16]
                )


def mix_kernel(
    place_ref, logit_ref, lse_ref, lse_top_ref, lse_bot_ref,
    fine_a_ref, mid_a_ref, low_a_ref, fine_b_ref, mid_b_ref, low_b_ref,
    d1_ref, d2_ref, u2_ref, u1_ref,
    left_ref, right_ref, w0_ref, s1_ref, w1_ref, s2_ref, s3_ref, s4_ref,
):
    strip, k = place_ref[0], place_ref[1]
    v1 = down_rows(32, 64, 2, strip * 16 - 8, 512)
    v2, p2, p1 = row_matrices(strip)
    col = column_of((16, W0), M0, W0)
    inside_col = (col >= -10) & (col <= 522) & (col + k * M0 >= 0) & (col + k * M0 < 2048)
    row = lax.broadcasted_iota(jnp.int32, (16, W0), 0)
    lses = (lse_top_ref[...], lse_ref[0:16], lse_ref[16:32], lse_bot_ref[...])
    keeps = []
    for b in range(4):
        r = row + (16 * b - 16)
        g = r + strip * 32
        keeps.append(inside_col & (r >= -10) & (r <= 42) & (g >= 0) & (g < 1024))
    for i in range(8):
        for b in range(4):
            rows = slice(16 * b, 16 * b + 16)
            w0_ref[i, rows] = jnp.where(keeps[b], jnp.exp(logit_ref[i, rows] - lses[b]), 0.0)
        put(s1_ref, 8, i, 32, dot(v1, stacked(w0_ref[i])))
    inside1, inside2 = level_masks(32, 16, k)
    w1_ref[...] = resampled(s1_ref, d1_ref)
    for i in range(8):
        w1 = jnp.where(inside1, w1_ref[i * 32 : i * 32 + 32], 0.0)
        w1_ref[i * 32 : i * 32 + 32] = w1
        put(s2_ref, 8, i, 16, dot(v2, stacked(w1)))
    w2 = resampled(s2_ref, d2_ref)

    def piece(pair, i, c, rows):
        ref = pair[i // 4]
        at = ((i % 4) * 3 + c) * rows
        return ref[at : at + rows]

    for c in range(3):
        blend2 = 0.0
        for i in range(8):
            blend2 = blend2 + w2[i * 16 : i * 16 + 16] * piece((low_a_ref, low_b_ref), i, c, 16)
        put(s3_ref, 3, c, 32, dot(p2, stacked(blend2)))
    rise = resampled(s3_ref, u2_ref)
    for c in range(3):
        total = jnp.where(inside1, rise[c * 32 : c * 32 + 32], 0.0)
        for i in range(8):
            total = total + w1_ref[i * 32 : i * 32 + 32] * piece((mid_a_ref, mid_b_ref), i, c, 32)
        put(s4_ref, 3, c, 32, dot(p1, stacked(total)))
    rise = resampled(s4_ref, u1_ref)
    for c in range(3):
        total = rise[c * 32 : c * 32 + 32]
        for i in range(8):
            total = total + w0_ref[i, 16:48, 0:M0] * piece((fine_a_ref, fine_b_ref), i, c, 32)
        total = total * (1.0 / 255.0)
        left_ref[c] = total[:, :256]
        right_ref[c] = total[:, 256:]


def vmem(count):
    return [pl.BlockSpec(memory_space=pltpu.VMEM)] * count


def smem():
    return [pl.BlockSpec(memory_space=pltpu.SMEM)]


def neighbours(low_part, high_part):
    count = lax.axis_size(ROWS)
    forward = [(i, i + 1) for i in range(count - 1)]
    backward = [(i + 1, i) for i in range(count - 1)]
    return lax.ppermute(high_part, ROWS, forward), lax.ppermute(low_part, ROWS, backward)


def partner(value, flip):
    return lax.ppermute(value, "zh", [(i, i ^ flip) for i in range(4)])


def join_lse(a, b):
    return jnp.maximum(a, b) + jnp.log(1.0 + jnp.exp(-jnp.abs(a - b)))


def on_device(samples, gain):
    place = jnp.stack([lax.axis_index(ROWS), lax.axis_index("x")]).astype(jnp.int32)
    packed = pl.pallas_call(
        pack_kernel,
        out_shape=jax.ShapeDtypeStruct((4, 2, 104, 512), F32),
        in_specs=vmem(1) + smem(),
        out_specs=vmem(1)[0],
        compiler_params=PARAMS,
        name="pack",
    )(samples, gain)
    main = lax.all_to_all(packed, "x", 0, 0)
    top, bot = neighbours(main[:, 0], main[:, 1])
    logits, lse = pl.pallas_call(
        energy_kernel,
        out_shape=(jax.ShapeDtypeStruct((8, 64, W0), F32), jax.ShapeDtypeStruct((32, W0), F32)),
        in_specs=smem() + vmem(3),
        out_specs=tuple(vmem(2)),
        scratch_shapes=[pltpu.VMEM((64, W0), F32)],
        compiler_params=PARAMS,
        name="energy",
    )(place, main, top, bot)

    taps = [
        jnp.asarray(t, BF)
        for t in (
            column_taps("down", M0, W0, M1, W1),
            column_taps("down", M1, W1, M2, W2),
            column_taps("up", M2, W2, M1, W1),
            column_taps("up", M1, W1, M0, W0)[:, :M0],
        )
    ]
    parts = lax.all_to_all(jnp.broadcast_to(lse, (4, 32, W0)), "zh", 0, 0)
    details = []
    for step, flip in enumerate((1, 3)):
        detail = pl.pallas_call(
            functools.partial(pyramid_kernel, (2 * step, 2 * step + 1)),
            out_shape=(
                jax.ShapeDtypeStruct((384, M0), F32),
                jax.ShapeDtypeStruct((384, W1), F32),
                jax.ShapeDtypeStruct((192, W2), F32),
            ),
            in_specs=smem() + vmem(7),
            out_specs=tuple(vmem(3)),
            scratch_shapes=[
                pltpu.VMEM((64, W0), BF),
                pltpu.VMEM((384, W0), BF),
                pltpu.VMEM((192, W1), F32),
                pltpu.VMEM((192, W1), BF),
                pltpu.VMEM((384, W2), BF),
                pltpu.VMEM((384, W1), BF),
            ],
            compiler_params=PARAMS,
            cost_estimate=pl.CostEstimate(flops=2_000_000_000, bytes_accessed=6_000_000, transcendentals=0),
            name="pyramid",
        )(place, main, top, bot, *taps)
        details += detail
    parts, *details = lax.optimization_barrier((parts, *details))
    peak = jnp.max(parts, axis=0)
    lse = peak + jnp.log(jnp.sum(jnp.exp(parts - peak), axis=0))
    lse_top, lse_bot = neighbours(lse[:16], lse[16:])

    left, right = pl.pallas_call(
        mix_kernel,
        out_shape=(jax.ShapeDtypeStruct((3, 32, 256), F32),) * 2,
        in_specs=smem() + vmem(14),
        out_specs=tuple(vmem(2)),
        scratch_shapes=[
            pltpu.VMEM((8, 64, W0), F32),
            pltpu.VMEM((512, W0), BF),
            pltpu.VMEM((256, W1), F32),
            pltpu.VMEM((256, W1), BF),
            pltpu.VMEM((192, W2), BF),
            pltpu.VMEM((192, W1), BF),
        ],
        compiler_params=PARAMS,
        name="mix",
    )(place, logits, lse, lse_top, lse_bot, *details, *taps)

    for a, b in ((1, 3), (3, 1)):
        left_in, right_in = partner(left, a), partner(right, b)
        left, right = left + left_in, right + right_in
    whole = jnp.concatenate([left, right], axis=-1)
    joined = lax.all_to_all(jnp.broadcast_to(whole, (4, 3, 32, 512)), "x", 0, 0)
    return joined.transpose(1, 2, 0, 3).reshape(3, 32, 2048)


def solution(mesh):
    fine = Mesh(mesh.devices.reshape(4, 4, 2, 4, 4), ROWS + GZ)
    return jax.shard_map(
        on_device,
        mesh=fine,
        in_specs=(P(GZ, None, ROWS, None), P(GZ)),
        out_specs=P(None, ROWS, None),
        check_vma=False,
    )
```

```python
import functools

import jax
import jax.numpy as jnp
import numpy as np
from jax import lax
from jax.experimental import pallas as pl
from jax.experimental.pallas import tpu as pltpu
from jax.sharding import Mesh
from jax.sharding import PartitionSpec as P

ROWS = ("zl", "y", "c")
GZ = ("zh", "x")
BF = jnp.bfloat16
F32 = jnp.float32
GREY = (0.299 / 255.0, 0.587 / 255.0, 0.114 / 255.0)
W0, W1, W2 = 640, 384, 256
M0, M1, M2 = 512, 256, 128
PARAMS = pltpu.CompilerParams(vmem_limit_bytes=20 * 1024 * 1024)


def lane_of(col, main, wide):
    if 0 <= col < main + 64:
        return col
    if -64 <= col < 0:
        return wide + col
    return None


def column_taps(kind, main_in, wide_in, main_out, wide_out):
    taps = np.zeros((wide_in, wide_out), np.float32)
    for lane in range(wide_out):
        col = lane if lane < main_out + 64 else lane - wide_out
        if kind == "down":
            picks = [(2 * col + d, t / 16.0) for d, t in zip(range(-2, 3), (1, 4, 6, 4, 1))]
        elif col % 2 == 0:
            picks = [(col // 2 - 1, 0.125), (col // 2, 0.75), (col // 2 + 1, 0.125)]
        else:
            picks = [(col // 2, 0.5), (col // 2 + 1, 0.5)]
        for source, tap in picks:
            at = lane_of(source, main_in, wide_in)
            if at is not None:
                taps[at, lane] += tap
    return taps


def pack_kernel(samples_ref, gain_ref, out_ref):
    lane = lax.broadcasted_iota(jnp.int32, (16, 128), 1)
    for j in range(4):
        for h in range(2):
            rows = slice(16 * h, 16 * h + 16)
            tiles = [
                jnp.zeros((16, 128), F32),
                jnp.where(lane < 64, 0.0, jnp.where(lane < 96, gain_ref[0], gain_ref[1])),
            ]
            for a in range(6):
                p, c = divmod(a, 3)
                out_ref[j, h, 16 * a : 16 * a + 16, :] = samples_ref[p, c, rows, 512 * j : 512 * j + 512].astype(F32)
                at, t = 32 * (a % 4), a // 4
                if j > 0:
                    piece = samples_ref[p, c, rows, 512 * j - 128 : 512 * j].astype(F32)
                    piece = pltpu.roll(piece, (at - 112) % 128, 1)
                    tiles[t] = jnp.where((lane >= at) & (lane < at + 16), piece, tiles[t])
                if j < 3:
                    piece = samples_ref[p, c, rows, 512 * j + 512 : 512 * j + 640].astype(F32)
                    piece = pltpu.roll(piece, (at + 16) % 128, 1)
                    tiles[t] = jnp.where((lane >= at + 16) & (lane < at + 32), piece, tiles[t])
            out_ref[j, h, 96:104, 0:128] = tiles[0][0:8]
            out_ref[j, h, 96:104, 128:256] = tiles[1][0:8]
            out_ref[j, h, 96:104, 256:384] = tiles[0][8:16]
            out_ref[j, h, 96:104, 384:512] = tiles[1][8:16]


def blocks_of(main_ref, top_ref, bot_ref, s):
    return (top_ref.at[s], main_ref.at[s, 0], main_ref.at[s, 1], bot_ref.at[s])


def halo_tile(block, a):
    base, at = 128 * (a // 4), 32 * (a % 4)
    tile = jnp.concatenate([block[96:104, base : base + 128], block[96:104, 256 + base : 384 + base]], axis=0)
    lane = lax.broadcasted_iota(jnp.int32, (16, 128), 1)
    return jnp.where((lane < 16) | (lane >= 112), pltpu.roll(tile, (112 - at) % 128, 1), 0.0)


def column_of(shape, main, wide):
    lane = lax.broadcasted_iota(jnp.int32, shape, len(shape) - 1)
    return jnp.where(lane < main + 64, lane, lane - wide)


def energy_kernel(place_ref, main_ref, top_ref, bot_ref, logit_ref, lse_ref, grey_ref):
    row = lax.broadcasted_iota(jnp.int32, (64, W0), 0) + (place_ref[0] * 32 - 16)
    col = column_of((64, W0), M0, W0) + place_ref[1] * M0
    keep = (row >= 0) & (row < 1024) & (col >= 0) & (col < 2048)

    @pl.loop(0, 4)
    def _(s):
        for p in range(2):
            for b, block in enumerate(blocks_of(main_ref, top_ref, bot_ref, s)):
                main = 0.0
                tile = 0.0
                for c in range(3):
                    a = 3 * p + c
                    main = main + block[16 * a : 16 * a + 16, :] * GREY[c]
                    tile = tile + halo_tile(block, a) * GREY[c]
                grey_ref[16 * b : 16 * b + 16, 0:M0] = main
                grey_ref[16 * b : 16 * b + 16, M0:W0] = tile
            grey = grey_ref[...]
            lap = (
                4.0 * grey
                - pltpu.roll(grey, 1, 0)
                - pltpu.roll(grey, 63, 0)
                - pltpu.roll(grey, 1, 1)
                - pltpu.roll(grey, W0 - 1, 1)
            )
            field = jnp.where(keep, lap * lap, 0.0)
            for axis, size in ((0, 64), (1, W0)):
                two = field + pltpu.roll(field, size - 1, axis)
                four = two + pltpu.roll(two, size - 2, axis)
                eight = four + pltpu.roll(four, size - 4, axis)
                field = pltpu.roll(eight, 4, axis) + pltpu.roll(field, size - 4, axis)
            gain = main_ref[s, 0, 96:97, 192 + 32 * p : 193 + 32 * p]
            logit_ref[2 * s + p] = gain * field

    peak = logit_ref[0, 16:48]
    for i in range(1, 8):
        peak = jnp.maximum(peak, logit_ref[i, 16:48])
    total = 0.0
    for i in range(8):
        total = total + jnp.exp(logit_ref[i, 16:48] - peak)
    lse_ref[...] = peak + jnp.log(total)


def split2(value):
    high = value.astype(BF)
    low = (value - high.astype(F32)).astype(BF)
    return high, low


def stacked(value):
    return jnp.concatenate(split2(value), axis=0)


def dot(a, b):
    return jnp.dot(a, b, preferred_element_type=F32)


def iota2(shape):
    return lax.broadcasted_iota(jnp.int32, shape, 0), lax.broadcasted_iota(jnp.int32, shape, 1)


def down_rows(count, inputs, copies, first, limit):
    q, e = iota2((count, inputs * copies))
    if copies == 2:
        e = jnp.where(e >= inputs, e - inputs, e)
    gap = jnp.abs(e - 2 * q)
    taps = jnp.where(gap == 0, 0.375, jnp.where(gap == 1, 0.25, jnp.where(gap == 2, 0.0625, 0.0)))
    inside = (q + first >= 0) & (q + first < limit)
    return jnp.where(inside, taps, 0.0).astype(BF)


def up_rows(count, inputs, offset, first, limit):
    r, q = iota2((count, 2 * inputs))
    q = jnp.where(q >= inputs, q - inputs, q)
    gap = jnp.abs(2 * q - (r + offset))
    even = (r & 1) == 0
    taps = jnp.where(
        even,
        jnp.where(gap == 0, 0.75, jnp.where(gap == 2, 0.125, 0.0)),
        jnp.where(gap == 1, 0.5, 0.0),
    )
    inside = (r + first >= 0) & (r + first < limit)
    return jnp.where(inside, taps, 0.0).astype(BF)


def row_matrices(strip):
    v2 = down_rows(16, 32, 2, strip * 8 - 4, 256)
    p2 = up_rows(32, 16, 0, strip * 16 - 8, 512)
    p1 = up_rows(32, 32, 16, 0, 32)
    return v2, p2, p1


def level_masks(rows1, rows2, k):
    col1 = column_of((rows1, W1), M1, W1) + k * M1
    col2 = column_of((rows2, W2), M2, W2) + k * M2
    return (col1 >= 0) & (col1 < 1024), (col2 >= 0) & (col2 < 512)


def put(ref, n, a, count, value):
    high, low = split2(value)
    ref[a * count : (a + 1) * count] = high
    ref[(n + a) * count : (n + a + 1) * count] = low


def resampled(source_ref, taps_ref):
    both = dot(source_ref[...], taps_ref[...])
    half = both.shape[0] // 2
    return both[:half] + both[half:]


def pyramid_kernel(
    sources, place_ref, main_ref, top_ref, bot_ref, d1_ref, d2_ref, u2_ref, u1_ref,
    detail0_ref, detail1_ref, l2_ref, x_ref, s1_ref, l1_ref, s2_ref, s3_ref, s4_ref,
):
    strip = place_ref[0]
    v1 = down_rows(32, 64, 1, strip * 16 - 8, 512)
    v2, p2, p1 = row_matrices(strip)
    inside1, inside2 = level_masks(192, 96, place_ref[1])
    for i, s in enumerate(sources):
        blocks = blocks_of(main_ref, top_ref, bot_ref, s)
        for a in range(6):
            for b, block in enumerate(blocks):
                x_ref[16 * b : 16 * b + 16, 0:M0] = block[16 * a : 16 * a + 16, :].astype(BF)
                x_ref[16 * b : 16 * b + 16, M0:W0] = halo_tile(block, a).astype(BF)
            put(s1_ref, 6, a, 32, dot(v1, x_ref[...]))
        l1_ref[...] = jnp.where(inside1, resampled(s1_ref, d1_ref), 0.0)
        for a in range(6):
            both = stacked(l1_ref[a * 32 : a * 32 + 32])
            put(s2_ref, 6, a, 16, dot(v2, both))
            put(s4_ref, 6, a, 32, dot(p1, both))
        l2 = jnp.where(inside2, resampled(s2_ref, d2_ref), 0.0)
        l2_ref[i * 96 : i * 96 + 96] = l2
        for a in range(6):
            put(s3_ref, 6, a, 32, dot(p2, stacked(l2[a * 16 : a * 16 + 16])))
        detail1_ref[i * 192 : i * 192 + 192] = l1_ref[...] - resampled(s3_ref, u2_ref)
        part = resampled(s4_ref, u1_ref)
        for a in range(6):
            for h in range(2):
                at = a * 32 + 16 * h
                detail0_ref[i * 192 + at : i * 192 + at + 16] = (
                    main_ref[s, h, 16 * a : 16 * a + 16, :] - part[at : at + 16]
                )


def mix_kernel(
    place_ref, logit_ref, lse_ref, lse_top_ref, lse_bot_ref,
    fine_a_ref, mid_a_ref, low_a_ref, fine_b_ref, mid_b_ref, low_b_ref,
    d1_ref, d2_ref, u2_ref, u1_ref,
    left_ref, right_ref, w0_ref, s1_ref, w1_ref, s2_ref, s3_ref, s4_ref,
):
    strip, k = place_ref[0], place_ref[1]
    v1 = down_rows(32, 64, 2, strip * 16 - 8, 512)
    v2, p2, p1 = row_matrices(strip)
    col = column_of((16, W0), M0, W0)
    inside_col = (col >= -10) & (col <= 522) & (col + k * M0 >= 0) & (col + k * M0 < 2048)
    row = lax.broadcasted_iota(jnp.int32, (16, W0), 0)
    lses = (lse_top_ref[...], lse_ref[0:16], lse_ref[16:32], lse_bot_ref[...])
    keeps = []
    for b in range(4):
        r = row + (16 * b - 16)
        g = r + strip * 32
        keeps.append(inside_col & (r >= -10) & (r <= 42) & (g >= 0) & (g < 1024))
    for i in range(8):
        for b in range(4):
            rows = slice(16 * b, 16 * b + 16)
            w0_ref[i, rows] = jnp.where(keeps[b], jnp.exp(logit_ref[i, rows] - lses[b]), 0.0)
        put(s1_ref, 8, i, 32, dot(v1, stacked(w0_ref[i])))
    inside1, inside2 = level_masks(32, 16, k)
    w1_ref[...] = resampled(s1_ref, d1_ref)
    for i in range(8):
        w1 = jnp.where(inside1, w1_ref[i * 32 : i * 32 + 32], 0.0)
        w1_ref[i * 32 : i * 32 + 32] = w1
        put(s2_ref, 8, i, 16, dot(v2, stacked(w1)))
    w2 = resampled(s2_ref, d2_ref)

    def piece(pair, i, c, rows):
        ref = pair[i // 4]
        at = ((i % 4) * 3 + c) * rows
        return ref[at : at + rows]

    for c in range(3):
        blend2 = 0.0
        for i in range(8):
            blend2 = blend2 + w2[i * 16 : i * 16 + 16] * piece((low_a_ref, low_b_ref), i, c, 16)
        put(s3_ref, 3, c, 32, dot(p2, stacked(blend2)))
    rise = resampled(s3_ref, u2_ref)
    for c in range(3):
        total = jnp.where(inside1, rise[c * 32 : c * 32 + 32], 0.0)
        for i in range(8):
            total = total + w1_ref[i * 32 : i * 32 + 32] * piece((mid_a_ref, mid_b_ref), i, c, 32)
        put(s4_ref, 3, c, 32, dot(p1, stacked(total)))
    rise = resampled(s4_ref, u1_ref)
    for c in range(3):
        total = rise[c * 32 : c * 32 + 32]
        for i in range(8):
            total = total + w0_ref[i, 16:48, 0:M0] * piece((fine_a_ref, fine_b_ref), i, c, 32)
        total = total * (1.0 / 255.0)
        left_ref[c] = total[:, :256]
        right_ref[c] = total[:, 256:]


def vmem(count):
    return [pl.BlockSpec(memory_space=pltpu.VMEM)] * count


def smem():
    return [pl.BlockSpec(memory_space=pltpu.SMEM)]


def neighbours(low_part, high_part):
    count = lax.axis_size(ROWS)
    forward = [(i, i + 1) for i in range(count - 1)]
    backward = [(i + 1, i) for i in range(count - 1)]
    return lax.ppermute(high_part, ROWS, forward), lax.ppermute(low_part, ROWS, backward)


def partner(value, flip):
    return lax.ppermute(value, "zh", [(i, i ^ flip) for i in range(4)])


def join_lse(a, b):
    return jnp.maximum(a, b) + jnp.log(1.0 + jnp.exp(-jnp.abs(a - b)))


def on_device(samples, gain):
    place = jnp.stack([lax.axis_index(ROWS), lax.axis_index("x")]).astype(jnp.int32)
    packed = pl.pallas_call(
        pack_kernel,
        out_shape=jax.ShapeDtypeStruct((4, 2, 104, 512), F32),
        in_specs=vmem(1) + smem(),
        out_specs=vmem(1)[0],
        compiler_params=PARAMS,
        name="pack",
    )(samples, gain)
    main = lax.all_to_all(packed, "x", 0, 0)
    top, bot = neighbours(main[:, 0], main[:, 1])
    logits, lse = pl.pallas_call(
        energy_kernel,
        out_shape=(jax.ShapeDtypeStruct((8, 64, W0), F32), jax.ShapeDtypeStruct((32, W0), F32)),
        in_specs=smem() + vmem(3),
        out_specs=tuple(vmem(2)),
        scratch_shapes=[pltpu.VMEM((64, W0), F32)],
        compiler_params=PARAMS,
        name="energy",
    )(place, main, top, bot)

    taps = [
        jnp.asarray(t, BF)
        for t in (
            column_taps("down", M0, W0, M1, W1),
            column_taps("down", M1, W1, M2, W2),
            column_taps("up", M2, W2, M1, W1),
            column_taps("up", M1, W1, M0, W0)[:, :M0],
        )
    ]
    details = []
    for step, flip in enumerate((1, 3)):
        other = partner(lse, flip)
        detail = pl.pallas_call(
            functools.partial(pyramid_kernel, (2 * step, 2 * step + 1)),
            out_shape=(
                jax.ShapeDtypeStruct((384, M0), F32),
                jax.ShapeDtypeStruct((384, W1), F32),
                jax.ShapeDtypeStruct((192, W2), F32),
            ),
            in_specs=smem() + vmem(7),
            out_specs=tuple(vmem(3)),
            scratch_shapes=[
                pltpu.VMEM((64, W0), BF),
                pltpu.VMEM((384, W0), BF),
                pltpu.VMEM((192, W1), F32),
                pltpu.VMEM((192, W1), BF),
                pltpu.VMEM((384, W2), BF),
                pltpu.VMEM((384, W1), BF),
            ],
            compiler_params=PARAMS,
            cost_estimate=pl.CostEstimate(flops=2_000_000_000, bytes_accessed=6_000_000, transcendentals=0),
            name="pyramid",
        )(place, main, top, bot, *taps)
        other, *detail = lax.optimization_barrier((other, *detail))
        details += detail
        lse = join_lse(lse, other)
    lse_top, lse_bot = neighbours(lse[:16], lse[16:])

    left, right = pl.pallas_call(
        mix_kernel,
        out_shape=(jax.ShapeDtypeStruct((3, 32, 256), F32),) * 2,
        in_specs=smem() + vmem(14),
        out_specs=tuple(vmem(2)),
        scratch_shapes=[
            pltpu.VMEM((8, 64, W0), F32),
            pltpu.VMEM((512, W0), BF),
            pltpu.VMEM((256, W1), F32),
            pltpu.VMEM((256, W1), BF),
            pltpu.VMEM((192, W2), BF),
            pltpu.VMEM((192, W1), BF),
        ],
        compiler_params=PARAMS,
        name="mix",
    )(place, logits, lse, lse_top, lse_bot, *details, *taps)

    for a, b in ((1, 3), (3, 1)):
        left_in, right_in = partner(left, a), partner(right, b)
        left, right = left + left_in, right + right_in
    whole = jnp.concatenate([left, right], axis=-1)
    joined = lax.all_to_all(jnp.broadcast_to(whole, (4, 3, 32, 512)), "x", 0, 0)
    return joined.transpose(1, 2, 0, 3).reshape(3, 32, 2048)


def solution(mesh):
    fine = Mesh(mesh.devices.reshape(4, 4, 2, 4, 4), ROWS + GZ)
    return jax.shard_map(
        on_device,
        mesh=fine,
        in_specs=(P(GZ, None, ROWS, None), P(GZ)),
        out_specs=P(None, ROWS, None),
        check_vma=False,
    )
```

```python
import functools

import jax
import jax.numpy as jnp
import numpy as np
from jax import lax
from jax.experimental import pallas as pl
from jax.experimental.pallas import tpu as pltpu
from jax.sharding import Mesh
from jax.sharding import PartitionSpec as P

ROWS = ("zl", "y", "c")
GZ = ("zh", "x")
BF = jnp.bfloat16
F32 = jnp.float32
GREY = (0.299 / 255.0, 0.587 / 255.0, 0.114 / 255.0)
W0, W1, W2 = 640, 384, 256
M0, M1, M2 = 512, 256, 128
PARAMS = pltpu.CompilerParams(vmem_limit_bytes=20 * 1024 * 1024)


def lane_of(col, main, wide):
    if 0 <= col < main + 64:
        return col
    if -64 <= col < 0:
        return wide + col
    return None


def column_taps(kind, main_in, wide_in, main_out, wide_out):
    taps = np.zeros((wide_in, wide_out), np.float32)
    for lane in range(wide_out):
        col = lane if lane < main_out + 64 else lane - wide_out
        if kind == "down":
            picks = [(2 * col + d, t / 16.0) for d, t in zip(range(-2, 3), (1, 4, 6, 4, 1))]
        elif col % 2 == 0:
            picks = [(col // 2 - 1, 0.125), (col // 2, 0.75), (col // 2 + 1, 0.125)]
        else:
            picks = [(col // 2, 0.5), (col // 2 + 1, 0.5)]
        for source, tap in picks:
            at = lane_of(source, main_in, wide_in)
            if at is not None:
                taps[at, lane] += tap
    return taps


def pack_kernel(samples_ref, gain_ref, out_ref):
    lane = lax.broadcasted_iota(jnp.int32, (16, 128), 1)
    for j in range(4):
        for h in range(2):
            rows = slice(16 * h, 16 * h + 16)
            tiles = [
                jnp.zeros((16, 128), F32),
                jnp.where(lane < 64, 0.0, jnp.where(lane < 96, gain_ref[0], gain_ref[1])),
            ]
            for a in range(6):
                p, c = divmod(a, 3)
                out_ref[j, h, 16 * a : 16 * a + 16, :] = samples_ref[p, c, rows, 512 * j : 512 * j + 512].astype(F32)
                at, t = 32 * (a % 4), a // 4
                if j > 0:
                    piece = samples_ref[p, c, rows, 512 * j - 128 : 512 * j].astype(F32)
                    piece = pltpu.roll(piece, (at - 112) % 128, 1)
                    tiles[t] = jnp.where((lane >= at) & (lane < at + 16), piece, tiles[t])
                if j < 3:
                    piece = samples_ref[p, c, rows, 512 * j + 512 : 512 * j + 640].astype(F32)
                    piece = pltpu.roll(piece, (at + 16) % 128, 1)
                    tiles[t] = jnp.where((lane >= at + 16) & (lane < at + 32), piece, tiles[t])
            out_ref[j, h, 96:104, 0:128] = tiles[0][0:8]
            out_ref[j, h, 96:104, 128:256] = tiles[1][0:8]
            out_ref[j, h, 96:104, 256:384] = tiles[0][8:16]
            out_ref[j, h, 96:104, 384:512] = tiles[1][8:16]


class Strips:
    def __init__(self, place_ref, main_ref, near_ref, far_ref):
        self.even = place_ref[2] == 0
        self.main, self.near, self.far = main_ref, near_ref, far_ref

    def get(self, s, b, rows, cols):
        if b in (1, 2):
            return self.main[s, b - 1, rows, cols]
        near, far = self.near[s, rows, cols], self.far[s, rows, cols]
        return jnp.where(self.even, far, near) if b == 0 else jnp.where(self.even, near, far)

    def samples(self, s, b, a):
        return self.get(s, b, slice(16 * a, 16 * a + 16), slice(0, M0))

    def halo(self, s, b, a):
        return halo_tile(lambda cols: self.get(s, b, slice(96, 104), cols), a)


def halo_tile(read, a):
    base, at = 128 * (a // 4), 32 * (a % 4)
    tile = jnp.concatenate([read(slice(base, base + 128)), read(slice(256 + base, 384 + base))], axis=0)
    lane = lax.broadcasted_iota(jnp.int32, (16, 128), 1)
    return jnp.where((lane < 16) | (lane >= 112), pltpu.roll(tile, (112 - at) % 128, 1), 0.0)


def column_of(shape, main, wide):
    lane = lax.broadcasted_iota(jnp.int32, shape, len(shape) - 1)
    return jnp.where(lane < main + 64, lane, lane - wide)


def energy_kernel(place_ref, main_ref, near_ref, far_ref, logit_ref, lse_ref, grey_ref):
    row = lax.broadcasted_iota(jnp.int32, (64, W0), 0) + (place_ref[0] * 32 - 16)
    col = column_of((64, W0), M0, W0) + place_ref[1] * M0
    keep = (row >= 0) & (row < 1024) & (col >= 0) & (col < 2048)

    strips = Strips(place_ref, main_ref, near_ref, far_ref)

    @pl.loop(0, 4)
    def _(s):
        for p in range(2):
            for b in range(4):
                main = 0.0
                tile = 0.0
                for c in range(3):
                    a = 3 * p + c
                    main = main + strips.samples(s, b, a) * GREY[c]
                    tile = tile + strips.halo(s, b, a) * GREY[c]
                grey_ref[16 * b : 16 * b + 16, 0:M0] = main
                grey_ref[16 * b : 16 * b + 16, M0:W0] = tile
            grey = grey_ref[...]
            lap = (
                4.0 * grey
                - pltpu.roll(grey, 1, 0)
                - pltpu.roll(grey, 63, 0)
                - pltpu.roll(grey, 1, 1)
                - pltpu.roll(grey, W0 - 1, 1)
            )
            field = jnp.where(keep, lap * lap, 0.0)
            for axis, size in ((0, 64), (1, W0)):
                two = field + pltpu.roll(field, size - 1, axis)
                four = two + pltpu.roll(two, size - 2, axis)
                eight = four + pltpu.roll(four, size - 4, axis)
                field = pltpu.roll(eight, 4, axis) + pltpu.roll(field, size - 4, axis)
            gain = main_ref[s, 0, 96:97, 192 + 32 * p : 193 + 32 * p]
            logit_ref[2 * s + p] = gain * field

    peak = logit_ref[0, 16:48]
    for i in range(1, 8):
        peak = jnp.maximum(peak, logit_ref[i, 16:48])
    total = 0.0
    for i in range(8):
        total = total + jnp.exp(logit_ref[i, 16:48] - peak)
    lse_ref[...] = peak + jnp.log(total)


def split2(value):
    high = value.astype(BF)
    low = (value - high.astype(F32)).astype(BF)
    return high, low


def stacked(value):
    return jnp.concatenate(split2(value), axis=0)


def dot(a, b):
    return jnp.dot(a, b, preferred_element_type=F32)


def iota2(shape):
    return lax.broadcasted_iota(jnp.int32, shape, 0), lax.broadcasted_iota(jnp.int32, shape, 1)


def down_rows(count, inputs, copies, first, limit):
    q, e = iota2((count, inputs * copies))
    if copies == 2:
        e = jnp.where(e >= inputs, e - inputs, e)
    gap = jnp.abs(e - 2 * q)
    taps = jnp.where(gap == 0, 0.375, jnp.where(gap == 1, 0.25, jnp.where(gap == 2, 0.0625, 0.0)))
    inside = (q + first >= 0) & (q + first < limit)
    return jnp.where(inside, taps, 0.0).astype(BF)


def up_rows(count, inputs, offset, first, limit):
    r, q = iota2((count, 2 * inputs))
    q = jnp.where(q >= inputs, q - inputs, q)
    gap = jnp.abs(2 * q - (r + offset))
    even = (r & 1) == 0
    taps = jnp.where(
        even,
        jnp.where(gap == 0, 0.75, jnp.where(gap == 2, 0.125, 0.0)),
        jnp.where(gap == 1, 0.5, 0.0),
    )
    inside = (r + first >= 0) & (r + first < limit)
    return jnp.where(inside, taps, 0.0).astype(BF)


def row_matrices(strip):
    v2 = down_rows(16, 32, 2, strip * 8 - 4, 256)
    p2 = up_rows(32, 16, 0, strip * 16 - 8, 512)
    p1 = up_rows(32, 32, 16, 0, 32)
    return v2, p2, p1


def level_masks(rows1, rows2, k):
    col1 = column_of((rows1, W1), M1, W1) + k * M1
    col2 = column_of((rows2, W2), M2, W2) + k * M2
    return (col1 >= 0) & (col1 < 1024), (col2 >= 0) & (col2 < 512)


def put(ref, n, a, count, value):
    high, low = split2(value)
    ref[a * count : (a + 1) * count] = high
    ref[(n + a) * count : (n + a + 1) * count] = low


def resampled(source_ref, taps_ref):
    both = dot(source_ref[...], taps_ref[...])
    half = both.shape[0] // 2
    return both[:half] + both[half:]


def pyramid_kernel(
    sources, place_ref, main_ref, near_ref, far_ref, d1_ref, d2_ref, u2_ref, u1_ref,
    detail0_ref, detail1_ref, l2_ref, x_ref, s1_ref, l1_ref, s2_ref, s3_ref, s4_ref,
):
    strip = place_ref[0]
    v1 = down_rows(32, 64, 1, strip * 16 - 8, 512)
    v2, p2, p1 = row_matrices(strip)
    inside1, inside2 = level_masks(192, 96, place_ref[1])
    strips = Strips(place_ref, main_ref, near_ref, far_ref)
    for i, s in enumerate(sources):
        for a in range(6):
            for b in range(4):
                x_ref[16 * b : 16 * b + 16, 0:M0] = strips.samples(s, b, a).astype(BF)
                x_ref[16 * b : 16 * b + 16, M0:W0] = strips.halo(s, b, a).astype(BF)
            put(s1_ref, 6, a, 32, dot(v1, x_ref[...]))
        l1_ref[...] = jnp.where(inside1, resampled(s1_ref, d1_ref), 0.0)
        for a in range(6):
            both = stacked(l1_ref[a * 32 : a * 32 + 32])
            put(s2_ref, 6, a, 16, dot(v2, both))
            put(s4_ref, 6, a, 32, dot(p1, both))
        l2 = jnp.where(inside2, resampled(s2_ref, d2_ref), 0.0)
        l2_ref[i * 96 : i * 96 + 96] = l2
        for a in range(6):
            put(s3_ref, 6, a, 32, dot(p2, stacked(l2[a * 16 : a * 16 + 16])))
        detail1_ref[i * 192 : i * 192 + 192] = l1_ref[...] - resampled(s3_ref, u2_ref)
        part = resampled(s4_ref, u1_ref)
        for a in range(6):
            for h in range(2):
                at = a * 32 + 16 * h
                detail0_ref[i * 192 + at : i * 192 + at + 16] = (
                    main_ref[s, h, 16 * a : 16 * a + 16, :] - part[at : at + 16]
                )


def mix_kernel(
    place_ref, logit_ref, lse_ref, near_ref, far_ref,
    fine_a_ref, mid_a_ref, low_a_ref, fine_b_ref, mid_b_ref, low_b_ref,
    d1_ref, d2_ref, u2_ref, u1_ref,
    left_ref, right_ref, w0_ref, s1_ref, w1_ref, s2_ref, s3_ref, s4_ref,
):
    strip, k = place_ref[0], place_ref[1]
    v1 = down_rows(32, 64, 2, strip * 16 - 8, 512)
    v2, p2, p1 = row_matrices(strip)
    col = column_of((16, W0), M0, W0)
    inside_col = (col >= -10) & (col <= 522) & (col + k * M0 >= 0) & (col + k * M0 < 2048)
    row = lax.broadcasted_iota(jnp.int32, (16, W0), 0)
    even = place_ref[2] == 0
    lses = (
        jnp.where(even, far_ref[...], near_ref[...]),
        lse_ref[0:16],
        lse_ref[16:32],
        jnp.where(even, near_ref[...], far_ref[...]),
    )
    keeps = []
    for b in range(4):
        r = row + (16 * b - 16)
        g = r + strip * 32
        keeps.append(inside_col & (r >= -10) & (r <= 42) & (g >= 0) & (g < 1024))
    for i in range(8):
        for b in range(4):
            rows = slice(16 * b, 16 * b + 16)
            w0_ref[i, rows] = jnp.where(keeps[b], jnp.exp(logit_ref[i, rows] - lses[b]), 0.0)
        put(s1_ref, 8, i, 32, dot(v1, stacked(w0_ref[i])))
    inside1, inside2 = level_masks(32, 16, k)
    w1_ref[...] = resampled(s1_ref, d1_ref)
    for i in range(8):
        w1 = jnp.where(inside1, w1_ref[i * 32 : i * 32 + 32], 0.0)
        w1_ref[i * 32 : i * 32 + 32] = w1
        put(s2_ref, 8, i, 16, dot(v2, stacked(w1)))
    w2 = resampled(s2_ref, d2_ref)

    def piece(pair, i, c, rows):
        ref = pair[i // 4]
        at = ((i % 4) * 3 + c) * rows
        return ref[at : at + rows]

    for c in range(3):
        blend2 = 0.0
        for i in range(8):
            blend2 = blend2 + w2[i * 16 : i * 16 + 16] * piece((low_a_ref, low_b_ref), i, c, 16)
        put(s3_ref, 3, c, 32, dot(p2, stacked(blend2)))
    rise = resampled(s3_ref, u2_ref)
    for c in range(3):
        total = jnp.where(inside1, rise[c * 32 : c * 32 + 32], 0.0)
        for i in range(8):
            total = total + w1_ref[i * 32 : i * 32 + 32] * piece((mid_a_ref, mid_b_ref), i, c, 32)
        put(s4_ref, 3, c, 32, dot(p1, stacked(total)))
    rise = resampled(s4_ref, u1_ref)
    for c in range(3):
        total = rise[c * 32 : c * 32 + 32]
        for i in range(8):
            total = total + w0_ref[i, 16:48, 0:M0] * piece((fine_a_ref, fine_b_ref), i, c, 32)
        total = total * (1.0 / 255.0)
        left_ref[c] = total[:, :256]
        right_ref[c] = total[:, 256:]


def vmem(count):
    return [pl.BlockSpec(memory_space=pltpu.VMEM)] * count


def smem():
    return [pl.BlockSpec(memory_space=pltpu.SMEM)]


def neighbours(halves, core):
    count = lax.axis_size(ROWS)
    swaps = [(i, i + 1) for i in range(1, count - 1, 2)]
    swaps += [(b, a) for a, b in swaps]
    pick = functools.partial(lax.dynamic_index_in_dim, halves, axis=-3, keepdims=False)
    near = lax.ppermute(pick(1 - core), "c", [(0, 1), (1, 0)])
    far = lax.ppermute(pick(core), ROWS, swaps)
    return near, far


def partner(value, flip):
    return lax.ppermute(value, "zh", [(i, i ^ flip) for i in range(4)])


def crossed(value, flips):
    pairs = [(4 * c + i, 4 * c + (i ^ flip)) for c, flip in enumerate(flips) for i in range(4)]
    return lax.ppermute(value, ("c", "zh"), pairs)


def join_lse(a, b):
    return jnp.maximum(a, b) + jnp.log(1.0 + jnp.exp(-jnp.abs(a - b)))


def on_device(samples, gain):
    samples, strip, column, core = lax.optimization_barrier(
        (samples, lax.axis_index(ROWS), lax.axis_index("x"), lax.axis_index("c"))
    )
    packed = pl.pallas_call(
        pack_kernel,
        out_shape=jax.ShapeDtypeStruct((4, 2, 104, 512), F32),
        in_specs=vmem(1) + smem(),
        out_specs=vmem(1)[0],
        compiler_params=PARAMS,
        name="pack",
    )(samples, gain)
    main = lax.all_to_all(packed, "x", 0, 0)
    main, strip, column, core = lax.optimization_barrier((main, strip, column, core))
    near, far = neighbours(main, core)
    place = jnp.stack([strip, column, core]).astype(jnp.int32)
    logits, lse = pl.pallas_call(
        energy_kernel,
        out_shape=(jax.ShapeDtypeStruct((8, 64, W0), F32), jax.ShapeDtypeStruct((32, W0), F32)),
        in_specs=smem() + vmem(3),
        out_specs=tuple(vmem(2)),
        scratch_shapes=[pltpu.VMEM((64, W0), F32)],
        compiler_params=PARAMS,
        name="energy",
    )(place, main, near, far)

    taps = [
        jnp.asarray(t, BF)
        for t in (
            column_taps("down", M0, W0, M1, W1),
            column_taps("down", M1, W1, M2, W2),
            column_taps("up", M2, W2, M1, W1),
            column_taps("up", M1, W1, M0, W0)[:, :M0],
        )
    ]
    details = []
    for step, flips in enumerate(((1, 3), (3, 1))):
        other = crossed(lse, flips)
        detail = pl.pallas_call(
            functools.partial(pyramid_kernel, (2 * step, 2 * step + 1)),
            out_shape=(
                jax.ShapeDtypeStruct((384, M0), F32),
                jax.ShapeDtypeStruct((384, W1), F32),
                jax.ShapeDtypeStruct((192, W2), F32),
            ),
            in_specs=smem() + vmem(7),
            out_specs=tuple(vmem(3)),
            scratch_shapes=[
                pltpu.VMEM((64, W0), BF),
                pltpu.VMEM((384, W0), BF),
                pltpu.VMEM((192, W1), F32),
                pltpu.VMEM((192, W1), BF),
                pltpu.VMEM((384, W2), BF),
                pltpu.VMEM((384, W1), BF),
            ],
            compiler_params=PARAMS,
            cost_estimate=pl.CostEstimate(flops=2_000_000_000, bytes_accessed=6_000_000, transcendentals=0),
            name="pyramid",
        )(place, main, near, far, *taps)
        other, *detail = lax.optimization_barrier((other, *detail))
        details += detail
        lse = join_lse(lse, other)
    lse_near, lse_far = neighbours(lse.reshape(2, 16, W0), core)

    left, right = pl.pallas_call(
        mix_kernel,
        out_shape=(jax.ShapeDtypeStruct((3, 32, 256), F32),) * 2,
        in_specs=smem() + vmem(14),
        out_specs=tuple(vmem(2)),
        scratch_shapes=[
            pltpu.VMEM((8, 64, W0), F32),
            pltpu.VMEM((512, W0), BF),
            pltpu.VMEM((256, W1), F32),
            pltpu.VMEM((256, W1), BF),
            pltpu.VMEM((192, W2), BF),
            pltpu.VMEM((192, W1), BF),
        ],
        compiler_params=PARAMS,
        name="mix",
    )(place, logits, lse, lse_near, lse_far, *details, *taps)

    for a, b in ((1, 3), (3, 1)):
        left_in, right_in = partner(left, a), partner(right, b)
        left, right = left + left_in, right + right_in
    whole = jnp.concatenate([left, right], axis=-1)
    joined = lax.all_to_all(jnp.broadcast_to(whole, (4, 3, 32, 512)), "x", 0, 0)
    return joined.transpose(1, 2, 0, 3).reshape(3, 32, 2048)


def solution(mesh):
    fine = Mesh(mesh.devices.reshape(4, 4, 2, 4, 4), ROWS + GZ)
    return jax.shard_map(
        on_device,
        mesh=fine,
        in_specs=(P(GZ, None, ROWS, None), P(GZ)),
        out_specs=P(None, ROWS, None),
        check_vma=False,
    )
```

```python
import functools

import jax
import jax.numpy as jnp
import numpy as np
from jax import lax
from jax.experimental import pallas as pl
from jax.experimental.pallas import tpu as pltpu
from jax.sharding import Mesh
from jax.sharding import PartitionSpec as P

ROWS = ("zl", "y", "c")
GZ = ("zh", "x")
BF = jnp.bfloat16
F32 = jnp.float32
GREY = (0.299 / 255.0, 0.587 / 255.0, 0.114 / 255.0)
W0, W1, W2 = 640, 384, 256
M0, M1, M2 = 512, 256, 128
PARAMS = pltpu.CompilerParams(vmem_limit_bytes=20 * 1024 * 1024)


def lane_of(col, main, wide):
    if 0 <= col < main + 64:
        return col
    if -64 <= col < 0:
        return wide + col
    return None


def column_taps(kind, main_in, wide_in, main_out, wide_out):
    taps = np.zeros((wide_in, wide_out), np.float32)
    for lane in range(wide_out):
        col = lane if lane < main_out + 64 else lane - wide_out
        if kind == "down":
            picks = [(2 * col + d, t / 16.0) for d, t in zip(range(-2, 3), (1, 4, 6, 4, 1))]
        elif col % 2 == 0:
            picks = [(col // 2 - 1, 0.125), (col // 2, 0.75), (col // 2 + 1, 0.125)]
        else:
            picks = [(col // 2, 0.5), (col // 2 + 1, 0.5)]
        for source, tap in picks:
            at = lane_of(source, main_in, wide_in)
            if at is not None:
                taps[at, lane] += tap
    return taps


def pack_kernel(samples_ref, gain_ref, out_ref):
    lane = lax.broadcasted_iota(jnp.int32, (16, 128), 1)
    for j in range(4):
        for h in range(2):
            rows = slice(16 * h, 16 * h + 16)
            tiles = [
                jnp.zeros((16, 128), F32),
                jnp.where(lane < 64, 0.0, jnp.where(lane < 96, gain_ref[0], gain_ref[1])),
            ]
            for a in range(6):
                p, c = divmod(a, 3)
                out_ref[j, h, 16 * a : 16 * a + 16, :] = samples_ref[p, c, rows, 512 * j : 512 * j + 512].astype(F32)
                at, t = 32 * (a % 4), a // 4
                if j > 0:
                    piece = samples_ref[p, c, rows, 512 * j - 128 : 512 * j].astype(F32)
                    piece = pltpu.roll(piece, (at - 112) % 128, 1)
                    tiles[t] = jnp.where((lane >= at) & (lane < at + 16), piece, tiles[t])
                if j < 3:
                    piece = samples_ref[p, c, rows, 512 * j + 512 : 512 * j + 640].astype(F32)
                    piece = pltpu.roll(piece, (at + 16) % 128, 1)
                    tiles[t] = jnp.where((lane >= at + 16) & (lane < at + 32), piece, tiles[t])
            out_ref[j, h, 96:104, 0:128] = tiles[0][0:8]
            out_ref[j, h, 96:104, 128:256] = tiles[1][0:8]
            out_ref[j, h, 96:104, 256:384] = tiles[0][8:16]
            out_ref[j, h, 96:104, 384:512] = tiles[1][8:16]


class Strips:
    def __init__(self, place_ref, main_ref, near_ref, far_ref):
        self.even = place_ref[2] == 0
        self.main, self.near, self.far = main_ref, near_ref, far_ref

    def get(self, s, b, rows, cols):
        if b in (1, 2):
            return self.main[s, b - 1, rows, cols]
        near, far = self.near[s, rows, cols], self.far[s, rows, cols]
        return jnp.where(self.even, far, near) if b == 0 else jnp.where(self.even, near, far)

    def samples(self, s, b, a):
        return self.get(s, b, slice(16 * a, 16 * a + 16), slice(0, M0))

    def halo(self, s, b, a):
        return halo_tile(lambda cols: self.get(s, b, slice(96, 104), cols), a)


def halo_tile(read, a):
    base, at = 128 * (a // 4), 32 * (a % 4)
    tile = jnp.concatenate([read(slice(base, base + 128)), read(slice(256 + base, 384 + base))], axis=0)
    lane = lax.broadcasted_iota(jnp.int32, (16, 128), 1)
    return jnp.where((lane < 16) | (lane >= 112), pltpu.roll(tile, (112 - at) % 128, 1), 0.0)


def column_of(shape, main, wide):
    lane = lax.broadcasted_iota(jnp.int32, shape, len(shape) - 1)
    return jnp.where(lane < main + 64, lane, lane - wide)


def energy_kernel(place_ref, main_ref, near_ref, far_ref, logit_ref, lse_ref, grey_ref):
    row = lax.broadcasted_iota(jnp.int32, (64, W0), 0) + (place_ref[0] * 32 - 16)
    col = column_of((64, W0), M0, W0) + place_ref[1] * M0
    keep = (row >= 0) & (row < 1024) & (col >= 0) & (col < 2048)

    strips = Strips(place_ref, main_ref, near_ref, far_ref)

    @pl.loop(0, 4)
    def _(s):
        for p in range(2):
            for b in range(4):
                main = 0.0
                tile = 0.0
                for c in range(3):
                    a = 3 * p + c
                    main = main + strips.samples(s, b, a) * GREY[c]
                    tile = tile + strips.halo(s, b, a) * GREY[c]
                grey_ref[16 * b : 16 * b + 16, 0:M0] = main
                grey_ref[16 * b : 16 * b + 16, M0:W0] = tile
            grey = grey_ref[...]
            lap = (
                4.0 * grey
                - pltpu.roll(grey, 1, 0)
                - pltpu.roll(grey, 63, 0)
                - pltpu.roll(grey, 1, 1)
                - pltpu.roll(grey, W0 - 1, 1)
            )
            field = jnp.where(keep, lap * lap, 0.0)
            for axis, size in ((0, 64), (1, W0)):
                two = field + pltpu.roll(field, size - 1, axis)
                four = two + pltpu.roll(two, size - 2, axis)
                eight = four + pltpu.roll(four, size - 4, axis)
                field = pltpu.roll(eight, 4, axis) + pltpu.roll(field, size - 4, axis)
            gain = main_ref[s, 0, 96:97, 192 + 32 * p : 193 + 32 * p]
            logit_ref[2 * s + p] = gain * field

    peak = logit_ref[0]
    for i in range(1, 8):
        peak = jnp.maximum(peak, logit_ref[i])
    total = 0.0
    for i in range(8):
        total = total + jnp.exp(logit_ref[i] - peak)
    lse_ref[...] = pltpu.roll(peak + jnp.log(total), 58, 0)[0:56]


def split2(value):
    high = value.astype(BF)
    low = (value - high.astype(F32)).astype(BF)
    return high, low


def stacked(value):
    return jnp.concatenate(split2(value), axis=0)


def dot(a, b):
    return jnp.dot(a, b, preferred_element_type=F32)


def iota2(shape):
    return lax.broadcasted_iota(jnp.int32, shape, 0), lax.broadcasted_iota(jnp.int32, shape, 1)


def down_rows(count, inputs, copies, first, limit):
    q, e = iota2((count, inputs * copies))
    if copies == 2:
        e = jnp.where(e >= inputs, e - inputs, e)
    gap = jnp.abs(e - 2 * q)
    taps = jnp.where(gap == 0, 0.375, jnp.where(gap == 1, 0.25, jnp.where(gap == 2, 0.0625, 0.0)))
    inside = (q + first >= 0) & (q + first < limit)
    return jnp.where(inside, taps, 0.0).astype(BF)


def up_rows(count, inputs, offset, first, limit):
    r, q = iota2((count, 2 * inputs))
    q = jnp.where(q >= inputs, q - inputs, q)
    gap = jnp.abs(2 * q - (r + offset))
    even = (r & 1) == 0
    taps = jnp.where(
        even,
        jnp.where(gap == 0, 0.75, jnp.where(gap == 2, 0.125, 0.0)),
        jnp.where(gap == 1, 0.5, 0.0),
    )
    inside = (r + first >= 0) & (r + first < limit)
    return jnp.where(inside, taps, 0.0).astype(BF)


def row_matrices(strip):
    v2 = down_rows(16, 32, 2, strip * 8 - 4, 256)
    p2 = up_rows(32, 16, 0, strip * 16 - 8, 512)
    p1 = up_rows(32, 32, 16, 0, 32)
    return v2, p2, p1


def level_masks(rows1, rows2, k):
    col1 = column_of((rows1, W1), M1, W1) + k * M1
    col2 = column_of((rows2, W2), M2, W2) + k * M2
    return (col1 >= 0) & (col1 < 1024), (col2 >= 0) & (col2 < 512)


def put(ref, n, a, count, value):
    high, low = split2(value)
    ref[a * count : (a + 1) * count] = high
    ref[(n + a) * count : (n + a + 1) * count] = low


def resampled(source_ref, taps_ref):
    both = dot(source_ref[...], taps_ref[...])
    half = both.shape[0] // 2
    return both[:half] + both[half:]


def pyramid_kernel(
    sources, place_ref, main_ref, near_ref, far_ref, d1_ref, d2_ref, u2_ref, u1_ref,
    detail0_ref, detail1_ref, l2_ref, x_ref, s1_ref, l1_ref, s2_ref, s3_ref, s4_ref,
):
    strip = place_ref[0]
    v1 = down_rows(32, 64, 1, strip * 16 - 8, 512)
    v2, p2, p1 = row_matrices(strip)
    inside1, inside2 = level_masks(192, 96, place_ref[1])
    strips = Strips(place_ref, main_ref, near_ref, far_ref)
    for i, s in enumerate(sources):
        for a in range(6):
            for b in range(4):
                x_ref[16 * b : 16 * b + 16, 0:M0] = strips.samples(s, b, a).astype(BF)
                x_ref[16 * b : 16 * b + 16, M0:W0] = strips.halo(s, b, a).astype(BF)
            put(s1_ref, 6, a, 32, dot(v1, x_ref[...]))
        l1_ref[...] = jnp.where(inside1, resampled(s1_ref, d1_ref), 0.0)
        for a in range(6):
            both = stacked(l1_ref[a * 32 : a * 32 + 32])
            put(s2_ref, 6, a, 16, dot(v2, both))
            put(s4_ref, 6, a, 32, dot(p1, both))
        l2 = jnp.where(inside2, resampled(s2_ref, d2_ref), 0.0)
        l2_ref[i * 96 : i * 96 + 96] = l2
        for a in range(6):
            put(s3_ref, 6, a, 32, dot(p2, stacked(l2[a * 16 : a * 16 + 16])))
        detail1_ref[i * 192 : i * 192 + 192] = l1_ref[...] - resampled(s3_ref, u2_ref)
        part = resampled(s4_ref, u1_ref)
        for a in range(6):
            for h in range(2):
                at = a * 32 + 16 * h
                detail0_ref[i * 192 + at : i * 192 + at + 16] = (
                    main_ref[s, h, 16 * a : 16 * a + 16, :] - part[at : at + 16]
                )


def mix_kernel(
    place_ref, logit_ref, lse_ref,
    fine_a_ref, mid_a_ref, low_a_ref, fine_b_ref, mid_b_ref, low_b_ref,
    d1_ref, d2_ref, u2_ref, u1_ref,
    left_ref, right_ref, w0_ref, s1_ref, w1_ref, s2_ref, s3_ref, s4_ref,
):
    strip, k = place_ref[0], place_ref[1]
    v1 = down_rows(32, 64, 2, strip * 16 - 8, 512)
    v2, p2, p1 = row_matrices(strip)
    col = column_of((16, W0), M0, W0)
    inside_col = (col >= -10) & (col <= 522) & (col + k * M0 >= 0) & (col + k * M0 < 2048)
    row = lax.broadcasted_iota(jnp.int32, (16, W0), 0)
    lse = pltpu.roll(jnp.concatenate([lse_ref[...], jnp.zeros((8, W0), F32)], axis=0), 6, 0)
    keeps = []
    for b in range(4):
        r = row + (16 * b - 16)
        g = r + strip * 32
        keeps.append(inside_col & (r >= -10) & (r <= 42) & (g >= 0) & (g < 1024))
    for i in range(8):
        for b in range(4):
            rows = slice(16 * b, 16 * b + 16)
            w0_ref[i, rows] = jnp.where(keeps[b], jnp.exp(logit_ref[i, rows] - lse[rows]), 0.0)
        put(s1_ref, 8, i, 32, dot(v1, stacked(w0_ref[i])))
    inside1, inside2 = level_masks(32, 16, k)
    w1_ref[...] = resampled(s1_ref, d1_ref)
    for i in range(8):
        w1 = jnp.where(inside1, w1_ref[i * 32 : i * 32 + 32], 0.0)
        w1_ref[i * 32 : i * 32 + 32] = w1
        put(s2_ref, 8, i, 16, dot(v2, stacked(w1)))
    w2 = resampled(s2_ref, d2_ref)

    def piece(pair, i, c, rows):
        ref = pair[i // 4]
        at = ((i % 4) * 3 + c) * rows
        return ref[at : at + rows]

    for c in range(3):
        blend2 = 0.0
        for i in range(8):
            blend2 = blend2 + w2[i * 16 : i * 16 + 16] * piece((low_a_ref, low_b_ref), i, c, 16)
        put(s3_ref, 3, c, 32, dot(p2, stacked(blend2)))
    rise = resampled(s3_ref, u2_ref)
    for c in range(3):
        total = jnp.where(inside1, rise[c * 32 : c * 32 + 32], 0.0)
        for i in range(8):
            total = total + w1_ref[i * 32 : i * 32 + 32] * piece((mid_a_ref, mid_b_ref), i, c, 32)
        put(s4_ref, 3, c, 32, dot(p1, stacked(total)))
    rise = resampled(s4_ref, u1_ref)
    for c in range(3):
        total = rise[c * 32 : c * 32 + 32]
        for i in range(8):
            total = total + w0_ref[i, 16:48, 0:M0] * piece((fine_a_ref, fine_b_ref), i, c, 32)
        total = total * (1.0 / 255.0)
        left_ref[c] = total[:, :256]
        right_ref[c] = total[:, 256:]


def gather_kernel(place_ref, *refs):
    out_ref = refs[-1]
    for half in range(2):
        for n, flip in enumerate((0, 1, 3, 2)):
            at = (place_ref[1] ^ flip) * 512 + half * 256
            out_ref[:, :, pl.ds(pl.multiple_of(at, 256), 256)] = refs[4 * half + n][...]


def vmem(count):
    return [pl.BlockSpec(memory_space=pltpu.VMEM)] * count


def smem():
    return [pl.BlockSpec(memory_space=pltpu.SMEM)]


def neighbours(halves, core):
    count = lax.axis_size(ROWS)
    swaps = [(i, i + 1) for i in range(1, count - 1, 2)]
    swaps += [(b, a) for a, b in swaps]
    pick = functools.partial(lax.dynamic_index_in_dim, halves, axis=-3, keepdims=False)
    near = lax.ppermute(pick(1 - core), "c", [(0, 1), (1, 0)])
    far = lax.ppermute(pick(core), ROWS, swaps)
    return near, far


def partner(value, flip):
    return lax.ppermute(value, "zh", [(i, i ^ flip) for i in range(4)])


def crossed(value, flips):
    pairs = [(4 * c + i, 4 * c + (i ^ flip)) for c, flip in enumerate(flips) for i in range(4)]
    return lax.ppermute(value, ("c", "zh"), pairs)


def join_lse(a, b):
    return jnp.maximum(a, b) + jnp.log(1.0 + jnp.exp(-jnp.abs(a - b)))


def on_device(samples, gain):
    samples, strip, column, core = lax.optimization_barrier(
        (samples, lax.axis_index(ROWS), lax.axis_index("x"), lax.axis_index("c"))
    )
    packed = pl.pallas_call(
        pack_kernel,
        out_shape=jax.ShapeDtypeStruct((4, 2, 104, 512), F32),
        in_specs=vmem(1) + smem(),
        out_specs=vmem(1)[0],
        compiler_params=PARAMS,
        name="pack",
    )(samples, gain)
    main = lax.all_to_all(packed, "x", 0, 0)
    main, strip, column, core = lax.optimization_barrier((main, strip, column, core))
    near, far = neighbours(main, core)
    place = jnp.stack([strip, column, core]).astype(jnp.int32)
    logits, lse = pl.pallas_call(
        energy_kernel,
        out_shape=(jax.ShapeDtypeStruct((8, 64, W0), F32), jax.ShapeDtypeStruct((56, W0), F32)),
        in_specs=smem() + vmem(3),
        out_specs=tuple(vmem(2)),
        scratch_shapes=[pltpu.VMEM((64, W0), F32)],
        compiler_params=PARAMS,
        name="energy",
    )(place, main, near, far)

    taps = [
        jnp.asarray(t, BF)
        for t in (
            column_taps("down", M0, W0, M1, W1),
            column_taps("down", M1, W1, M2, W2),
            column_taps("up", M2, W2, M1, W1),
            column_taps("up", M1, W1, M0, W0)[:, :M0],
        )
    ]
    details = []
    for step, flips in enumerate(((1, 3), (3, 1))):
        other = crossed(lse, flips)
        detail = pl.pallas_call(
            functools.partial(pyramid_kernel, (2 * step, 2 * step + 1)),
            out_shape=(
                jax.ShapeDtypeStruct((384, M0), F32),
                jax.ShapeDtypeStruct((384, W1), F32),
                jax.ShapeDtypeStruct((192, W2), F32),
            ),
            in_specs=smem() + vmem(7),
            out_specs=tuple(vmem(3)),
            scratch_shapes=[
                pltpu.VMEM((64, W0), BF),
                pltpu.VMEM((384, W0), BF),
                pltpu.VMEM((192, W1), F32),
                pltpu.VMEM((192, W1), BF),
                pltpu.VMEM((384, W2), BF),
                pltpu.VMEM((384, W1), BF),
            ],
            compiler_params=PARAMS,
            cost_estimate=pl.CostEstimate(flops=2_000_000_000, bytes_accessed=6_000_000, transcendentals=0),
            name="pyramid",
        )(place, main, near, far, *taps)
        other, *detail = lax.optimization_barrier((other, *detail))
        details += detail
        lse = join_lse(lse, other)

    left, right = pl.pallas_call(
        mix_kernel,
        out_shape=(jax.ShapeDtypeStruct((3, 32, 256), F32),) * 2,
        in_specs=smem() + vmem(12),
        out_specs=tuple(vmem(2)),
        scratch_shapes=[
            pltpu.VMEM((8, 64, W0), F32),
            pltpu.VMEM((512, W0), BF),
            pltpu.VMEM((256, W1), F32),
            pltpu.VMEM((256, W1), BF),
            pltpu.VMEM((192, W2), BF),
            pltpu.VMEM((192, W1), BF),
        ],
        compiler_params=PARAMS,
        name="mix",
    )(place, logits, lse, *details, *taps)

    for a, b in ((1, 3), (3, 1)):
        left_in, right_in = partner(left, a), partner(right, b)
        left, right = left + left_in, right + right_in
    pieces = []
    for half in (left, right):
        pieces.append(half)
        for flip in (1, 3, 2):
            pieces.append(lax.ppermute(half, "x", [(i, i ^ flip) for i in range(4)]))
    return pl.pallas_call(
        gather_kernel,
        out_shape=jax.ShapeDtypeStruct((3, 32, 2048), F32),
        in_specs=smem() + vmem(8),
        out_specs=vmem(1)[0],
        compiler_params=PARAMS,
        name="gather",
    )(place, *pieces)


def solution(mesh):
    fine = Mesh(mesh.devices.reshape(4, 4, 2, 4, 4), ROWS + GZ)
    return jax.shard_map(
        on_device,
        mesh=fine,
        in_specs=(P(GZ, None, ROWS, None), P(GZ)),
        out_specs=P(None, ROWS, None),
        check_vma=False,
    )
```

```python
import functools

import jax
import jax.numpy as jnp
import numpy as np
from jax import lax
from jax.experimental import pallas as pl
from jax.experimental.pallas import tpu as pltpu
from jax.sharding import Mesh
from jax.sharding import PartitionSpec as P

ROWS = ("zl", "y", "c")
GZ = ("zh", "x")
BF = jnp.bfloat16
F32 = jnp.float32
GREY = (0.299 / 255.0, 0.587 / 255.0, 0.114 / 255.0)
W0, W1, W2 = 640, 384, 256
M0, M1, M2 = 512, 256, 128
PARAMS = pltpu.CompilerParams(vmem_limit_bytes=20 * 1024 * 1024)


def lane_of(col, main, wide):
    if 0 <= col < main + 64:
        return col
    if -64 <= col < 0:
        return wide + col
    return None


def column_taps(kind, main_in, wide_in, main_out, wide_out):
    taps = np.zeros((wide_in, wide_out), np.float32)
    for lane in range(wide_out):
        col = lane if lane < main_out + 64 else lane - wide_out
        if kind == "down":
            picks = [(2 * col + d, t / 16.0) for d, t in zip(range(-2, 3), (1, 4, 6, 4, 1))]
        elif col % 2 == 0:
            picks = [(col // 2 - 1, 0.125), (col // 2, 0.75), (col // 2 + 1, 0.125)]
        else:
            picks = [(col // 2, 0.5), (col // 2 + 1, 0.5)]
        for source, tap in picks:
            at = lane_of(source, main_in, wide_in)
            if at is not None:
                taps[at, lane] += tap
    return taps


def pack_kernel(samples_ref, gain_hbm_ref, packed_ref, held_ref, gain_ref, out_ref, sems, gain_sem, out_sems):
    copies = []
    for a in range(6):
        p, c = divmod(a, 3)
        copies.append(pltpu.make_async_copy(samples_ref.at[p, c], held_ref.at[a], sems.at[a]))
        copies[a].start()
    gain_copy = pltpu.make_async_copy(gain_hbm_ref, gain_ref, gain_sem)
    gain_copy.start()
    written = []

    def write(n, lo, hi):
        written.append(pltpu.make_async_copy(out_ref.at[:, :, lo:hi], packed_ref.at[:, :, lo:hi], out_sems.at[n]))
        written[n].start()

    for a in range(6):
        copies[a].wait()
        for j in range(4):
            for h in range(2):
                out_ref[j, h, 16 * a : 16 * a + 16, :] = held_ref[
                    a, 16 * h : 16 * h + 16, 512 * j : 512 * j + 512
                ].astype(F32)
        write(a, 16 * a, 16 * a + 16)
    gain_copy.wait()
    lane = lax.broadcasted_iota(jnp.int32, (16, 128), 1)
    for j in range(4):
        for h in range(2):
            rows = slice(16 * h, 16 * h + 16)
            tiles = [
                jnp.zeros((16, 128), F32),
                jnp.where(lane < 64, 0.0, jnp.where(lane < 96, gain_ref[0], gain_ref[1])),
            ]
            for a in range(6):
                at, t = 32 * (a % 4), a // 4
                if j > 0:
                    piece = held_ref[a, rows, 512 * j - 128 : 512 * j].astype(F32)
                    piece = pltpu.roll(piece, (at - 112) % 128, 1)
                    tiles[t] = jnp.where((lane >= at) & (lane < at + 16), piece, tiles[t])
                if j < 3:
                    piece = held_ref[a, rows, 512 * j + 512 : 512 * j + 640].astype(F32)
                    piece = pltpu.roll(piece, (at + 16) % 128, 1)
                    tiles[t] = jnp.where((lane >= at + 16) & (lane < at + 32), piece, tiles[t])
            out_ref[j, h, 96:104, 0:128] = tiles[0][0:8]
            out_ref[j, h, 96:104, 128:256] = tiles[1][0:8]
            out_ref[j, h, 96:104, 256:384] = tiles[0][8:16]
            out_ref[j, h, 96:104, 384:512] = tiles[1][8:16]
    write(6, 96, 104)
    for copy in written:
        copy.wait()


class Strips:
    def __init__(self, first, place_ref, main_ref, near_ref, far_ref):
        self.first = first
        self.even = place_ref[2] == 0
        self.main, self.near, self.far = main_ref, near_ref, far_ref

    def get(self, s, b, rows, cols):
        if b in (1, 2):
            return self.main[s, b - 1, rows, cols]
        near, far = self.near[s, rows, cols], self.far[s - self.first, rows, cols]
        return jnp.where(self.even, far, near) if b == 0 else jnp.where(self.even, near, far)

    def samples(self, s, b, a):
        return self.get(s, b, slice(16 * a, 16 * a + 16), slice(0, M0))

    def halo(self, s, b, a):
        return halo_tile(lambda cols: self.get(s, b, slice(96, 104), cols), a)


def halo_tile(read, a):
    base, at = 128 * (a // 4), 32 * (a % 4)
    tile = jnp.concatenate([read(slice(base, base + 128)), read(slice(256 + base, 384 + base))], axis=0)
    lane = lax.broadcasted_iota(jnp.int32, (16, 128), 1)
    return jnp.where((lane < 16) | (lane >= 112), pltpu.roll(tile, (112 - at) % 128, 1), 0.0)


def column_of(shape, main, wide):
    lane = lax.broadcasted_iota(jnp.int32, shape, len(shape) - 1)
    return jnp.where(lane < main + 64, lane, lane - wide)


def energy_kernel(first, place_ref, main_ref, near_ref, far_ref, *refs):
    earlier_ref, logit_ref, lse_ref, grey_ref = refs if first else (None, refs[0], None, refs[1])
    row = lax.broadcasted_iota(jnp.int32, (64, W0), 0) + (place_ref[0] * 32 - 16)
    col = column_of((64, W0), M0, W0) + place_ref[1] * M0
    keep = (row >= 0) & (row < 1024) & (col >= 0) & (col < 2048)

    strips = Strips(first, place_ref, main_ref, near_ref, far_ref)

    @pl.loop(0, 2)
    def _(t):
        s = first + t
        for p in range(2):
            for b in range(4):
                main = 0.0
                tile = 0.0
                for c in range(3):
                    a = 3 * p + c
                    main = main + strips.samples(s, b, a) * GREY[c]
                    tile = tile + strips.halo(s, b, a) * GREY[c]
                grey_ref[16 * b : 16 * b + 16, 0:M0] = main
                grey_ref[16 * b : 16 * b + 16, M0:W0] = tile
            grey = grey_ref[...]
            lap = (
                4.0 * grey
                - pltpu.roll(grey, 1, 0)
                - pltpu.roll(grey, 63, 0)
                - pltpu.roll(grey, 1, 1)
                - pltpu.roll(grey, W0 - 1, 1)
            )
            field = jnp.where(keep, lap * lap, 0.0)
            for axis, size in ((0, 64), (1, W0)):
                two = field + pltpu.roll(field, size - 1, axis)
                four = two + pltpu.roll(two, size - 2, axis)
                eight = four + pltpu.roll(four, size - 4, axis)
                field = pltpu.roll(eight, 4, axis) + pltpu.roll(field, size - 4, axis)
            gain = main_ref[s, 0, 96:97, 192 + 32 * p : 193 + 32 * p]
            logit_ref[2 * t + p] = gain * field

    if first:
        logits = [ref.at[i] for ref in (earlier_ref, logit_ref) for i in range(4)]
        peak = logits[0][...]
        for ref in logits[1:]:
            peak = jnp.maximum(peak, ref[...])
        total = 0.0
        for ref in logits:
            total = total + jnp.exp(ref[...] - peak)
        lse_ref[...] = pltpu.roll(peak + jnp.log(total), 58, 0)[0:56]


def split2(value):
    high = value.astype(BF)
    low = (value - high.astype(F32)).astype(BF)
    return high, low


def stacked(value):
    return jnp.concatenate(split2(value), axis=0)


def dot(a, b):
    return jnp.dot(a, b, preferred_element_type=F32)


def iota2(shape):
    return lax.broadcasted_iota(jnp.int32, shape, 0), lax.broadcasted_iota(jnp.int32, shape, 1)


def down_rows(count, inputs, copies, first, limit):
    q, e = iota2((count, inputs * copies))
    if copies == 2:
        e = jnp.where(e >= inputs, e - inputs, e)
    gap = jnp.abs(e - 2 * q)
    taps = jnp.where(gap == 0, 0.375, jnp.where(gap == 1, 0.25, jnp.where(gap == 2, 0.0625, 0.0)))
    inside = (q + first >= 0) & (q + first < limit)
    return jnp.where(inside, taps, 0.0).astype(BF)


def up_rows(count, inputs, offset, first, limit):
    r, q = iota2((count, 2 * inputs))
    q = jnp.where(q >= inputs, q - inputs, q)
    gap = jnp.abs(2 * q - (r + offset))
    even = (r & 1) == 0
    taps = jnp.where(
        even,
        jnp.where(gap == 0, 0.75, jnp.where(gap == 2, 0.125, 0.0)),
        jnp.where(gap == 1, 0.5, 0.0),
    )
    inside = (r + first >= 0) & (r + first < limit)
    return jnp.where(inside, taps, 0.0).astype(BF)


def row_matrices(strip):
    v2 = down_rows(16, 32, 2, strip * 8 - 4, 256)
    p2 = up_rows(32, 16, 0, strip * 16 - 8, 512)
    p1 = up_rows(32, 32, 16, 0, 32)
    return v2, p2, p1


def level_masks(rows1, rows2, k):
    col1 = column_of((rows1, W1), M1, W1) + k * M1
    col2 = column_of((rows2, W2), M2, W2) + k * M2
    return (col1 >= 0) & (col1 < 1024), (col2 >= 0) & (col2 < 512)


def put(ref, n, a, count, value):
    high, low = split2(value)
    ref[a * count : (a + 1) * count] = high
    ref[(n + a) * count : (n + a + 1) * count] = low


def resampled(source_ref, taps_ref):
    both = dot(source_ref[...], taps_ref[...])
    half = both.shape[0] // 2
    return both[:half] + both[half:]


def pyramid_kernel(
    sources, place_ref, main_ref, near_ref, far_ref, d1_ref, d2_ref, u2_ref, u1_ref,
    detail0_ref, detail1_ref, l2_ref, x_ref, s1_ref, l1_ref, s2_ref, s3_ref, s4_ref,
):
    strip = place_ref[0]
    v1 = down_rows(32, 64, 1, strip * 16 - 8, 512)
    v2, p2, p1 = row_matrices(strip)
    inside1, inside2 = level_masks(192, 96, place_ref[1])
    strips = Strips(sources[0], place_ref, main_ref, near_ref, far_ref)
    for i, s in enumerate(sources):
        for a in range(6):
            for b in range(4):
                x_ref[16 * b : 16 * b + 16, 0:M0] = strips.samples(s, b, a).astype(BF)
                x_ref[16 * b : 16 * b + 16, M0:W0] = strips.halo(s, b, a).astype(BF)
            put(s1_ref, 6, a, 32, dot(v1, x_ref[...]))
        l1_ref[...] = jnp.where(inside1, resampled(s1_ref, d1_ref), 0.0)
        for a in range(6):
            both = stacked(l1_ref[a * 32 : a * 32 + 32])
            put(s2_ref, 6, a, 16, dot(v2, both))
            put(s4_ref, 6, a, 32, dot(p1, both))
        l2 = jnp.where(inside2, resampled(s2_ref, d2_ref), 0.0)
        l2_ref[i * 96 : i * 96 + 96] = l2
        for a in range(6):
            put(s3_ref, 6, a, 32, dot(p2, stacked(l2[a * 16 : a * 16 + 16])))
        detail1_ref[i * 192 : i * 192 + 192] = l1_ref[...] - resampled(s3_ref, u2_ref)
        part = resampled(s4_ref, u1_ref)
        for a in range(6):
            for h in range(2):
                at = a * 32 + 16 * h
                detail0_ref[i * 192 + at : i * 192 + at + 16] = (
                    main_ref[s, h, 16 * a : 16 * a + 16, :] - part[at : at + 16]
                )


def mix_kernel(
    place_ref, logit_a_ref, logit_b_ref, lse_ref,
    fine_a_ref, mid_a_ref, low_a_ref, fine_b_ref, mid_b_ref, low_b_ref,
    d1_ref, d2_ref, u2_ref, u1_ref,
    left_ref, right_ref, w0_ref, s1_ref, w1_ref, s2_ref, s3_ref, s4_ref,
):
    strip, k = place_ref[0], place_ref[1]
    v1 = down_rows(32, 64, 2, strip * 16 - 8, 512)
    v2, p2, p1 = row_matrices(strip)
    col = column_of((16, W0), M0, W0)
    inside_col = (col >= -10) & (col <= 522) & (col + k * M0 >= 0) & (col + k * M0 < 2048)
    row = lax.broadcasted_iota(jnp.int32, (16, W0), 0)
    lse = pltpu.roll(jnp.concatenate([lse_ref[...], jnp.zeros((8, W0), F32)], axis=0), 6, 0)
    keeps = []
    for b in range(4):
        r = row + (16 * b - 16)
        g = r + strip * 32
        keeps.append(inside_col & (r >= -10) & (r <= 42) & (g >= 0) & (g < 1024))
    for i in range(8):
        logit_ref = (logit_a_ref, logit_b_ref)[i // 4]
        for b in range(4):
            rows = slice(16 * b, 16 * b + 16)
            w0_ref[i, rows] = jnp.where(keeps[b], jnp.exp(logit_ref[i % 4, rows] - lse[rows]), 0.0)
        put(s1_ref, 8, i, 32, dot(v1, stacked(w0_ref[i])))
    inside1, inside2 = level_masks(32, 16, k)
    w1_ref[...] = resampled(s1_ref, d1_ref)
    for i in range(8):
        w1 = jnp.where(inside1, w1_ref[i * 32 : i * 32 + 32], 0.0)
        w1_ref[i * 32 : i * 32 + 32] = w1
        put(s2_ref, 8, i, 16, dot(v2, stacked(w1)))
    w2 = resampled(s2_ref, d2_ref)

    def piece(pair, i, c, rows):
        ref = pair[i // 4]
        at = ((i % 4) * 3 + c) * rows
        return ref[at : at + rows]

    for c in range(3):
        blend2 = 0.0
        for i in range(8):
            blend2 = blend2 + w2[i * 16 : i * 16 + 16] * piece((low_a_ref, low_b_ref), i, c, 16)
        put(s3_ref, 3, c, 32, dot(p2, stacked(blend2)))
    rise = resampled(s3_ref, u2_ref)
    for c in range(3):
        total = jnp.where(inside1, rise[c * 32 : c * 32 + 32], 0.0)
        for i in range(8):
            total = total + w1_ref[i * 32 : i * 32 + 32] * piece((mid_a_ref, mid_b_ref), i, c, 32)
        put(s4_ref, 3, c, 32, dot(p1, stacked(total)))
    rise = resampled(s4_ref, u1_ref)
    for c in range(3):
        total = rise[c * 32 : c * 32 + 32]
        for i in range(8):
            total = total + w0_ref[i, 16:48, 0:M0] * piece((fine_a_ref, fine_b_ref), i, c, 32)
        total = total * (1.0 / 255.0)
        left_ref[c] = total[:, :256]
        right_ref[c] = total[:, 256:]


def vmem(count):
    return [pl.BlockSpec(memory_space=pltpu.VMEM)] * count


def smem():
    return [pl.BlockSpec(memory_space=pltpu.SMEM)]


def neighbours(halves, core):
    count = lax.axis_size(ROWS)
    swaps = [(i, i + 1) for i in range(1, count - 1, 2)]
    swaps += [(b, a) for a, b in swaps]
    pick = functools.partial(lax.dynamic_index_in_dim, halves, axis=1, keepdims=False)
    near = lax.ppermute(pick(1 - core), "c", [(0, 1), (1, 0)])
    far = pick(core)
    return near, lax.ppermute(far[:2], ROWS, swaps), lax.ppermute(far[2:], ROWS, swaps)


def partner(value, flip):
    return lax.ppermute(value, "zh", [(i, i ^ flip) for i in range(4)])


def crossed(value, flips):
    pairs = [(4 * c + i, 4 * c + (i ^ flip)) for c, flip in enumerate(flips) for i in range(4)]
    return lax.ppermute(value, ("c", "zh"), pairs)


def join_lse(a, b):
    return jnp.maximum(a, b) + jnp.log(1.0 + jnp.exp(-jnp.abs(a - b)))


def on_device(samples, gain):
    samples, strip, column, core = lax.optimization_barrier(
        (samples, lax.axis_index(ROWS), lax.axis_index("x"), lax.axis_index("c"))
    )
    packed = pl.pallas_call(
        pack_kernel,
        out_shape=jax.ShapeDtypeStruct((4, 2, 104, 512), F32),
        in_specs=[pl.BlockSpec(memory_space=pltpu.HBM)] * 2,
        out_specs=pl.BlockSpec(memory_space=pltpu.HBM),
        scratch_shapes=[
            pltpu.VMEM((6, 32, 2048), jnp.int32),
            pltpu.SMEM((2,), F32),
            pltpu.VMEM((4, 2, 104, 512), F32),
            pltpu.SemaphoreType.DMA((6,)),
            pltpu.SemaphoreType.DMA,
            pltpu.SemaphoreType.DMA((7,)),
        ],
        compiler_params=pltpu.CompilerParams(vmem_limit_bytes=60 * 1024 * 1024),
        name="pack",
    )(samples, gain)
    main = lax.all_to_all(packed, "x", 0, 0)
    main, strip, column, core = lax.optimization_barrier((main, strip, column, core))
    near, *far = neighbours(main, core)
    place = jnp.stack([strip, column, core]).astype(jnp.int32)
    logit_shape = jax.ShapeDtypeStruct((4, 64, W0), F32)

    def energy(first, *earlier):
        return pl.pallas_call(
            functools.partial(energy_kernel, first),
            out_shape=(logit_shape,) + (jax.ShapeDtypeStruct((56, W0), F32),) * len(earlier),
            in_specs=smem() + vmem(3 + len(earlier)),
            out_specs=tuple(vmem(1 + len(earlier))),
            scratch_shapes=[pltpu.VMEM((64, W0), F32)],
            compiler_params=PARAMS,
            cost_estimate=pl.CostEstimate(flops=2_000_000_000, bytes_accessed=6_000_000, transcendentals=0),
            name="energy",
        )(place, main, near, far[first // 2], *earlier)

    logits = energy(0)
    *more, lse = energy(2, *logits)
    logits = [*logits, *more]

    taps = [
        jnp.asarray(t, BF)
        for t in (
            column_taps("down", M0, W0, M1, W1),
            column_taps("down", M1, W1, M2, W2),
            column_taps("up", M2, W2, M1, W1),
            column_taps("up", M1, W1, M0, W0)[:, :M0],
        )
    ]
    details = []
    for step, flips in enumerate(((1, 3), (3, 1))):
        other = crossed(lse, flips)
        detail = pl.pallas_call(
            functools.partial(pyramid_kernel, (2 * step, 2 * step + 1)),
            out_shape=(
                jax.ShapeDtypeStruct((384, M0), F32),
                jax.ShapeDtypeStruct((384, W1), F32),
                jax.ShapeDtypeStruct((192, W2), F32),
            ),
            in_specs=smem() + vmem(7),
            out_specs=tuple(vmem(3)),
            scratch_shapes=[
                pltpu.VMEM((64, W0), BF),
                pltpu.VMEM((384, W0), BF),
                pltpu.VMEM((192, W1), F32),
                pltpu.VMEM((192, W1), BF),
                pltpu.VMEM((384, W2), BF),
                pltpu.VMEM((384, W1), BF),
            ],
            compiler_params=PARAMS,
            cost_estimate=pl.CostEstimate(flops=2_000_000_000, bytes_accessed=6_000_000, transcendentals=0),
            name="pyramid",
        )(place, main, near, far[step], *taps)
        other, *detail = lax.optimization_barrier((other, *detail))
        details += detail
        lse = join_lse(lse, other)

    left, right = pl.pallas_call(
        mix_kernel,
        out_shape=(jax.ShapeDtypeStruct((3, 32, 256), F32),) * 2,
        in_specs=smem() + vmem(13),
        out_specs=tuple(vmem(2)),
        scratch_shapes=[
            pltpu.VMEM((8, 64, W0), F32),
            pltpu.VMEM((512, W0), BF),
            pltpu.VMEM((256, W1), F32),
            pltpu.VMEM((256, W1), BF),
            pltpu.VMEM((192, W2), BF),
            pltpu.VMEM((192, W1), BF),
        ],
        compiler_params=PARAMS,
        name="mix",
    )(place, *logits, lse, *details, *taps)

    for a, b in ((1, 3), (3, 1)):
        left_in, right_in = partner(left, a), partner(right, b)
        left, right = left + left_in, right + right_in
    whole = jnp.concatenate([left, right], axis=-1)
    joined = lax.all_to_all(jnp.broadcast_to(whole, (4, 3, 32, 512)), "x", 0, 0)
    return joined.transpose(1, 2, 0, 3).reshape(3, 32, 2048)


def solution(mesh):
    fine = Mesh(mesh.devices.reshape(4, 4, 2, 4, 4), ROWS + GZ)
    return jax.shard_map(
        on_device,
        mesh=fine,
        in_specs=(P(GZ, None, ROWS, None), P(GZ)),
        out_specs=P(None, ROWS, None),
        check_vma=False,
    )
```

```python
import functools

import jax
import jax.numpy as jnp
import numpy as np
from jax import lax
from jax.experimental import pallas as pl
from jax.experimental.pallas import tpu as pltpu
from jax.sharding import Mesh
from jax.sharding import PartitionSpec as P

ROWS = ("zl", "y", "c")
GZ = ("zh", "x")
BF = jnp.bfloat16
F32 = jnp.float32
GREY = (0.299 / 255.0, 0.587 / 255.0, 0.114 / 255.0)
W0, W1, W2 = 640, 384, 256
M0, M1, M2 = 512, 256, 128
FLIPS = (0, 1, 3, 2)
PARAMS = pltpu.CompilerParams(vmem_limit_bytes=20 * 1024 * 1024)


def lane_of(col, main, wide):
    if 0 <= col < main + 64:
        return col
    if -64 <= col < 0:
        return wide + col
    return None


def column_taps(kind, main_in, wide_in, main_out, wide_out):
    taps = np.zeros((wide_in, wide_out), np.float32)
    for lane in range(wide_out):
        col = lane if lane < main_out + 64 else lane - wide_out
        if kind == "down":
            picks = [(2 * col + d, t / 16.0) for d, t in zip(range(-2, 3), (1, 4, 6, 4, 1))]
        elif col % 2 == 0:
            picks = [(col // 2 - 1, 0.125), (col // 2, 0.75), (col // 2 + 1, 0.125)]
        else:
            picks = [(col // 2, 0.5), (col // 2 + 1, 0.5)]
        for source, tap in picks:
            at = lane_of(source, main_in, wide_in)
            if at is not None:
                taps[at, lane] += tap
    return taps


def pack_kernel(samples_ref, gain_hbm_ref, *refs):
    packed_refs, (held_ref, gain_ref, out_ref, sems, gain_sem, out_sems) = refs[:4], refs[4:]
    copies = []
    for a in range(6):
        p, c = divmod(a, 3)
        copies.append(pltpu.make_async_copy(samples_ref.at[p, c], held_ref.at[a], sems.at[a]))
        copies[a].start()
    gain_copy = pltpu.make_async_copy(gain_hbm_ref, gain_ref, gain_sem)
    gain_copy.start()
    mine = lax.axis_index("x")
    lane = lax.broadcasted_iota(jnp.int32, (16, 128), 1)
    written = []
    for m, flip in enumerate(FLIPS):
        j = mine ^ flip
        base = pl.multiple_of(512 * j, 512)
        before = pl.multiple_of(jnp.maximum(base - 128, 0), 128)
        after = pl.multiple_of(jnp.minimum(base + 512, 1920), 128)
        has_before, has_after = j > 0, j < 3
        for a in range(6):
            if m == 0:
                copies[a].wait()
            for h in range(2):
                out_ref[m, h, 16 * a : 16 * a + 16, :] = held_ref[a, 16 * h : 16 * h + 16, pl.ds(base, 512)].astype(F32)
        if m == 0:
            gain_copy.wait()
        for h in range(2):
            rows = slice(16 * h, 16 * h + 16)
            tiles = [
                jnp.zeros((16, 128), F32),
                jnp.where(lane < 64, 0.0, jnp.where(lane < 96, gain_ref[0], gain_ref[1])),
            ]
            for a in range(6):
                at, t = 32 * (a % 4), a // 4
                piece = pltpu.roll(held_ref[a, rows, pl.ds(before, 128)].astype(F32), (at - 112) % 128, 1)
                piece = jnp.where(has_before, piece, 0.0)
                tiles[t] = jnp.where((lane >= at) & (lane < at + 16), piece, tiles[t])
                piece = pltpu.roll(held_ref[a, rows, pl.ds(after, 128)].astype(F32), (at + 16) % 128, 1)
                piece = jnp.where(has_after, piece, 0.0)
                tiles[t] = jnp.where((lane >= at + 16) & (lane < at + 32), piece, tiles[t])
            out_ref[m, h, 96:104, 0:128] = tiles[0][0:8]
            out_ref[m, h, 96:104, 128:256] = tiles[1][0:8]
            out_ref[m, h, 96:104, 256:384] = tiles[0][8:16]
            out_ref[m, h, 96:104, 384:512] = tiles[1][8:16]
        written.append(pltpu.make_async_copy(out_ref.at[m], packed_refs[m], out_sems.at[m]))
        written[m].start()
    for copy in written:
        copy.wait()


class Strips:
    def __init__(self, place_ref, mains, near_ref, far_ref):
        self.even = place_ref[2] == 0
        self.mains, self.near, self.far = mains, near_ref, far_ref

    def get(self, s, b, rows, cols):
        if b in (1, 2):
            return self.mains[s][b - 1, rows, cols]
        near, far = self.near[s, rows, cols], self.far[s, rows, cols]
        return jnp.where(self.even, far, near) if b == 0 else jnp.where(self.even, near, far)

    def samples(self, s, b, a):
        return self.get(s, b, slice(16 * a, 16 * a + 16), slice(0, M0))

    def halo(self, s, b, a):
        return halo_tile(lambda cols: self.get(s, b, slice(96, 104), cols), a)


def halo_tile(read, a):
    base, at = 128 * (a // 4), 32 * (a % 4)
    tile = jnp.concatenate([read(slice(base, base + 128)), read(slice(256 + base, 384 + base))], axis=0)
    lane = lax.broadcasted_iota(jnp.int32, (16, 128), 1)
    return jnp.where((lane < 16) | (lane >= 112), pltpu.roll(tile, (112 - at) % 128, 1), 0.0)


def column_of(shape, main, wide):
    lane = lax.broadcasted_iota(jnp.int32, shape, len(shape) - 1)
    return jnp.where(lane < main + 64, lane, lane - wide)


def energy_kernel(second, place_ref, main_a_ref, main_b_ref, near_ref, far_ref, *refs):
    earlier_ref, logit_ref, lse_ref, grey_ref = refs if second else (None, refs[0], None, refs[1])
    row = lax.broadcasted_iota(jnp.int32, (64, W0), 0) + (place_ref[0] * 32 - 16)
    col = column_of((64, W0), M0, W0) + place_ref[1] * M0
    keep = (row >= 0) & (row < 1024) & (col >= 0) & (col < 2048)

    mains = (main_a_ref, main_b_ref)
    strips = Strips(place_ref, mains, near_ref, far_ref)
    for s in range(2):
        for p in range(2):
            for b in range(4):
                main = 0.0
                tile = 0.0
                for c in range(3):
                    a = 3 * p + c
                    main = main + strips.samples(s, b, a) * GREY[c]
                    tile = tile + strips.halo(s, b, a) * GREY[c]
                grey_ref[16 * b : 16 * b + 16, 0:M0] = main
                grey_ref[16 * b : 16 * b + 16, M0:W0] = tile
            grey = grey_ref[...]
            lap = (
                4.0 * grey
                - pltpu.roll(grey, 1, 0)
                - pltpu.roll(grey, 63, 0)
                - pltpu.roll(grey, 1, 1)
                - pltpu.roll(grey, W0 - 1, 1)
            )
            field = jnp.where(keep, lap * lap, 0.0)
            for axis, size in ((0, 64), (1, W0)):
                two = field + pltpu.roll(field, size - 1, axis)
                four = two + pltpu.roll(two, size - 2, axis)
                eight = four + pltpu.roll(four, size - 4, axis)
                field = pltpu.roll(eight, 4, axis) + pltpu.roll(field, size - 4, axis)
            gain = mains[s][0, 96:97, 192 + 32 * p : 193 + 32 * p]
            logit_ref[2 * s + p] = gain * field

    if second:
        logits = [ref.at[i] for ref in (earlier_ref, logit_ref) for i in range(4)]
        peak = logits[0][...]
        for ref in logits[1:]:
            peak = jnp.maximum(peak, ref[...])
        total = 0.0
        for ref in logits:
            total = total + jnp.exp(ref[...] - peak)
        lse_ref[...] = pltpu.roll(peak + jnp.log(total), 58, 0)[0:56]


def split2(value):
    high = value.astype(BF)
    low = (value - high.astype(F32)).astype(BF)
    return high, low


def stacked(value):
    return jnp.concatenate(split2(value), axis=0)


def dot(a, b):
    return jnp.dot(a, b, preferred_element_type=F32)


def iota2(shape):
    return lax.broadcasted_iota(jnp.int32, shape, 0), lax.broadcasted_iota(jnp.int32, shape, 1)


def down_rows(count, inputs, copies, first, limit):
    q, e = iota2((count, inputs * copies))
    if copies == 2:
        e = jnp.where(e >= inputs, e - inputs, e)
    gap = jnp.abs(e - 2 * q)
    taps = jnp.where(gap == 0, 0.375, jnp.where(gap == 1, 0.25, jnp.where(gap == 2, 0.0625, 0.0)))
    inside = (q + first >= 0) & (q + first < limit)
    return jnp.where(inside, taps, 0.0).astype(BF)


def up_rows(count, inputs, offset, first, limit):
    r, q = iota2((count, 2 * inputs))
    q = jnp.where(q >= inputs, q - inputs, q)
    gap = jnp.abs(2 * q - (r + offset))
    even = (r & 1) == 0
    taps = jnp.where(
        even,
        jnp.where(gap == 0, 0.75, jnp.where(gap == 2, 0.125, 0.0)),
        jnp.where(gap == 1, 0.5, 0.0),
    )
    inside = (r + first >= 0) & (r + first < limit)
    return jnp.where(inside, taps, 0.0).astype(BF)


def row_matrices(strip):
    v2 = down_rows(16, 32, 2, strip * 8 - 4, 256)
    p2 = up_rows(32, 16, 0, strip * 16 - 8, 512)
    p1 = up_rows(32, 32, 16, 0, 32)
    return v2, p2, p1


def level_masks(rows1, rows2, k):
    col1 = column_of((rows1, W1), M1, W1) + k * M1
    col2 = column_of((rows2, W2), M2, W2) + k * M2
    return (col1 >= 0) & (col1 < 1024), (col2 >= 0) & (col2 < 512)


def put(ref, n, a, count, value):
    high, low = split2(value)
    ref[a * count : (a + 1) * count] = high
    ref[(n + a) * count : (n + a + 1) * count] = low


def resampled(source_ref, taps_ref):
    both = dot(source_ref[...], taps_ref[...])
    half = both.shape[0] // 2
    return both[:half] + both[half:]


def pyramid_kernel(
    place_ref, main_a_ref, main_b_ref, near_ref, far_ref, d1_ref, d2_ref, u2_ref, u1_ref,
    detail0_ref, detail1_ref, l2_ref, x_ref, s1_ref, l1_ref, s2_ref, s3_ref, s4_ref,
):
    strip = place_ref[0]
    v1 = down_rows(32, 64, 1, strip * 16 - 8, 512)
    v2, p2, p1 = row_matrices(strip)
    inside1, inside2 = level_masks(192, 96, place_ref[1])
    mains = (main_a_ref, main_b_ref)
    strips = Strips(place_ref, mains, near_ref, far_ref)
    for i in range(2):
        for a in range(6):
            for b in range(4):
                x_ref[16 * b : 16 * b + 16, 0:M0] = strips.samples(i, b, a).astype(BF)
                x_ref[16 * b : 16 * b + 16, M0:W0] = strips.halo(i, b, a).astype(BF)
            put(s1_ref, 6, a, 32, dot(v1, x_ref[...]))
        l1_ref[...] = jnp.where(inside1, resampled(s1_ref, d1_ref), 0.0)
        for a in range(6):
            both = stacked(l1_ref[a * 32 : a * 32 + 32])
            put(s2_ref, 6, a, 16, dot(v2, both))
            put(s4_ref, 6, a, 32, dot(p1, both))
        l2 = jnp.where(inside2, resampled(s2_ref, d2_ref), 0.0)
        l2_ref[i * 96 : i * 96 + 96] = l2
        for a in range(6):
            put(s3_ref, 6, a, 32, dot(p2, stacked(l2[a * 16 : a * 16 + 16])))
        detail1_ref[i * 192 : i * 192 + 192] = l1_ref[...] - resampled(s3_ref, u2_ref)
        part = resampled(s4_ref, u1_ref)
        for a in range(6):
            for h in range(2):
                at = a * 32 + 16 * h
                detail0_ref[i * 192 + at : i * 192 + at + 16] = (
                    mains[i][h, 16 * a : 16 * a + 16, :] - part[at : at + 16]
                )


def mix_kernel(
    place_ref, logit_a_ref, logit_b_ref, lse_ref,
    fine_a_ref, mid_a_ref, low_a_ref, fine_b_ref, mid_b_ref, low_b_ref,
    d1_ref, d2_ref, u2_ref, u1_ref,
    left_ref, right_ref, w0_ref, s1_ref, w1_ref, s2_ref, s3_ref, s4_ref,
):
    strip, k = place_ref[0], place_ref[1]
    v1 = down_rows(32, 64, 2, strip * 16 - 8, 512)
    v2, p2, p1 = row_matrices(strip)
    col = column_of((16, W0), M0, W0)
    inside_col = (col >= -10) & (col <= 522) & (col + k * M0 >= 0) & (col + k * M0 < 2048)
    row = lax.broadcasted_iota(jnp.int32, (16, W0), 0)
    lse = pltpu.roll(jnp.concatenate([lse_ref[...], jnp.zeros((8, W0), F32)], axis=0), 6, 0)
    keeps = []
    for b in range(4):
        r = row + (16 * b - 16)
        g = r + strip * 32
        keeps.append(inside_col & (r >= -10) & (r <= 42) & (g >= 0) & (g < 1024))
    for i in range(8):
        logit_ref = (logit_a_ref, logit_b_ref)[i // 4]
        for b in range(4):
            rows = slice(16 * b, 16 * b + 16)
            w0_ref[i, rows] = jnp.where(keeps[b], jnp.exp(logit_ref[i % 4, rows] - lse[rows]), 0.0)
        put(s1_ref, 8, i, 32, dot(v1, stacked(w0_ref[i])))
    inside1, inside2 = level_masks(32, 16, k)
    w1_ref[...] = resampled(s1_ref, d1_ref)
    for i in range(8):
        w1 = jnp.where(inside1, w1_ref[i * 32 : i * 32 + 32], 0.0)
        w1_ref[i * 32 : i * 32 + 32] = w1
        put(s2_ref, 8, i, 16, dot(v2, stacked(w1)))
    w2 = resampled(s2_ref, d2_ref)

    def piece(pair, i, c, rows):
        ref = pair[i // 4]
        at = ((i % 4) * 3 + c) * rows
        return ref[at : at + rows]

    for c in range(3):
        blend2 = 0.0
        for i in range(8):
            blend2 = blend2 + w2[i * 16 : i * 16 + 16] * piece((low_a_ref, low_b_ref), i, c, 16)
        put(s3_ref, 3, c, 32, dot(p2, stacked(blend2)))
    rise = resampled(s3_ref, u2_ref)
    for c in range(3):
        total = jnp.where(inside1, rise[c * 32 : c * 32 + 32], 0.0)
        for i in range(8):
            total = total + w1_ref[i * 32 : i * 32 + 32] * piece((mid_a_ref, mid_b_ref), i, c, 32)
        put(s4_ref, 3, c, 32, dot(p1, stacked(total)))
    rise = resampled(s4_ref, u1_ref)
    for c in range(3):
        total = rise[c * 32 : c * 32 + 32]
        for i in range(8):
            total = total + w0_ref[i, 16:48, 0:M0] * piece((fine_a_ref, fine_b_ref), i, c, 32)
        total = total * (1.0 / 255.0)
        left_ref[c] = total[:, :256]
        right_ref[c] = total[:, 256:]


def vmem(count):
    return [pl.BlockSpec(memory_space=pltpu.VMEM)] * count


def smem():
    return [pl.BlockSpec(memory_space=pltpu.SMEM)]


def neighbours(group, core):
    count = lax.axis_size(ROWS)
    swaps = [(i, i + 1) for i in range(1, count - 1, 2)]
    swaps += [(b, a) for a, b in swaps]

    def half(index):
        return jnp.stack([lax.dynamic_index_in_dim(main, index, axis=0, keepdims=False) for main in group])

    return lax.ppermute(half(1 - core), "c", [(0, 1), (1, 0)]), lax.ppermute(half(core), ROWS, swaps)


def partner(value, flip):
    return lax.ppermute(value, "zh", [(i, i ^ flip) for i in range(4)])


def crossed(value, flips):
    pairs = [(4 * c + i, 4 * c + (i ^ flip)) for c, flip in enumerate(flips) for i in range(4)]
    return lax.ppermute(value, ("c", "zh"), pairs)


def join_lse(a, b):
    return jnp.maximum(a, b) + jnp.log(1.0 + jnp.exp(-jnp.abs(a - b)))


def on_device(samples, gain):
    samples, strip, column, core = lax.optimization_barrier(
        (samples, lax.axis_index(ROWS), lax.axis_index("x"), lax.axis_index("c"))
    )
    packed = pl.pallas_call(
        pack_kernel,
        out_shape=(jax.ShapeDtypeStruct((2, 104, 512), F32),) * 4,
        in_specs=[pl.BlockSpec(memory_space=pltpu.HBM)] * 2,
        out_specs=(pl.BlockSpec(memory_space=pltpu.HBM),) * 4,
        scratch_shapes=[
            pltpu.VMEM((6, 32, 2048), jnp.int32),
            pltpu.SMEM((2,), F32),
            pltpu.VMEM((4, 2, 104, 512), F32),
            pltpu.SemaphoreType.DMA((6,)),
            pltpu.SemaphoreType.DMA,
            pltpu.SemaphoreType.DMA((4,)),
        ],
        compiler_params=pltpu.CompilerParams(vmem_limit_bytes=60 * 1024 * 1024),
        name="pack",
    )(samples, gain)
    mains = [packed[0]] + [
        lax.ppermute(packed[m], "x", [(i, i ^ FLIPS[m]) for i in range(4)]) for m in (1, 2, 3)
    ]
    place = jnp.stack([strip, column, core]).astype(jnp.int32)
    groups = [(*pair, *neighbours(pair, core)) for pair in (mains[:2], mains[2:])]
    logit_shape = jax.ShapeDtypeStruct((4, 64, W0), F32)

    def energy(step, *earlier):
        return pl.pallas_call(
            functools.partial(energy_kernel, step == 1),
            out_shape=(logit_shape,) + (jax.ShapeDtypeStruct((56, W0), F32),) * step,
            in_specs=smem() + vmem(4 + step),
            out_specs=tuple(vmem(1 + step)),
            scratch_shapes=[pltpu.VMEM((64, W0), F32)],
            compiler_params=PARAMS,
            cost_estimate=pl.CostEstimate(flops=2_000_000_000, bytes_accessed=6_000_000, transcendentals=0),
            name="energy",
        )(place, *groups[step], *earlier)

    logits = energy(0)
    *more, lse = energy(1, *logits)
    logits = [*logits, *more]

    taps = [
        jnp.asarray(t, BF)
        for t in (
            column_taps("down", M0, W0, M1, W1),
            column_taps("down", M1, W1, M2, W2),
            column_taps("up", M2, W2, M1, W1),
            column_taps("up", M1, W1, M0, W0)[:, :M0],
        )
    ]
    details = []
    for step, flips in enumerate(((1, 3), (3, 1))):
        other = crossed(lse, flips)
        detail = pl.pallas_call(
            pyramid_kernel,
            out_shape=(
                jax.ShapeDtypeStruct((384, M0), F32),
                jax.ShapeDtypeStruct((384, W1), F32),
                jax.ShapeDtypeStruct((192, W2), F32),
            ),
            in_specs=smem() + vmem(8),
            out_specs=tuple(vmem(3)),
            scratch_shapes=[
                pltpu.VMEM((64, W0), BF),
                pltpu.VMEM((384, W0), BF),
                pltpu.VMEM((192, W1), F32),
                pltpu.VMEM((192, W1), BF),
                pltpu.VMEM((384, W2), BF),
                pltpu.VMEM((384, W1), BF),
            ],
            compiler_params=PARAMS,
            cost_estimate=pl.CostEstimate(flops=2_000_000_000, bytes_accessed=6_000_000, transcendentals=0),
            name="pyramid",
        )(place, *groups[step], *taps)
        other, *detail = lax.optimization_barrier((other, *detail))
        details += detail
        lse = join_lse(lse, other)

    left, right = pl.pallas_call(
        mix_kernel,
        out_shape=(jax.ShapeDtypeStruct((3, 32, 256), F32),) * 2,
        in_specs=smem() + vmem(13),
        out_specs=tuple(vmem(2)),
        scratch_shapes=[
            pltpu.VMEM((8, 64, W0), F32),
            pltpu.VMEM((512, W0), BF),
            pltpu.VMEM((256, W1), F32),
            pltpu.VMEM((256, W1), BF),
            pltpu.VMEM((192, W2), BF),
            pltpu.VMEM((192, W1), BF),
        ],
        compiler_params=PARAMS,
        name="mix",
    )(place, *logits, lse, *details, *taps)

    for a, b in ((1, 3), (3, 1)):
        left_in, right_in = partner(left, a), partner(right, b)
        left, right = left + left_in, right + right_in
    whole = jnp.concatenate([left, right], axis=-1)
    joined = lax.all_to_all(jnp.broadcast_to(whole, (4, 3, 32, 512)), "x", 0, 0)
    return joined.transpose(1, 2, 0, 3).reshape(3, 32, 2048)


def solution(mesh):
    fine = Mesh(mesh.devices.reshape(4, 4, 2, 4, 4), ROWS + GZ)
    return jax.shard_map(
        on_device,
        mesh=fine,
        in_specs=(P(GZ, None, ROWS, None), P(GZ)),
        out_specs=P(None, ROWS, None),
        check_vma=False,
    )
```

```python
import functools

import jax
import jax.numpy as jnp
import numpy as np
from jax import lax
from jax.experimental import pallas as pl
from jax.experimental.pallas import tpu as pltpu
from jax.sharding import Mesh
from jax.sharding import PartitionSpec as P

ROWS = ("zl", "y", "c")
GZ = ("zh", "x")
BF = jnp.bfloat16
F32 = jnp.float32
GREY = (0.299 / 255.0, 0.587 / 255.0, 0.114 / 255.0)
W0, W1, W2 = 640, 384, 256
M0, M1, M2 = 512, 256, 128
FLIPS = (0, 1, 3, 2)
PARAMS = pltpu.CompilerParams(vmem_limit_bytes=20 * 1024 * 1024)


def lane_of(col, main, wide):
    if 0 <= col < main + 64:
        return col
    if -64 <= col < 0:
        return wide + col
    return None


def column_taps(kind, main_in, wide_in, main_out, wide_out):
    taps = np.zeros((wide_in, wide_out), np.float32)
    for lane in range(wide_out):
        col = lane if lane < main_out + 64 else lane - wide_out
        if kind == "down":
            picks = [(2 * col + d, t / 16.0) for d, t in zip(range(-2, 3), (1, 4, 6, 4, 1))]
        elif col % 2 == 0:
            picks = [(col // 2 - 1, 0.125), (col // 2, 0.75), (col // 2 + 1, 0.125)]
        else:
            picks = [(col // 2, 0.5), (col // 2 + 1, 0.5)]
        for source, tap in picks:
            at = lane_of(source, main_in, wide_in)
            if at is not None:
                taps[at, lane] += tap
    return taps


def pack_kernel(samples_ref, gain_hbm_ref, *refs):
    packed_refs, (held_ref, gain_ref, out_ref, sems, gain_sem, out_sems) = refs[:4], refs[4:]
    copies = []
    for a in range(6):
        p, c = divmod(a, 3)
        copies.append(pltpu.make_async_copy(samples_ref.at[p, c], held_ref.at[a], sems.at[a]))
        copies[a].start()
    gain_copy = pltpu.make_async_copy(gain_hbm_ref, gain_ref, gain_sem)
    gain_copy.start()
    mine = lax.axis_index("x")
    lane = lax.broadcasted_iota(jnp.int32, (16, 128), 1)
    written = []
    for m, flip in enumerate(FLIPS):
        j = mine ^ flip
        base = pl.multiple_of(512 * j, 512)
        before = pl.multiple_of(jnp.maximum(base - 128, 0), 128)
        after = pl.multiple_of(jnp.minimum(base + 512, 1920), 128)
        has_before, has_after = j > 0, j < 3
        for a in range(6):
            if m == 0:
                copies[a].wait()
            for h in range(2):
                out_ref[m, h, 16 * a : 16 * a + 16, :] = held_ref[a, 16 * h : 16 * h + 16, pl.ds(base, 512)].astype(F32)
        if m == 0:
            gain_copy.wait()
        for h in range(2):
            rows = slice(16 * h, 16 * h + 16)
            tiles = [
                jnp.zeros((16, 128), F32),
                jnp.where(lane < 64, 0.0, jnp.where(lane < 96, gain_ref[0], gain_ref[1])),
            ]
            for a in range(6):
                at, t = 32 * (a % 4), a // 4
                piece = pltpu.roll(held_ref[a, rows, pl.ds(before, 128)].astype(F32), (at - 112) % 128, 1)
                piece = jnp.where(has_before, piece, 0.0)
                tiles[t] = jnp.where((lane >= at) & (lane < at + 16), piece, tiles[t])
                piece = pltpu.roll(held_ref[a, rows, pl.ds(after, 128)].astype(F32), (at + 16) % 128, 1)
                piece = jnp.where(has_after, piece, 0.0)
                tiles[t] = jnp.where((lane >= at + 16) & (lane < at + 32), piece, tiles[t])
            out_ref[m, h, 96:104, 0:128] = tiles[0][0:8]
            out_ref[m, h, 96:104, 128:256] = tiles[1][0:8]
            out_ref[m, h, 96:104, 256:384] = tiles[0][8:16]
            out_ref[m, h, 96:104, 384:512] = tiles[1][8:16]
        written.append(pltpu.make_async_copy(out_ref.at[m], packed_refs[m], out_sems.at[m]))
        written[m].start()
    for copy in written:
        copy.wait()


class Strips:
    def __init__(self, place_ref, mains, near_ref, far_ref):
        self.even = place_ref[2] == 0
        self.mains, self.near, self.far = mains, near_ref, far_ref

    def get(self, s, b, rows, cols):
        if b in (1, 2):
            return self.mains[s][b - 1, rows, cols]
        near, far = self.near[s, rows, cols], self.far[s, rows, cols]
        return jnp.where(self.even, far, near) if b == 0 else jnp.where(self.even, near, far)

    def samples(self, s, b, a):
        return self.get(s, b, slice(16 * a, 16 * a + 16), slice(0, M0))

    def halo(self, s, b, a):
        return halo_tile(lambda cols: self.get(s, b, slice(96, 104), cols), a)


def halo_tile(read, a):
    base, at = 128 * (a // 4), 32 * (a % 4)
    tile = jnp.concatenate([read(slice(base, base + 128)), read(slice(256 + base, 384 + base))], axis=0)
    lane = lax.broadcasted_iota(jnp.int32, (16, 128), 1)
    return jnp.where((lane < 16) | (lane >= 112), pltpu.roll(tile, (112 - at) % 128, 1), 0.0)


def column_of(shape, main, wide):
    lane = lax.broadcasted_iota(jnp.int32, shape, len(shape) - 1)
    return jnp.where(lane < main + 64, lane, lane - wide)


def energy_kernel(second, place_ref, main_a_ref, main_b_ref, near_ref, far_ref, *refs):
    earlier_ref, logit_ref, lse_ref, grey_ref = refs if second else (None, refs[0], None, refs[1])
    row = lax.broadcasted_iota(jnp.int32, (64, W0), 0) + (place_ref[0] * 32 - 16)
    col = column_of((64, W0), M0, W0) + place_ref[1] * M0
    keep = (row >= 0) & (row < 1024) & (col >= 0) & (col < 2048)

    mains = (main_a_ref, main_b_ref)
    strips = Strips(place_ref, mains, near_ref, far_ref)
    for s in range(2):
        for p in range(2):
            for b in range(4):
                main = 0.0
                tile = 0.0
                for c in range(3):
                    a = 3 * p + c
                    main = main + strips.samples(s, b, a) * GREY[c]
                    tile = tile + strips.halo(s, b, a) * GREY[c]
                grey_ref[16 * b : 16 * b + 16, 0:M0] = main
                grey_ref[16 * b : 16 * b + 16, M0:W0] = tile
            grey = grey_ref[...]
            lap = (
                4.0 * grey
                - pltpu.roll(grey, 1, 0)
                - pltpu.roll(grey, 63, 0)
                - pltpu.roll(grey, 1, 1)
                - pltpu.roll(grey, W0 - 1, 1)
            )
            field = jnp.where(keep, lap * lap, 0.0)
            for axis, size in ((0, 64), (1, W0)):
                two = field + pltpu.roll(field, size - 1, axis)
                four = two + pltpu.roll(two, size - 2, axis)
                eight = four + pltpu.roll(four, size - 4, axis)
                field = pltpu.roll(eight, 4, axis) + pltpu.roll(field, size - 4, axis)
            gain = mains[s][0, 96:97, 192 + 32 * p : 193 + 32 * p]
            logit_ref[2 * s + p] = gain * field

    if second:
        logits = [ref.at[i] for ref in (earlier_ref, logit_ref) for i in range(4)]
        peak = logits[0][...]
        for ref in logits[1:]:
            peak = jnp.maximum(peak, ref[...])
        total = 0.0
        for ref in logits:
            total = total + jnp.exp(ref[...] - peak)
        lse_ref[...] = pltpu.roll(peak + jnp.log(total), 58, 0)[0:56]


def split2(value):
    high = value.astype(BF)
    low = (value - high.astype(F32)).astype(BF)
    return high, low


def stacked(value):
    return jnp.concatenate(split2(value), axis=0)


def dot(a, b):
    return jnp.dot(a, b, preferred_element_type=F32)


def iota2(shape):
    return lax.broadcasted_iota(jnp.int32, shape, 0), lax.broadcasted_iota(jnp.int32, shape, 1)


def down_rows(count, inputs, copies, first, limit):
    q, e = iota2((count, inputs * copies))
    if copies == 2:
        e = jnp.where(e >= inputs, e - inputs, e)
    gap = jnp.abs(e - 2 * q)
    taps = jnp.where(gap == 0, 0.375, jnp.where(gap == 1, 0.25, jnp.where(gap == 2, 0.0625, 0.0)))
    inside = (q + first >= 0) & (q + first < limit)
    return jnp.where(inside, taps, 0.0).astype(BF)


def up_rows(count, inputs, offset, first, limit):
    r, q = iota2((count, 2 * inputs))
    q = jnp.where(q >= inputs, q - inputs, q)
    gap = jnp.abs(2 * q - (r + offset))
    even = (r & 1) == 0
    taps = jnp.where(
        even,
        jnp.where(gap == 0, 0.75, jnp.where(gap == 2, 0.125, 0.0)),
        jnp.where(gap == 1, 0.5, 0.0),
    )
    inside = (r + first >= 0) & (r + first < limit)
    return jnp.where(inside, taps, 0.0).astype(BF)


def row_matrices(strip):
    v2 = down_rows(16, 32, 2, strip * 8 - 4, 256)
    p2 = up_rows(32, 16, 0, strip * 16 - 8, 512)
    p1 = up_rows(32, 32, 16, 0, 32)
    return v2, p2, p1


def level_masks(rows1, rows2, k):
    col1 = column_of((rows1, W1), M1, W1) + k * M1
    col2 = column_of((rows2, W2), M2, W2) + k * M2
    return (col1 >= 0) & (col1 < 1024), (col2 >= 0) & (col2 < 512)


def put(ref, n, a, count, value):
    high, low = split2(value)
    ref[a * count : (a + 1) * count] = high
    ref[(n + a) * count : (n + a + 1) * count] = low


def resampled(source_ref, taps_ref):
    both = dot(source_ref[...], taps_ref[...])
    half = both.shape[0] // 2
    return both[:half] + both[half:]


def pyramid_kernel(
    place_ref, main_a_ref, main_b_ref, near_ref, far_ref, d1_ref, d2_ref, u2_ref, u1_ref,
    detail0_ref, detail1_ref, l2_ref, x_ref, s1_ref, l1_ref, s2_ref, s3_ref, s4_ref,
):
    strip = place_ref[0]
    v1 = down_rows(32, 64, 1, strip * 16 - 8, 512)
    v2, p2, p1 = row_matrices(strip)
    inside1, inside2 = level_masks(192, 96, place_ref[1])
    mains = (main_a_ref, main_b_ref)
    strips = Strips(place_ref, mains, near_ref, far_ref)
    for i in range(2):
        for a in range(6):
            for b in range(4):
                x_ref[16 * b : 16 * b + 16, 0:M0] = strips.samples(i, b, a).astype(BF)
                x_ref[16 * b : 16 * b + 16, M0:W0] = strips.halo(i, b, a).astype(BF)
            put(s1_ref, 6, a, 32, dot(v1, x_ref[...]))
        l1_ref[...] = jnp.where(inside1, resampled(s1_ref, d1_ref), 0.0)
        for a in range(6):
            both = stacked(l1_ref[a * 32 : a * 32 + 32])
            put(s2_ref, 6, a, 16, dot(v2, both))
            put(s4_ref, 6, a, 32, dot(p1, both))
        l2 = jnp.where(inside2, resampled(s2_ref, d2_ref), 0.0)
        l2_ref[i * 96 : i * 96 + 96] = l2
        for a in range(6):
            put(s3_ref, 6, a, 32, dot(p2, stacked(l2[a * 16 : a * 16 + 16])))
        detail1_ref[i * 192 : i * 192 + 192] = l1_ref[...] - resampled(s3_ref, u2_ref)
        part = resampled(s4_ref, u1_ref)
        for a in range(6):
            for h in range(2):
                at = a * 32 + 16 * h
                detail0_ref[i * 192 + at : i * 192 + at + 16] = (
                    mains[i][h, 16 * a : 16 * a + 16, :] - part[at : at + 16]
                )


def mix_kernel(
    place_ref, logit_a_ref, logit_b_ref, lse_ref,
    fine_a_ref, mid_a_ref, low_a_ref, fine_b_ref, mid_b_ref, low_b_ref,
    d1_ref, d2_ref, u2_ref, u1_ref,
    out_ref, w0_ref, s1_ref, w1_ref, s2_ref, s3_ref, s4_ref,
):
    strip, k = place_ref[0], place_ref[1]
    v1 = down_rows(32, 64, 2, strip * 16 - 8, 512)
    v2, p2, p1 = row_matrices(strip)
    col = column_of((16, W0), M0, W0)
    inside_col = (col >= -10) & (col <= 522) & (col + k * M0 >= 0) & (col + k * M0 < 2048)
    row = lax.broadcasted_iota(jnp.int32, (16, W0), 0)
    lse = pltpu.roll(jnp.concatenate([lse_ref[...], jnp.zeros((8, W0), F32)], axis=0), 6, 0)
    keeps = []
    for b in range(4):
        r = row + (16 * b - 16)
        g = r + strip * 32
        keeps.append(inside_col & (r >= -10) & (r <= 42) & (g >= 0) & (g < 1024))
    for i in range(8):
        logit_ref = (logit_a_ref, logit_b_ref)[i // 4]
        for b in range(4):
            rows = slice(16 * b, 16 * b + 16)
            w0_ref[i, rows] = jnp.where(keeps[b], jnp.exp(logit_ref[i % 4, rows] - lse[rows]), 0.0)
        put(s1_ref, 8, i, 32, dot(v1, stacked(w0_ref[i])))
    inside1, inside2 = level_masks(32, 16, k)
    w1_ref[...] = resampled(s1_ref, d1_ref)
    for i in range(8):
        w1 = jnp.where(inside1, w1_ref[i * 32 : i * 32 + 32], 0.0)
        w1_ref[i * 32 : i * 32 + 32] = w1
        put(s2_ref, 8, i, 16, dot(v2, stacked(w1)))
    w2 = resampled(s2_ref, d2_ref)

    def piece(pair, i, c, rows):
        ref = pair[i // 4]
        at = ((i % 4) * 3 + c) * rows
        return ref[at : at + rows]

    for c in range(3):
        blend2 = 0.0
        for i in range(8):
            blend2 = blend2 + w2[i * 16 : i * 16 + 16] * piece((low_a_ref, low_b_ref), i, c, 16)
        put(s3_ref, 3, c, 32, dot(p2, stacked(blend2)))
    rise = resampled(s3_ref, u2_ref)
    for c in range(3):
        total = jnp.where(inside1, rise[c * 32 : c * 32 + 32], 0.0)
        for i in range(8):
            total = total + w1_ref[i * 32 : i * 32 + 32] * piece((mid_a_ref, mid_b_ref), i, c, 32)
        put(s4_ref, 3, c, 32, dot(p1, stacked(total)))
    rise = resampled(s4_ref, u1_ref)
    for c in range(3):
        total = rise[c * 32 : c * 32 + 32]
        for i in range(8):
            total = total + w0_ref[i, 16:48, 0:M0] * piece((fine_a_ref, fine_b_ref), i, c, 32)
        out_ref[c] = total * (1.0 / 255.0)


def vmem(count):
    return [pl.BlockSpec(memory_space=pltpu.VMEM)] * count


def smem():
    return [pl.BlockSpec(memory_space=pltpu.SMEM)]


def neighbours(group, core):
    count = lax.axis_size(ROWS)
    swaps = [(i, i + 1) for i in range(1, count - 1, 2)]
    swaps += [(b, a) for a, b in swaps]

    def half(index):
        return jnp.stack([lax.dynamic_index_in_dim(main, index, axis=0, keepdims=False) for main in group])

    return lax.ppermute(half(1 - core), "c", [(0, 1), (1, 0)]), lax.ppermute(half(core), ROWS, swaps)


def crossed(value, flips):
    pairs = [(4 * low + i, 4 * low + (i ^ flips[low % 2])) for low in range(4) for i in range(4)]
    return lax.ppermute(value, ("zl", "zh"), pairs)


def join_lse(a, b):
    return jnp.maximum(a, b) + jnp.log(1.0 + jnp.exp(-jnp.abs(a - b)))


def on_device(samples, gain):
    samples, strip, column, core = lax.optimization_barrier(
        (samples, lax.axis_index(ROWS), lax.axis_index("x"), lax.axis_index("c"))
    )
    packed = pl.pallas_call(
        pack_kernel,
        out_shape=(jax.ShapeDtypeStruct((2, 104, 512), F32),) * 4,
        in_specs=[pl.BlockSpec(memory_space=pltpu.HBM)] * 2,
        out_specs=(pl.BlockSpec(memory_space=pltpu.HBM),) * 4,
        scratch_shapes=[
            pltpu.VMEM((6, 32, 2048), jnp.int32),
            pltpu.SMEM((2,), F32),
            pltpu.VMEM((4, 2, 104, 512), F32),
            pltpu.SemaphoreType.DMA((6,)),
            pltpu.SemaphoreType.DMA,
            pltpu.SemaphoreType.DMA((4,)),
        ],
        compiler_params=pltpu.CompilerParams(vmem_limit_bytes=60 * 1024 * 1024),
        name="pack",
    )(samples, gain)
    mains = [packed[0]] + [
        lax.ppermute(packed[m], "x", [(i, i ^ FLIPS[m]) for i in range(4)]) for m in (1, 2, 3)
    ]
    place = jnp.stack([strip, column, core]).astype(jnp.int32)
    groups = [(*pair, *neighbours(pair, core)) for pair in (mains[:2], mains[2:])]
    logit_shape = jax.ShapeDtypeStruct((4, 64, W0), F32)

    def energy(step, *earlier):
        return pl.pallas_call(
            functools.partial(energy_kernel, step == 1),
            out_shape=(logit_shape,) + (jax.ShapeDtypeStruct((56, W0), F32),) * step,
            in_specs=smem() + vmem(4 + step),
            out_specs=tuple(vmem(1 + step)),
            scratch_shapes=[pltpu.VMEM((64, W0), F32)],
            compiler_params=PARAMS,
            cost_estimate=pl.CostEstimate(flops=2_000_000_000, bytes_accessed=6_000_000, transcendentals=0),
            name="energy",
        )(place, *groups[step], *earlier)

    logits = energy(0)
    *more, lse = energy(1, *logits)
    logits = [*logits, *more]

    taps = [
        jnp.asarray(t, BF)
        for t in (
            column_taps("down", M0, W0, M1, W1),
            column_taps("down", M1, W1, M2, W2),
            column_taps("up", M2, W2, M1, W1),
            column_taps("up", M1, W1, M0, W0)[:, :M0],
        )
    ]
    details = []
    for step, flips in enumerate(((1, 3), (3, 1))):
        other = crossed(lse, flips)
        detail = pl.pallas_call(
            pyramid_kernel,
            out_shape=(
                jax.ShapeDtypeStruct((384, M0), F32),
                jax.ShapeDtypeStruct((384, W1), F32),
                jax.ShapeDtypeStruct((192, W2), F32),
            ),
            in_specs=smem() + vmem(8),
            out_specs=tuple(vmem(3)),
            scratch_shapes=[
                pltpu.VMEM((64, W0), BF),
                pltpu.VMEM((384, W0), BF),
                pltpu.VMEM((192, W1), F32),
                pltpu.VMEM((192, W1), BF),
                pltpu.VMEM((384, W2), BF),
                pltpu.VMEM((384, W1), BF),
            ],
            compiler_params=PARAMS,
            cost_estimate=pl.CostEstimate(flops=2_000_000_000, bytes_accessed=6_000_000, transcendentals=0),
            name="pyramid",
        )(place, *groups[step], *taps)
        other, *detail = lax.optimization_barrier((other, *detail))
        details += detail
        lse = join_lse(lse, other)

    whole = pl.pallas_call(
        mix_kernel,
        out_shape=jax.ShapeDtypeStruct((3, 32, M0), F32),
        in_specs=smem() + vmem(13),
        out_specs=vmem(1)[0],
        scratch_shapes=[
            pltpu.VMEM((8, 64, W0), F32),
            pltpu.VMEM((512, W0), BF),
            pltpu.VMEM((256, W1), F32),
            pltpu.VMEM((256, W1), BF),
            pltpu.VMEM((192, W2), BF),
            pltpu.VMEM((192, W1), BF),
        ],
        compiler_params=PARAMS,
        name="mix",
    )(place, *logits, lse, *details, *taps)

    for flips in ((1, 3), (3, 1)):
        whole = whole + crossed(whole, flips)
    joined = lax.all_to_all(jnp.broadcast_to(whole, (4, 3, 32, 512)), "x", 0, 0)
    return joined.transpose(1, 2, 0, 3).reshape(3, 32, 2048)


def solution(mesh):
    fine = Mesh(mesh.devices.reshape(4, 4, 2, 4, 4), ROWS + GZ)
    return jax.shard_map(
        on_device,
        mesh=fine,
        in_specs=(P(GZ, None, ROWS, None), P(GZ)),
        out_specs=P(None, ROWS, None),
        check_vma=False,
    )
```

```python
import functools

import jax
import jax.numpy as jnp
import numpy as np
from jax import lax
from jax.experimental import pallas as pl
from jax.experimental.pallas import tpu as pltpu
from jax.sharding import Mesh
from jax.sharding import PartitionSpec as P

ROWS = ("zl", "y", "c")
GZ = ("zh", "x")
BF = jnp.bfloat16
F32 = jnp.float32
GREY = (0.299 / 255.0, 0.587 / 255.0, 0.114 / 255.0)
W0, W1, W2 = 640, 384, 256
M0, M1, M2 = 512, 256, 128
FLIPS = (0, 1, 3, 2)
PARAMS = pltpu.CompilerParams(vmem_limit_bytes=20 * 1024 * 1024)


def lane_of(col, main, wide):
    if 0 <= col < main + 64:
        return col
    if -64 <= col < 0:
        return wide + col
    return None


def column_taps(kind, main_in, wide_in, main_out, wide_out):
    taps = np.zeros((wide_in, wide_out), np.float32)
    for lane in range(wide_out):
        col = lane if lane < main_out + 64 else lane - wide_out
        if kind == "down":
            picks = [(2 * col + d, t / 16.0) for d, t in zip(range(-2, 3), (1, 4, 6, 4, 1))]
        elif col % 2 == 0:
            picks = [(col // 2 - 1, 0.125), (col // 2, 0.75), (col // 2 + 1, 0.125)]
        else:
            picks = [(col // 2, 0.5), (col // 2 + 1, 0.5)]
        for source, tap in picks:
            at = lane_of(source, main_in, wide_in)
            if at is not None:
                taps[at, lane] += tap
    return taps


def pack_kernel(samples_ref, gain_hbm_ref, *refs):
    packed_refs, (held_ref, gain_ref, out_ref, sems, gain_sem, out_sems) = refs[:4], refs[4:]
    copies = []
    for a in range(6):
        p, c = divmod(a, 3)
        copies.append(pltpu.make_async_copy(samples_ref.at[p, c], held_ref.at[a], sems.at[a]))
        copies[a].start()
    gain_copy = pltpu.make_async_copy(gain_hbm_ref, gain_ref, gain_sem)
    gain_copy.start()
    mine = lax.axis_index("x")
    lane = lax.broadcasted_iota(jnp.int32, (16, 128), 1)
    written = []
    for m, flip in enumerate(FLIPS):
        j = mine ^ flip
        base = pl.multiple_of(512 * j, 512)
        before = pl.multiple_of(jnp.maximum(base - 128, 0), 128)
        after = pl.multiple_of(jnp.minimum(base + 512, 1920), 128)
        has_before, has_after = j > 0, j < 3
        for a in range(6):
            if m == 0:
                copies[a].wait()
            for h in range(2):
                out_ref[m, h, 16 * a : 16 * a + 16, :] = held_ref[a, 16 * h : 16 * h + 16, pl.ds(base, 512)].astype(F32)
        if m == 0:
            gain_copy.wait()
        for h in range(2):
            rows = slice(16 * h, 16 * h + 16)
            tiles = [
                jnp.zeros((16, 128), F32),
                jnp.where(lane < 64, 0.0, jnp.where(lane < 96, gain_ref[0], gain_ref[1])),
            ]
            for a in range(6):
                at, t = 32 * (a % 4), a // 4
                piece = pltpu.roll(held_ref[a, rows, pl.ds(before, 128)].astype(F32), (at - 112) % 128, 1)
                piece = jnp.where(has_before, piece, 0.0)
                tiles[t] = jnp.where((lane >= at) & (lane < at + 16), piece, tiles[t])
                piece = pltpu.roll(held_ref[a, rows, pl.ds(after, 128)].astype(F32), (at + 16) % 128, 1)
                piece = jnp.where(has_after, piece, 0.0)
                tiles[t] = jnp.where((lane >= at + 16) & (lane < at + 32), piece, tiles[t])
            out_ref[m, h, 96:104, 0:128] = tiles[0][0:8]
            out_ref[m, h, 96:104, 128:256] = tiles[1][0:8]
            out_ref[m, h, 96:104, 256:384] = tiles[0][8:16]
            out_ref[m, h, 96:104, 384:512] = tiles[1][8:16]
        written.append(pltpu.make_async_copy(out_ref.at[m], packed_refs[m], out_sems.at[m]))
        written[m].start()
    for copy in written:
        copy.wait()


class Strips:
    def __init__(self, place_ref, mains, near_ref, far_ref):
        self.even = place_ref[2] == 0
        self.mains, self.near, self.far = mains, near_ref, far_ref

    def get(self, s, b, rows, cols):
        if b in (1, 2):
            return self.mains[s][b - 1, rows, cols]
        near, far = self.near[s, rows, cols], self.far[s, rows, cols]
        return jnp.where(self.even, far, near) if b == 0 else jnp.where(self.even, near, far)

    def samples(self, s, b, a):
        return self.get(s, b, slice(16 * a, 16 * a + 16), slice(0, M0))

    def halo(self, s, b, a):
        return halo_tile(lambda cols: self.get(s, b, slice(96, 104), cols), a)


def halo_tile(read, a):
    base, at = 128 * (a // 4), 32 * (a % 4)
    tile = jnp.concatenate([read(slice(base, base + 128)), read(slice(256 + base, 384 + base))], axis=0)
    lane = lax.broadcasted_iota(jnp.int32, (16, 128), 1)
    return jnp.where((lane < 16) | (lane >= 112), pltpu.roll(tile, (112 - at) % 128, 1), 0.0)


def column_of(shape, main, wide):
    lane = lax.broadcasted_iota(jnp.int32, shape, len(shape) - 1)
    return jnp.where(lane < main + 64, lane, lane - wide)


def energy_kernel(second, place_ref, main_a_ref, main_b_ref, near_ref, far_ref, *refs):
    earlier_ref, logit_ref, lse_ref, grey_ref = refs if second else (None, refs[0], None, refs[1])
    row = lax.broadcasted_iota(jnp.int32, (64, W0), 0) + (place_ref[0] * 32 - 16)
    col = column_of((64, W0), M0, W0) + place_ref[1] * M0
    keep = (row >= 0) & (row < 1024) & (col >= 0) & (col < 2048)

    mains = (main_a_ref, main_b_ref)
    strips = Strips(place_ref, mains, near_ref, far_ref)
    for s in range(2):
        for p in range(2):
            for b in range(4):
                main = 0.0
                tile = 0.0
                for c in range(3):
                    a = 3 * p + c
                    main = main + strips.samples(s, b, a) * GREY[c]
                    tile = tile + strips.halo(s, b, a) * GREY[c]
                grey_ref[16 * b : 16 * b + 16, 0:M0] = main
                grey_ref[16 * b : 16 * b + 16, M0:W0] = tile
            grey = grey_ref[...]
            lap = (
                4.0 * grey
                - pltpu.roll(grey, 1, 0)
                - pltpu.roll(grey, 63, 0)
                - pltpu.roll(grey, 1, 1)
                - pltpu.roll(grey, W0 - 1, 1)
            )
            field = jnp.where(keep, lap * lap, 0.0)
            for axis, size in ((0, 64), (1, W0)):
                two = field + pltpu.roll(field, size - 1, axis)
                four = two + pltpu.roll(two, size - 2, axis)
                eight = four + pltpu.roll(four, size - 4, axis)
                field = pltpu.roll(eight, 4, axis) + pltpu.roll(field, size - 4, axis)
            gain = mains[s][0, 96:97, 192 + 32 * p : 193 + 32 * p]
            logit_ref[2 * s + p] = gain * field

    if second:
        logits = [ref.at[i] for ref in (earlier_ref, logit_ref) for i in range(4)]
        peak = logits[0][...]
        for ref in logits[1:]:
            peak = jnp.maximum(peak, ref[...])
        total = 0.0
        for ref in logits:
            total = total + jnp.exp(ref[...] - peak)
        lse_ref[...] = pltpu.roll(peak + jnp.log(total), 58, 0)[0:56]


def split2(value):
    high = value.astype(BF)
    low = (value - high.astype(F32)).astype(BF)
    return high, low


def stacked(value):
    return jnp.concatenate(split2(value), axis=0)


def dot(a, b):
    return jnp.dot(a, b, preferred_element_type=F32)


def iota2(shape):
    return lax.broadcasted_iota(jnp.int32, shape, 0), lax.broadcasted_iota(jnp.int32, shape, 1)


def down_rows(count, inputs, copies, first, limit):
    q, e = iota2((count, inputs * copies))
    if copies == 2:
        e = jnp.where(e >= inputs, e - inputs, e)
    gap = jnp.abs(e - 2 * q)
    taps = jnp.where(gap == 0, 0.375, jnp.where(gap == 1, 0.25, jnp.where(gap == 2, 0.0625, 0.0)))
    inside = (q + first >= 0) & (q + first < limit)
    return jnp.where(inside, taps, 0.0).astype(BF)


def up_rows(count, inputs, offset, first, limit):
    r, q = iota2((count, 2 * inputs))
    q = jnp.where(q >= inputs, q - inputs, q)
    gap = jnp.abs(2 * q - (r + offset))
    even = (r & 1) == 0
    taps = jnp.where(
        even,
        jnp.where(gap == 0, 0.75, jnp.where(gap == 2, 0.125, 0.0)),
        jnp.where(gap == 1, 0.5, 0.0),
    )
    inside = (r + first >= 0) & (r + first < limit)
    return jnp.where(inside, taps, 0.0).astype(BF)


def row_matrices(strip):
    v2 = down_rows(16, 32, 2, strip * 8 - 4, 256)
    p2 = up_rows(32, 16, 0, strip * 16 - 8, 512)
    p1 = up_rows(32, 32, 16, 0, 32)
    return v2, p2, p1


def level_masks(rows1, rows2, k):
    col1 = column_of((rows1, W1), M1, W1) + k * M1
    col2 = column_of((rows2, W2), M2, W2) + k * M2
    return (col1 >= 0) & (col1 < 1024), (col2 >= 0) & (col2 < 512)


def put(ref, n, a, count, value):
    high, low = split2(value)
    ref[a * count : (a + 1) * count] = high
    ref[(n + a) * count : (n + a + 1) * count] = low


def resampled(source_ref, taps_ref):
    both = dot(source_ref[...], taps_ref[...])
    half = both.shape[0] // 2
    return both[:half] + both[half:]


def pyramid_kernel(
    place_ref, main_a_ref, main_b_ref, near_ref, far_ref, d1_ref, d2_ref, u2_ref, u1_ref,
    detail0_ref, detail1_ref, l2_ref, x_ref, s1_ref, l1_ref, s2_ref, s3_ref, s4_ref,
):
    strip = place_ref[0]
    v1 = down_rows(32, 64, 1, strip * 16 - 8, 512)
    v2, p2, p1 = row_matrices(strip)
    inside1, inside2 = level_masks(192, 96, place_ref[1])
    mains = (main_a_ref, main_b_ref)
    strips = Strips(place_ref, mains, near_ref, far_ref)
    for i in range(2):
        for a in range(6):
            for b in range(4):
                x_ref[16 * b : 16 * b + 16, 0:M0] = strips.samples(i, b, a).astype(BF)
                x_ref[16 * b : 16 * b + 16, M0:W0] = strips.halo(i, b, a).astype(BF)
            put(s1_ref, 6, a, 32, dot(v1, x_ref[...]))
        l1_ref[...] = jnp.where(inside1, resampled(s1_ref, d1_ref), 0.0)
        for a in range(6):
            both = stacked(l1_ref[a * 32 : a * 32 + 32])
            put(s2_ref, 6, a, 16, dot(v2, both))
            put(s4_ref, 6, a, 32, dot(p1, both))
        l2 = jnp.where(inside2, resampled(s2_ref, d2_ref), 0.0)
        l2_ref[i * 96 : i * 96 + 96] = l2
        for a in range(6):
            put(s3_ref, 6, a, 32, dot(p2, stacked(l2[a * 16 : a * 16 + 16])))
        detail1_ref[i * 192 : i * 192 + 192] = l1_ref[...] - resampled(s3_ref, u2_ref)
        part = resampled(s4_ref, u1_ref)
        for a in range(6):
            for h in range(2):
                at = a * 32 + 16 * h
                detail0_ref[i * 192 + at : i * 192 + at + 16] = (
                    mains[i][h, 16 * a : 16 * a + 16, :] - part[at : at + 16]
                )


def mix_kernel(
    place_ref, logit_a_ref, logit_b_ref, lse_ref,
    fine_a_ref, mid_a_ref, low_a_ref, fine_b_ref, mid_b_ref, low_b_ref,
    d1_ref, d2_ref, u2_ref, u1_ref,
    left_ref, right_ref, w0_ref, s1_ref, w1_ref, s2_ref, s3_ref, s4_ref,
):
    strip, k = place_ref[0], place_ref[1]
    v1 = down_rows(32, 64, 2, strip * 16 - 8, 512)
    v2, p2, p1 = row_matrices(strip)
    col = column_of((16, W0), M0, W0)
    inside_col = (col >= -10) & (col <= 522) & (col + k * M0 >= 0) & (col + k * M0 < 2048)
    row = lax.broadcasted_iota(jnp.int32, (16, W0), 0)
    lse = pltpu.roll(jnp.concatenate([lse_ref[...], jnp.zeros((8, W0), F32)], axis=0), 6, 0)
    keeps = []
    for b in range(4):
        r = row + (16 * b - 16)
        g = r + strip * 32
        keeps.append(inside_col & (r >= -10) & (r <= 42) & (g >= 0) & (g < 1024))
    for i in range(8):
        logit_ref = (logit_a_ref, logit_b_ref)[i // 4]
        for b in range(4):
            rows = slice(16 * b, 16 * b + 16)
            w0_ref[i, rows] = jnp.where(keeps[b], jnp.exp(logit_ref[i % 4, rows] - lse[rows]), 0.0)
        put(s1_ref, 8, i, 32, dot(v1, stacked(w0_ref[i])))
    inside1, inside2 = level_masks(32, 16, k)
    w1_ref[...] = resampled(s1_ref, d1_ref)
    for i in range(8):
        w1 = jnp.where(inside1, w1_ref[i * 32 : i * 32 + 32], 0.0)
        w1_ref[i * 32 : i * 32 + 32] = w1
        put(s2_ref, 8, i, 16, dot(v2, stacked(w1)))
    w2 = resampled(s2_ref, d2_ref)

    def piece(pair, i, c, rows):
        ref = pair[i // 4]
        at = ((i % 4) * 3 + c) * rows
        return ref[at : at + rows]

    for c in range(3):
        blend2 = 0.0
        for i in range(8):
            blend2 = blend2 + w2[i * 16 : i * 16 + 16] * piece((low_a_ref, low_b_ref), i, c, 16)
        put(s3_ref, 3, c, 32, dot(p2, stacked(blend2)))
    rise = resampled(s3_ref, u2_ref)
    for c in range(3):
        total = jnp.where(inside1, rise[c * 32 : c * 32 + 32], 0.0)
        for i in range(8):
            total = total + w1_ref[i * 32 : i * 32 + 32] * piece((mid_a_ref, mid_b_ref), i, c, 32)
        put(s4_ref, 3, c, 32, dot(p1, stacked(total)))
    rise = resampled(s4_ref, u1_ref)
    for c in range(3):
        total = rise[c * 32 : c * 32 + 32]
        for i in range(8):
            total = total + w0_ref[i, 16:48, 0:M0] * piece((fine_a_ref, fine_b_ref), i, c, 32)
        total = total * (1.0 / 255.0)
        left_ref[c] = total[:, :256]
        right_ref[c] = total[:, 256:]


def vmem(count):
    return [pl.BlockSpec(memory_space=pltpu.VMEM)] * count


def smem():
    return [pl.BlockSpec(memory_space=pltpu.SMEM)]


def half(group, index):
    return jnp.stack([lax.dynamic_index_in_dim(main, index, axis=0, keepdims=False) for main in group])


def near_rows(group, core):
    return lax.ppermute(half(group, 1 - core), "c", [(0, 1), (1, 0)])


def far_rows(group, core):
    count = lax.axis_size(ROWS)
    swaps = [(i, i + 1) for i in range(1, count - 1, 2)]
    swaps += [(b, a) for a, b in swaps]
    return lax.ppermute(half(group, core), ROWS, swaps)


def partner(value, flip):
    return lax.ppermute(value, "zh", [(i, i ^ flip) for i in range(4)])


def crossed(value, flips):
    pairs = [(4 * c + i, 4 * c + (i ^ flip)) for c, flip in enumerate(flips) for i in range(4)]
    return lax.ppermute(value, ("c", "zh"), pairs)


def join_lse(a, b):
    return jnp.maximum(a, b) + jnp.log(1.0 + jnp.exp(-jnp.abs(a - b)))


def on_device(samples, gain):
    samples, strip, column, core = lax.optimization_barrier(
        (samples, lax.axis_index(ROWS), lax.axis_index("x"), lax.axis_index("c"))
    )
    packed = pl.pallas_call(
        pack_kernel,
        out_shape=(jax.ShapeDtypeStruct((2, 104, 512), F32),) * 4,
        in_specs=[pl.BlockSpec(memory_space=pltpu.HBM)] * 2,
        out_specs=(pl.BlockSpec(memory_space=pltpu.HBM),) * 4,
        scratch_shapes=[
            pltpu.VMEM((6, 32, 2048), jnp.int32),
            pltpu.SMEM((2,), F32),
            pltpu.VMEM((4, 2, 104, 512), F32),
            pltpu.SemaphoreType.DMA((6,)),
            pltpu.SemaphoreType.DMA,
            pltpu.SemaphoreType.DMA((4,)),
        ],
        compiler_params=pltpu.CompilerParams(vmem_limit_bytes=60 * 1024 * 1024),
        name="pack",
    )(samples, gain)
    mains = [packed[0]] + [
        lax.ppermute(packed[m], "x", [(i, i ^ FLIPS[m]) for i in range(4)]) for m in (1, 2, 3)
    ]
    place = jnp.stack([strip, column, core]).astype(jnp.int32)
    far = [far_rows(pair, core) for pair in (mains[:2], mains[2:])]
    logit_shape = jax.ShapeDtypeStruct((4, 64, W0), F32)

    def energy(step, group, *earlier):
        return pl.pallas_call(
            functools.partial(energy_kernel, step == 1),
            out_shape=(logit_shape,) + (jax.ShapeDtypeStruct((56, W0), F32),) * step,
            in_specs=smem() + vmem(4 + step),
            out_specs=tuple(vmem(1 + step)),
            scratch_shapes=[pltpu.VMEM((64, W0), F32)],
            compiler_params=PARAMS,
            cost_estimate=pl.CostEstimate(flops=2_000_000_000, bytes_accessed=6_000_000, transcendentals=0),
            name="energy",
        )(place, *group, *earlier)

    groups = [(*mains[:2], near_rows(mains[:2], core), far[0])]
    logits = energy(0, groups[0])
    late, _ = lax.optimization_barrier((mains[2:], logits))
    groups.append((*mains[2:], near_rows(late, core), far[1]))
    *more, lse = energy(1, groups[1], *logits)
    logits = [*logits, *more]

    taps = [
        jnp.asarray(t, BF)
        for t in (
            column_taps("down", M0, W0, M1, W1),
            column_taps("down", M1, W1, M2, W2),
            column_taps("up", M2, W2, M1, W1),
            column_taps("up", M1, W1, M0, W0)[:, :M0],
        )
    ]
    details = []
    for step, flips in enumerate(((1, 3), (3, 1))):
        other = crossed(lse, flips)
        detail = pl.pallas_call(
            pyramid_kernel,
            out_shape=(
                jax.ShapeDtypeStruct((384, M0), F32),
                jax.ShapeDtypeStruct((384, W1), F32),
                jax.ShapeDtypeStruct((192, W2), F32),
            ),
            in_specs=smem() + vmem(8),
            out_specs=tuple(vmem(3)),
            scratch_shapes=[
                pltpu.VMEM((64, W0), BF),
                pltpu.VMEM((384, W0), BF),
                pltpu.VMEM((192, W1), F32),
                pltpu.VMEM((192, W1), BF),
                pltpu.VMEM((384, W2), BF),
                pltpu.VMEM((384, W1), BF),
            ],
            compiler_params=PARAMS,
            cost_estimate=pl.CostEstimate(flops=2_000_000_000, bytes_accessed=6_000_000, transcendentals=0),
            name="pyramid",
        )(place, *groups[step], *taps)
        other, *detail = lax.optimization_barrier((other, *detail))
        details += detail
        lse = join_lse(lse, other)

    left, right = pl.pallas_call(
        mix_kernel,
        out_shape=(jax.ShapeDtypeStruct((3, 32, 256), F32),) * 2,
        in_specs=smem() + vmem(13),
        out_specs=tuple(vmem(2)),
        scratch_shapes=[
            pltpu.VMEM((8, 64, W0), F32),
            pltpu.VMEM((512, W0), BF),
            pltpu.VMEM((256, W1), F32),
            pltpu.VMEM((256, W1), BF),
            pltpu.VMEM((192, W2), BF),
            pltpu.VMEM((192, W1), BF),
        ],
        compiler_params=PARAMS,
        name="mix",
    )(place, *logits, lse, *details, *taps)

    for a, b in ((1, 3), (3, 1)):
        left_in, right_in = partner(left, a), partner(right, b)
        left, right = left + left_in, right + right_in
    whole = jnp.concatenate([left, right], axis=-1)
    joined = lax.all_to_all(jnp.broadcast_to(whole, (4, 3, 32, 512)), "x", 0, 0)
    return joined.transpose(1, 2, 0, 3).reshape(3, 32, 2048)


def solution(mesh):
    fine = Mesh(mesh.devices.reshape(4, 4, 2, 4, 4), ROWS + GZ)
    return jax.shard_map(
        on_device,
        mesh=fine,
        in_specs=(P(GZ, None, ROWS, None), P(GZ)),
        out_specs=P(None, ROWS, None),
        check_vma=False,
    )
```

```python
import functools

import jax
import jax.numpy as jnp
import numpy as np
from jax import lax
from jax.experimental import pallas as pl
from jax.experimental.pallas import tpu as pltpu
from jax.sharding import Mesh
from jax.sharding import PartitionSpec as P

ROWS = ("zl", "y", "c")
GZ = ("zh", "x")
BF = jnp.bfloat16
F32 = jnp.float32
GREY = (0.299 / 255.0, 0.587 / 255.0, 0.114 / 255.0)
W0, W1, W2 = 640, 384, 256
M0, M1, M2 = 512, 256, 128
FLIPS = (0, 2, 1, 3)
PARAMS = pltpu.CompilerParams(vmem_limit_bytes=20 * 1024 * 1024)


def lane_of(col, main, wide):
    if 0 <= col < main + 64:
        return col
    if -64 <= col < 0:
        return wide + col
    return None


def column_taps(kind, main_in, wide_in, main_out, wide_out):
    taps = np.zeros((wide_in, wide_out), np.float32)
    for lane in range(wide_out):
        col = lane if lane < main_out + 64 else lane - wide_out
        if kind == "down":
            picks = [(2 * col + d, t / 16.0) for d, t in zip(range(-2, 3), (1, 4, 6, 4, 1))]
        elif col % 2 == 0:
            picks = [(col // 2 - 1, 0.125), (col // 2, 0.75), (col // 2 + 1, 0.125)]
        else:
            picks = [(col // 2, 0.5), (col // 2 + 1, 0.5)]
        for source, tap in picks:
            at = lane_of(source, main_in, wide_in)
            if at is not None:
                taps[at, lane] += tap
    return taps


def pack_kernel(samples_ref, gain_hbm_ref, *refs):
    packed_refs, (held_ref, gain_ref, out_ref, sems, gain_sem, out_sems) = refs[:4], refs[4:]
    copies = []
    for a in range(6):
        p, c = divmod(a, 3)
        copies.append(pltpu.make_async_copy(samples_ref.at[p, c], held_ref.at[a], sems.at[a]))
        copies[a].start()
    gain_copy = pltpu.make_async_copy(gain_hbm_ref, gain_ref, gain_sem)
    gain_copy.start()
    mine = lax.axis_index("x")
    lane = lax.broadcasted_iota(jnp.int32, (16, 128), 1)
    written = []
    for m, flip in enumerate(FLIPS):
        j = mine ^ flip
        base = pl.multiple_of(512 * j, 512)
        before = pl.multiple_of(jnp.maximum(base - 128, 0), 128)
        after = pl.multiple_of(jnp.minimum(base + 512, 1920), 128)
        has_before, has_after = j > 0, j < 3
        for a in range(6):
            if m == 0:
                copies[a].wait()
            for h in range(2):
                out_ref[m, h, 16 * a : 16 * a + 16, :] = held_ref[a, 16 * h : 16 * h + 16, pl.ds(base, 512)].astype(F32)
        if m == 0:
            gain_copy.wait()
        for h in range(2):
            rows = slice(16 * h, 16 * h + 16)
            tiles = [
                jnp.zeros((16, 128), F32),
                jnp.where(lane < 64, 0.0, jnp.where(lane < 96, gain_ref[0], gain_ref[1])),
            ]
            for a in range(6):
                at, t = 32 * (a % 4), a // 4
                piece = pltpu.roll(held_ref[a, rows, pl.ds(before, 128)].astype(F32), (at - 112) % 128, 1)
                piece = jnp.where(has_before, piece, 0.0)
                tiles[t] = jnp.where((lane >= at) & (lane < at + 16), piece, tiles[t])
                piece = pltpu.roll(held_ref[a, rows, pl.ds(after, 128)].astype(F32), (at + 16) % 128, 1)
                piece = jnp.where(has_after, piece, 0.0)
                tiles[t] = jnp.where((lane >= at + 16) & (lane < at + 32), piece, tiles[t])
            out_ref[m, h, 96:104, 0:128] = tiles[0][0:8]
            out_ref[m, h, 96:104, 128:256] = tiles[1][0:8]
            out_ref[m, h, 96:104, 256:384] = tiles[0][8:16]
            out_ref[m, h, 96:104, 384:512] = tiles[1][8:16]
        written.append(pltpu.make_async_copy(out_ref.at[m], packed_refs[m], out_sems.at[m]))
        written[m].start()
    for copy in written:
        copy.wait()


class Strips:
    def __init__(self, place_ref, mains, near_ref, far_ref):
        self.even = place_ref[2] == 0
        self.mains, self.near, self.far = mains, near_ref, far_ref

    def get(self, s, b, rows, cols):
        if b in (1, 2):
            return self.mains[s][b - 1, rows, cols]
        near, far = self.near[s, rows, cols], self.far[s, rows, cols]
        return jnp.where(self.even, far, near) if b == 0 else jnp.where(self.even, near, far)

    def samples(self, s, b, a):
        return self.get(s, b, slice(16 * a, 16 * a + 16), slice(0, M0))

    def halo(self, s, b, a):
        return halo_tile(lambda cols: self.get(s, b, slice(96, 104), cols), a)


def halo_tile(read, a):
    base, at = 128 * (a // 4), 32 * (a % 4)
    tile = jnp.concatenate([read(slice(base, base + 128)), read(slice(256 + base, 384 + base))], axis=0)
    lane = lax.broadcasted_iota(jnp.int32, (16, 128), 1)
    return jnp.where((lane < 16) | (lane >= 112), pltpu.roll(tile, (112 - at) % 128, 1), 0.0)


def column_of(shape, main, wide):
    lane = lax.broadcasted_iota(jnp.int32, shape, len(shape) - 1)
    return jnp.where(lane < main + 64, lane, lane - wide)


def energy_kernel(second, place_ref, main_a_ref, main_b_ref, near_ref, far_ref, *refs):
    earlier_ref, logit_ref, lse_ref, grey_ref = refs if second else (None, refs[0], None, refs[1])
    row = lax.broadcasted_iota(jnp.int32, (64, W0), 0) + (place_ref[0] * 32 - 16)
    col = column_of((64, W0), M0, W0) + place_ref[1] * M0
    keep = (row >= 0) & (row < 1024) & (col >= 0) & (col < 2048)

    mains = (main_a_ref, main_b_ref)
    strips = Strips(place_ref, mains, near_ref, far_ref)
    for s in range(2):
        for p in range(2):
            for b in range(4):
                main = 0.0
                tile = 0.0
                for c in range(3):
                    a = 3 * p + c
                    main = main + strips.samples(s, b, a) * GREY[c]
                    tile = tile + strips.halo(s, b, a) * GREY[c]
                grey_ref[16 * b : 16 * b + 16, 0:M0] = main
                grey_ref[16 * b : 16 * b + 16, M0:W0] = tile
            grey = grey_ref[...]
            lap = (
                4.0 * grey
                - pltpu.roll(grey, 1, 0)
                - pltpu.roll(grey, 63, 0)
                - pltpu.roll(grey, 1, 1)
                - pltpu.roll(grey, W0 - 1, 1)
            )
            field = jnp.where(keep, lap * lap, 0.0)
            for axis, size in ((0, 64), (1, W0)):
                two = field + pltpu.roll(field, size - 1, axis)
                four = two + pltpu.roll(two, size - 2, axis)
                eight = four + pltpu.roll(four, size - 4, axis)
                field = pltpu.roll(eight, 4, axis) + pltpu.roll(field, size - 4, axis)
            gain = mains[s][0, 96:97, 192 + 32 * p : 193 + 32 * p]
            logit_ref[2 * s + p] = gain * field

    if second:
        logits = [ref.at[i] for ref in (earlier_ref, logit_ref) for i in range(4)]
        peak = logits[0][...]
        for ref in logits[1:]:
            peak = jnp.maximum(peak, ref[...])
        total = 0.0
        for ref in logits:
            total = total + jnp.exp(ref[...] - peak)
        lse_ref[...] = pltpu.roll(peak + jnp.log(total), 58, 0)[0:56]


def split2(value):
    high = value.astype(BF)
    low = (value - high.astype(F32)).astype(BF)
    return high, low


def stacked(value):
    return jnp.concatenate(split2(value), axis=0)


def dot(a, b):
    return jnp.dot(a, b, preferred_element_type=F32)


def iota2(shape):
    return lax.broadcasted_iota(jnp.int32, shape, 0), lax.broadcasted_iota(jnp.int32, shape, 1)


def down_rows(count, inputs, copies, first, limit):
    q, e = iota2((count, inputs * copies))
    if copies == 2:
        e = jnp.where(e >= inputs, e - inputs, e)
    gap = jnp.abs(e - 2 * q)
    taps = jnp.where(gap == 0, 0.375, jnp.where(gap == 1, 0.25, jnp.where(gap == 2, 0.0625, 0.0)))
    inside = (q + first >= 0) & (q + first < limit)
    return jnp.where(inside, taps, 0.0).astype(BF)


def up_rows(count, inputs, offset, first, limit):
    r, q = iota2((count, 2 * inputs))
    q = jnp.where(q >= inputs, q - inputs, q)
    gap = jnp.abs(2 * q - (r + offset))
    even = (r & 1) == 0
    taps = jnp.where(
        even,
        jnp.where(gap == 0, 0.75, jnp.where(gap == 2, 0.125, 0.0)),
        jnp.where(gap == 1, 0.5, 0.0),
    )
    inside = (r + first >= 0) & (r + first < limit)
    return jnp.where(inside, taps, 0.0).astype(BF)


def row_matrices(strip):
    v2 = down_rows(16, 32, 2, strip * 8 - 4, 256)
    p2 = up_rows(32, 16, 0, strip * 16 - 8, 512)
    p1 = up_rows(32, 32, 16, 0, 32)
    return v2, p2, p1


def level_masks(rows1, rows2, k):
    col1 = column_of((rows1, W1), M1, W1) + k * M1
    col2 = column_of((rows2, W2), M2, W2) + k * M2
    return (col1 >= 0) & (col1 < 1024), (col2 >= 0) & (col2 < 512)


def put(ref, n, a, count, value):
    high, low = split2(value)
    ref[a * count : (a + 1) * count] = high
    ref[(n + a) * count : (n + a + 1) * count] = low


def resampled(source_ref, taps_ref):
    both = dot(source_ref[...], taps_ref[...])
    half = both.shape[0] // 2
    return both[:half] + both[half:]


def pyramid_kernel(
    place_ref, main_a_ref, main_b_ref, near_ref, far_ref, d1_ref, d2_ref, u2_ref, u1_ref,
    detail0_ref, detail1_ref, l2_ref, x_ref, s1_ref, l1_ref, s2_ref, s3_ref, s4_ref,
):
    strip = place_ref[0]
    v1 = down_rows(32, 64, 1, strip * 16 - 8, 512)
    v2, p2, p1 = row_matrices(strip)
    inside1, inside2 = level_masks(192, 96, place_ref[1])
    mains = (main_a_ref, main_b_ref)
    strips = Strips(place_ref, mains, near_ref, far_ref)
    for i in range(2):
        for a in range(6):
            for b in range(4):
                x_ref[16 * b : 16 * b + 16, 0:M0] = strips.samples(i, b, a).astype(BF)
                x_ref[16 * b : 16 * b + 16, M0:W0] = strips.halo(i, b, a).astype(BF)
            put(s1_ref, 6, a, 32, dot(v1, x_ref[...]))
        l1_ref[...] = jnp.where(inside1, resampled(s1_ref, d1_ref), 0.0)
        for a in range(6):
            both = stacked(l1_ref[a * 32 : a * 32 + 32])
            put(s2_ref, 6, a, 16, dot(v2, both))
            put(s4_ref, 6, a, 32, dot(p1, both))
        l2 = jnp.where(inside2, resampled(s2_ref, d2_ref), 0.0)
        l2_ref[i * 96 : i * 96 + 96] = l2
        for a in range(6):
            put(s3_ref, 6, a, 32, dot(p2, stacked(l2[a * 16 : a * 16 + 16])))
        detail1_ref[i * 192 : i * 192 + 192] = l1_ref[...] - resampled(s3_ref, u2_ref)
        part = resampled(s4_ref, u1_ref)
        for a in range(6):
            for h in range(2):
                at = a * 32 + 16 * h
                detail0_ref[i * 192 + at : i * 192 + at + 16] = (
                    mains[i][h, 16 * a : 16 * a + 16, :] - part[at : at + 16]
                )


def mix_kernel(
    place_ref, logit_a_ref, logit_b_ref, lse_ref,
    fine_a_ref, mid_a_ref, low_a_ref, fine_b_ref, mid_b_ref, low_b_ref,
    d1_ref, d2_ref, u2_ref, u1_ref,
    left_ref, right_ref, w0_ref, s1_ref, w1_ref, s2_ref, s3_ref, s4_ref,
):
    strip, k = place_ref[0], place_ref[1]
    v1 = down_rows(32, 64, 2, strip * 16 - 8, 512)
    v2, p2, p1 = row_matrices(strip)
    col = column_of((16, W0), M0, W0)
    inside_col = (col >= -10) & (col <= 522) & (col + k * M0 >= 0) & (col + k * M0 < 2048)
    row = lax.broadcasted_iota(jnp.int32, (16, W0), 0)
    lse = pltpu.roll(jnp.concatenate([lse_ref[...], jnp.zeros((8, W0), F32)], axis=0), 6, 0)
    keeps = []
    for b in range(4):
        r = row + (16 * b - 16)
        g = r + strip * 32
        keeps.append(inside_col & (r >= -10) & (r <= 42) & (g >= 0) & (g < 1024))
    for i in range(8):
        logit_ref = (logit_a_ref, logit_b_ref)[i // 4]
        for b in range(4):
            rows = slice(16 * b, 16 * b + 16)
            w0_ref[i, rows] = jnp.where(keeps[b], jnp.exp(logit_ref[i % 4, rows] - lse[rows]), 0.0)
        put(s1_ref, 8, i, 32, dot(v1, stacked(w0_ref[i])))
    inside1, inside2 = level_masks(32, 16, k)
    w1_ref[...] = resampled(s1_ref, d1_ref)
    for i in range(8):
        w1 = jnp.where(inside1, w1_ref[i * 32 : i * 32 + 32], 0.0)
        w1_ref[i * 32 : i * 32 + 32] = w1
        put(s2_ref, 8, i, 16, dot(v2, stacked(w1)))
    w2 = resampled(s2_ref, d2_ref)

    def piece(pair, i, c, rows):
        ref = pair[i // 4]
        at = ((i % 4) * 3 + c) * rows
        return ref[at : at + rows]

    for c in range(3):
        blend2 = 0.0
        for i in range(8):
            blend2 = blend2 + w2[i * 16 : i * 16 + 16] * piece((low_a_ref, low_b_ref), i, c, 16)
        put(s3_ref, 3, c, 32, dot(p2, stacked(blend2)))
    rise = resampled(s3_ref, u2_ref)
    for c in range(3):
        total = jnp.where(inside1, rise[c * 32 : c * 32 + 32], 0.0)
        for i in range(8):
            total = total + w1_ref[i * 32 : i * 32 + 32] * piece((mid_a_ref, mid_b_ref), i, c, 32)
        put(s4_ref, 3, c, 32, dot(p1, stacked(total)))
    rise = resampled(s4_ref, u1_ref)
    for c in range(3):
        total = rise[c * 32 : c * 32 + 32]
        for i in range(8):
            total = total + w0_ref[i, 16:48, 0:M0] * piece((fine_a_ref, fine_b_ref), i, c, 32)
        total = total * (1.0 / 255.0)
        left_ref[c] = total[:, :256]
        right_ref[c] = total[:, 256:]


def vmem(count):
    return [pl.BlockSpec(memory_space=pltpu.VMEM)] * count


def smem():
    return [pl.BlockSpec(memory_space=pltpu.SMEM)]


def half(group, index):
    return jnp.stack([lax.dynamic_index_in_dim(main, index, axis=0, keepdims=False) for main in group])


def near_rows(group, core):
    return lax.ppermute(half(group, 1 - core), "c", [(0, 1), (1, 0)])


def far_rows(group, core):
    count = lax.axis_size(ROWS)
    swaps = [(i, i + 1) for i in range(1, count - 1, 2)]
    swaps += [(b, a) for a, b in swaps]
    return lax.ppermute(half(group, core), ROWS, swaps)


def partner(value, flip):
    return lax.ppermute(value, "zh", [(i, i ^ flip) for i in range(4)])


def crossed(value, flips):
    pairs = [(4 * c + i, 4 * c + (i ^ flip)) for c, flip in enumerate(flips) for i in range(4)]
    return lax.ppermute(value, ("c", "zh"), pairs)


def join_lse(a, b):
    return jnp.maximum(a, b) + jnp.log(1.0 + jnp.exp(-jnp.abs(a - b)))


def on_device(samples, gain):
    samples, strip, column, core = lax.optimization_barrier(
        (samples, lax.axis_index(ROWS), lax.axis_index("x"), lax.axis_index("c"))
    )
    packed = pl.pallas_call(
        pack_kernel,
        out_shape=(jax.ShapeDtypeStruct((2, 104, 512), F32),) * 4,
        in_specs=[pl.BlockSpec(memory_space=pltpu.HBM)] * 2,
        out_specs=(pl.BlockSpec(memory_space=pltpu.HBM),) * 4,
        scratch_shapes=[
            pltpu.VMEM((6, 32, 2048), jnp.int32),
            pltpu.SMEM((2,), F32),
            pltpu.VMEM((4, 2, 104, 512), F32),
            pltpu.SemaphoreType.DMA((6,)),
            pltpu.SemaphoreType.DMA,
            pltpu.SemaphoreType.DMA((4,)),
        ],
        compiler_params=pltpu.CompilerParams(vmem_limit_bytes=60 * 1024 * 1024),
        name="pack",
    )(samples, gain)
    mains = [packed[0]] + [
        lax.ppermute(packed[m], "x", [(i, i ^ FLIPS[m]) for i in range(4)]) for m in (1, 2, 3)
    ]
    place = jnp.stack([strip, column, core]).astype(jnp.int32)
    far = [far_rows(pair, core) for pair in (mains[:2], mains[2:])]
    logit_shape = jax.ShapeDtypeStruct((4, 64, W0), F32)

    def energy(step, group, *earlier):
        return pl.pallas_call(
            functools.partial(energy_kernel, step == 1),
            out_shape=(logit_shape,) + (jax.ShapeDtypeStruct((56, W0), F32),) * step,
            in_specs=smem() + vmem(4 + step),
            out_specs=tuple(vmem(1 + step)),
            scratch_shapes=[pltpu.VMEM((64, W0), F32)],
            compiler_params=PARAMS,
            cost_estimate=pl.CostEstimate(flops=2_000_000_000, bytes_accessed=6_000_000, transcendentals=0),
            name="energy",
        )(place, *group, *earlier)

    groups = [(*mains[:2], near_rows(mains[:2], core), far[0])]
    logits = energy(0, groups[0])
    late, _ = lax.optimization_barrier((mains[2:], logits))
    groups.append((*mains[2:], near_rows(late, core), far[1]))
    *more, lse = energy(1, groups[1], *logits)
    logits = [*logits, *more]

    taps = [
        jnp.asarray(t, BF)
        for t in (
            column_taps("down", M0, W0, M1, W1),
            column_taps("down", M1, W1, M2, W2),
            column_taps("up", M2, W2, M1, W1),
            column_taps("up", M1, W1, M0, W0)[:, :M0],
        )
    ]
    details = []
    for step, flips in enumerate(((1, 3), (3, 1))):
        other = crossed(lse, flips)
        detail = pl.pallas_call(
            pyramid_kernel,
            out_shape=(
                jax.ShapeDtypeStruct((384, M0), F32),
                jax.ShapeDtypeStruct((384, W1), F32),
                jax.ShapeDtypeStruct((192, W2), F32),
            ),
            in_specs=smem() + vmem(8),
            out_specs=tuple(vmem(3)),
            scratch_shapes=[
                pltpu.VMEM((64, W0), BF),
                pltpu.VMEM((384, W0), BF),
                pltpu.VMEM((192, W1), F32),
                pltpu.VMEM((192, W1), BF),
                pltpu.VMEM((384, W2), BF),
                pltpu.VMEM((384, W1), BF),
            ],
            compiler_params=PARAMS,
            cost_estimate=pl.CostEstimate(flops=2_000_000_000, bytes_accessed=6_000_000, transcendentals=0),
            name="pyramid",
        )(place, *groups[step], *taps)
        other, *detail = lax.optimization_barrier((other, *detail))
        details += detail
        lse = join_lse(lse, other)

    left, right = pl.pallas_call(
        mix_kernel,
        out_shape=(jax.ShapeDtypeStruct((3, 32, 256), F32),) * 2,
        in_specs=smem() + vmem(13),
        out_specs=tuple(vmem(2)),
        scratch_shapes=[
            pltpu.VMEM((8, 64, W0), F32),
            pltpu.VMEM((512, W0), BF),
            pltpu.VMEM((256, W1), F32),
            pltpu.VMEM((256, W1), BF),
            pltpu.VMEM((192, W2), BF),
            pltpu.VMEM((192, W1), BF),
        ],
        compiler_params=PARAMS,
        name="mix",
    )(place, *logits, lse, *details, *taps)

    for a, b in ((1, 3), (3, 1)):
        left_in, right_in = partner(left, a), partner(right, b)
        left, right = left + left_in, right + right_in
    whole = jnp.concatenate([left, right], axis=-1)
    joined = lax.all_to_all(jnp.broadcast_to(whole, (4, 3, 32, 512)), "x", 0, 0)
    return joined.transpose(1, 2, 0, 3).reshape(3, 32, 2048)


def solution(mesh):
    fine = Mesh(mesh.devices.reshape(4, 4, 2, 4, 4), ROWS + GZ)
    return jax.shard_map(
        on_device,
        mesh=fine,
        in_specs=(P(GZ, None, ROWS, None), P(GZ)),
        out_specs=P(None, ROWS, None),
        check_vma=False,
    )
```

```python
import functools

import jax
import jax.numpy as jnp
import numpy as np
from jax import lax
from jax.experimental import pallas as pl
from jax.experimental.pallas import tpu as pltpu
from jax.sharding import Mesh
from jax.sharding import PartitionSpec as P

ROWS = ("zl", "y", "c")
GZ = ("zh", "x")
BF = jnp.bfloat16
F32 = jnp.float32
GREY = (0.299 / 255.0, 0.587 / 255.0, 0.114 / 255.0)
W0, W1, W2 = 640, 384, 256
M0, M1, M2 = 512, 256, 128
FLIPS = (0, 2, 1, 3)
PARAMS = pltpu.CompilerParams(vmem_limit_bytes=20 * 1024 * 1024)


def lane_of(col, main, wide):
    if 0 <= col < main + 64:
        return col
    if -64 <= col < 0:
        return wide + col
    return None


def column_taps(kind, main_in, wide_in, main_out, wide_out):
    taps = np.zeros((wide_in, wide_out), np.float32)
    for lane in range(wide_out):
        col = lane if lane < main_out + 64 else lane - wide_out
        if kind == "down":
            picks = [(2 * col + d, t / 16.0) for d, t in zip(range(-2, 3), (1, 4, 6, 4, 1))]
        elif col % 2 == 0:
            picks = [(col // 2 - 1, 0.125), (col // 2, 0.75), (col // 2 + 1, 0.125)]
        else:
            picks = [(col // 2, 0.5), (col // 2 + 1, 0.5)]
        for source, tap in picks:
            at = lane_of(source, main_in, wide_in)
            if at is not None:
                taps[at, lane] += tap
    return taps


def pack_kernel(samples_ref, gain_hbm_ref, *refs):
    packed_refs, (held_ref, gain_ref, out_ref, sems, gain_sem, out_sems) = refs[:4], refs[4:]
    copies = []
    for a in range(6):
        p, c = divmod(a, 3)
        copies.append(pltpu.make_async_copy(samples_ref.at[p, c], held_ref.at[a], sems.at[a]))
        copies[a].start()
    gain_copy = pltpu.make_async_copy(gain_hbm_ref, gain_ref, gain_sem)
    gain_copy.start()
    mine = lax.axis_index("x")
    lane = lax.broadcasted_iota(jnp.int32, (16, 128), 1)
    written = []
    for m, flip in enumerate(FLIPS):
        j = mine ^ flip
        base = pl.multiple_of(512 * j, 512)
        before = pl.multiple_of(jnp.maximum(base - 128, 0), 128)
        after = pl.multiple_of(jnp.minimum(base + 512, 1920), 128)
        has_before, has_after = j > 0, j < 3
        for a in range(6):
            if m == 0:
                copies[a].wait()
            for h in range(2):
                out_ref[m, h, 16 * a : 16 * a + 16, :] = held_ref[a, 16 * h : 16 * h + 16, pl.ds(base, 512)].astype(F32)
        if m == 0:
            gain_copy.wait()
        for h in range(2):
            rows = slice(16 * h, 16 * h + 16)
            tiles = [
                jnp.zeros((16, 128), F32),
                jnp.where(lane < 64, 0.0, jnp.where(lane < 96, gain_ref[0], gain_ref[1])),
            ]
            for a in range(6):
                at, t = 32 * (a % 4), a // 4
                piece = pltpu.roll(held_ref[a, rows, pl.ds(before, 128)].astype(F32), (at - 112) % 128, 1)
                piece = jnp.where(has_before, piece, 0.0)
                tiles[t] = jnp.where((lane >= at) & (lane < at + 16), piece, tiles[t])
                piece = pltpu.roll(held_ref[a, rows, pl.ds(after, 128)].astype(F32), (at + 16) % 128, 1)
                piece = jnp.where(has_after, piece, 0.0)
                tiles[t] = jnp.where((lane >= at + 16) & (lane < at + 32), piece, tiles[t])
            out_ref[m, h, 96:104, 0:128] = tiles[0][0:8]
            out_ref[m, h, 96:104, 128:256] = tiles[1][0:8]
            out_ref[m, h, 96:104, 256:384] = tiles[0][8:16]
            out_ref[m, h, 96:104, 384:512] = tiles[1][8:16]
        written.append(pltpu.make_async_copy(out_ref.at[m], packed_refs[m], out_sems.at[m]))
        written[m].start()
    for copy in written:
        copy.wait()


class Strips:
    def __init__(self, place_ref, mains, near_ref, far_ref):
        self.even = place_ref[2] == 0
        self.mains, self.near, self.far = mains, near_ref, far_ref

    def get(self, s, b, rows, cols):
        if b in (1, 2):
            return self.mains[s][b - 1, rows, cols]
        near, far = self.near[s, rows, cols], self.far[s, rows, cols]
        return jnp.where(self.even, far, near) if b == 0 else jnp.where(self.even, near, far)

    def samples(self, s, b, a):
        return self.get(s, b, slice(16 * a, 16 * a + 16), slice(0, M0))

    def halo(self, s, b, a):
        return halo_tile(lambda cols: self.get(s, b, slice(96, 104), cols), a)


def halo_tile(read, a):
    base, at = 128 * (a // 4), 32 * (a % 4)
    tile = jnp.concatenate([read(slice(base, base + 128)), read(slice(256 + base, 384 + base))], axis=0)
    lane = lax.broadcasted_iota(jnp.int32, (16, 128), 1)
    return jnp.where((lane < 16) | (lane >= 112), pltpu.roll(tile, (112 - at) % 128, 1), 0.0)


def column_of(shape, main, wide):
    lane = lax.broadcasted_iota(jnp.int32, shape, len(shape) - 1)
    return jnp.where(lane < main + 64, lane, lane - wide)


def energy_kernel(second, place_ref, main_a_ref, main_b_ref, near_ref, far_ref, *refs):
    earlier_ref, logit_ref, lse_ref, grey_ref = refs if second else (None, refs[0], None, refs[1])
    row = lax.broadcasted_iota(jnp.int32, (64, W0), 0) + (place_ref[0] * 32 - 16)
    col = column_of((64, W0), M0, W0) + place_ref[1] * M0
    keep = (row >= 0) & (row < 1024) & (col >= 0) & (col < 2048)

    mains = (main_a_ref, main_b_ref)
    strips = Strips(place_ref, mains, near_ref, far_ref)
    for s in range(2):
        for p in range(2):
            for b in range(4):
                main = 0.0
                tile = 0.0
                for c in range(3):
                    a = 3 * p + c
                    main = main + strips.samples(s, b, a) * GREY[c]
                    tile = tile + strips.halo(s, b, a) * GREY[c]
                grey_ref[16 * b : 16 * b + 16, 0:M0] = main
                grey_ref[16 * b : 16 * b + 16, M0:W0] = tile
            grey = grey_ref[...]
            lap = (
                4.0 * grey
                - pltpu.roll(grey, 1, 0)
                - pltpu.roll(grey, 63, 0)
                - pltpu.roll(grey, 1, 1)
                - pltpu.roll(grey, W0 - 1, 1)
            )
            field = jnp.where(keep, lap * lap, 0.0)
            for axis, size in ((0, 64), (1, W0)):
                two = field + pltpu.roll(field, size - 1, axis)
                four = two + pltpu.roll(two, size - 2, axis)
                eight = four + pltpu.roll(four, size - 4, axis)
                field = pltpu.roll(eight, 4, axis) + pltpu.roll(field, size - 4, axis)
            gain = mains[s][0, 96:97, 192 + 32 * p : 193 + 32 * p]
            logit_ref[2 * s + p] = gain * field

    if second:
        logits = [ref.at[i] for ref in (earlier_ref, logit_ref) for i in range(4)]
        peak = logits[0][...]
        for ref in logits[1:]:
            peak = jnp.maximum(peak, ref[...])
        total = 0.0
        for ref in logits:
            total = total + jnp.exp(ref[...] - peak)
        lse_ref[...] = pltpu.roll(peak + jnp.log(total), 58, 0)[0:56]


def split2(value):
    high = value.astype(BF)
    low = (value - high.astype(F32)).astype(BF)
    return high, low


def stacked(value):
    return jnp.concatenate(split2(value), axis=0)


def dot(a, b):
    return jnp.dot(a, b, preferred_element_type=F32)


def iota2(shape):
    return lax.broadcasted_iota(jnp.int32, shape, 0), lax.broadcasted_iota(jnp.int32, shape, 1)


def down_rows(count, inputs, copies, first, limit):
    q, e = iota2((count, inputs * copies))
    if copies == 2:
        e = jnp.where(e >= inputs, e - inputs, e)
    gap = jnp.abs(e - 2 * q)
    taps = jnp.where(gap == 0, 0.375, jnp.where(gap == 1, 0.25, jnp.where(gap == 2, 0.0625, 0.0)))
    inside = (q + first >= 0) & (q + first < limit)
    return jnp.where(inside, taps, 0.0).astype(BF)


def up_rows(count, inputs, offset, first, limit):
    r, q = iota2((count, 2 * inputs))
    q = jnp.where(q >= inputs, q - inputs, q)
    gap = jnp.abs(2 * q - (r + offset))
    even = (r & 1) == 0
    taps = jnp.where(
        even,
        jnp.where(gap == 0, 0.75, jnp.where(gap == 2, 0.125, 0.0)),
        jnp.where(gap == 1, 0.5, 0.0),
    )
    inside = (r + first >= 0) & (r + first < limit)
    return jnp.where(inside, taps, 0.0).astype(BF)


def row_matrices(strip):
    v2 = down_rows(16, 32, 2, strip * 8 - 4, 256)
    p2 = up_rows(32, 16, 0, strip * 16 - 8, 512)
    p1 = up_rows(32, 32, 16, 0, 32)
    return v2, p2, p1


def level_masks(rows1, rows2, k):
    col1 = column_of((rows1, W1), M1, W1) + k * M1
    col2 = column_of((rows2, W2), M2, W2) + k * M2
    return (col1 >= 0) & (col1 < 1024), (col2 >= 0) & (col2 < 512)


def put(ref, n, a, count, value):
    high, low = split2(value)
    ref[a * count : (a + 1) * count] = high
    ref[(n + a) * count : (n + a + 1) * count] = low


def resampled(source_ref, taps_ref):
    both = dot(source_ref[...], taps_ref[...])
    half = both.shape[0] // 2
    return both[:half] + both[half:]


def pyramid_kernel(
    place_ref, main_a_ref, main_b_ref, near_ref, far_ref, d1_ref, d2_ref, u2_ref, u1_ref,
    detail0_ref, detail1_ref, l2_ref, x_ref, s1_ref, l1_ref, s2_ref, s3_ref, s4_ref,
):
    strip = place_ref[0]
    v1 = down_rows(32, 64, 1, strip * 16 - 8, 512)
    v2, p2, p1 = row_matrices(strip)
    inside1, inside2 = level_masks(192, 96, place_ref[1])
    mains = (main_a_ref, main_b_ref)
    strips = Strips(place_ref, mains, near_ref, far_ref)
    for i in range(2):
        for a in range(6):
            for b in range(4):
                x_ref[16 * b : 16 * b + 16, 0:M0] = strips.samples(i, b, a).astype(BF)
                x_ref[16 * b : 16 * b + 16, M0:W0] = strips.halo(i, b, a).astype(BF)
            put(s1_ref, 6, a, 32, dot(v1, x_ref[...]))
        l1_ref[...] = jnp.where(inside1, resampled(s1_ref, d1_ref), 0.0)
        for a in range(6):
            both = stacked(l1_ref[a * 32 : a * 32 + 32])
            put(s2_ref, 6, a, 16, dot(v2, both))
            put(s4_ref, 6, a, 32, dot(p1, both))
        l2 = jnp.where(inside2, resampled(s2_ref, d2_ref), 0.0)
        l2_ref[i * 96 : i * 96 + 96] = l2
        for a in range(6):
            put(s3_ref, 6, a, 32, dot(p2, stacked(l2[a * 16 : a * 16 + 16])))
        detail1_ref[i * 192 : i * 192 + 192] = l1_ref[...] - resampled(s3_ref, u2_ref)
        part = resampled(s4_ref, u1_ref)
        for a in range(6):
            for h in range(2):
                at = a * 32 + 16 * h
                detail0_ref[i * 192 + at : i * 192 + at + 16] = (
                    mains[i][h, 16 * a : 16 * a + 16, :] - part[at : at + 16]
                )


def mix_kernel(
    place_ref, logit_a_ref, logit_b_ref, lse_ref,
    fine_a_ref, mid_a_ref, low_a_ref, fine_b_ref, mid_b_ref, low_b_ref,
    d1_ref, d2_ref, u2_ref, u1_ref,
    left_ref, right_ref, w0_ref, s1_ref, w1_ref, s2_ref, s3_ref, s4_ref,
):
    strip, k = place_ref[0], place_ref[1]
    v1 = down_rows(32, 64, 2, strip * 16 - 8, 512)
    v2, p2, p1 = row_matrices(strip)
    col = column_of((16, W0), M0, W0)
    inside_col = (col >= -10) & (col <= 522) & (col + k * M0 >= 0) & (col + k * M0 < 2048)
    row = lax.broadcasted_iota(jnp.int32, (16, W0), 0)
    lse = pltpu.roll(jnp.concatenate([lse_ref[...], jnp.zeros((8, W0), F32)], axis=0), 6, 0)
    keeps = []
    for b in range(4):
        r = row + (16 * b - 16)
        g = r + strip * 32
        keeps.append(inside_col & (r >= -10) & (r <= 42) & (g >= 0) & (g < 1024))
    for i in range(8):
        logit_ref = (logit_a_ref, logit_b_ref)[i // 4]
        for b in range(4):
            rows = slice(16 * b, 16 * b + 16)
            w0_ref[i, rows] = jnp.where(keeps[b], jnp.exp(logit_ref[i % 4, rows] - lse[rows]), 0.0)
        put(s1_ref, 8, i, 32, dot(v1, stacked(w0_ref[i])))
    inside1, inside2 = level_masks(32, 16, k)
    w1_ref[...] = resampled(s1_ref, d1_ref)
    for i in range(8):
        w1 = jnp.where(inside1, w1_ref[i * 32 : i * 32 + 32], 0.0)
        w1_ref[i * 32 : i * 32 + 32] = w1
        put(s2_ref, 8, i, 16, dot(v2, stacked(w1)))
    w2 = resampled(s2_ref, d2_ref)

    def piece(pair, i, c, rows):
        ref = pair[i // 4]
        at = ((i % 4) * 3 + c) * rows
        return ref[at : at + rows]

    for c in range(3):
        blend2 = 0.0
        for i in range(8):
            blend2 = blend2 + w2[i * 16 : i * 16 + 16] * piece((low_a_ref, low_b_ref), i, c, 16)
        put(s3_ref, 3, c, 32, dot(p2, stacked(blend2)))
    rise = resampled(s3_ref, u2_ref)
    for c in range(3):
        total = jnp.where(inside1, rise[c * 32 : c * 32 + 32], 0.0)
        for i in range(8):
            total = total + w1_ref[i * 32 : i * 32 + 32] * piece((mid_a_ref, mid_b_ref), i, c, 32)
        put(s4_ref, 3, c, 32, dot(p1, stacked(total)))
    rise = resampled(s4_ref, u1_ref)
    for c in range(3):
        total = rise[c * 32 : c * 32 + 32]
        for i in range(8):
            total = total + w0_ref[i, 16:48, 0:M0] * piece((fine_a_ref, fine_b_ref), i, c, 32)
        total = total * (1.0 / 255.0)
        left_ref[c] = total[:, :256]
        right_ref[c] = total[:, 256:]


def vmem(count):
    return [pl.BlockSpec(memory_space=pltpu.VMEM)] * count


def smem():
    return [pl.BlockSpec(memory_space=pltpu.SMEM)]


def half(group, index):
    return jnp.stack([lax.dynamic_index_in_dim(main, index, axis=0, keepdims=False) for main in group])


def near_rows(group, core):
    return lax.ppermute(half(group, 1 - core), "c", [(0, 1), (1, 0)])


def far_rows(group, core):
    count = lax.axis_size(ROWS)
    swaps = [(i, i + 1) for i in range(1, count - 1, 2)]
    swaps += [(b, a) for a, b in swaps]
    return lax.ppermute(half(group, core), ROWS, swaps)


def crossed(value, flips):
    pairs = [(4 * c + i, 4 * c + (i ^ flip)) for c, flip in enumerate(flips) for i in range(4)]
    return lax.ppermute(value, ("c", "zh"), pairs)


def join_lse(a, b):
    return jnp.maximum(a, b) + jnp.log(1.0 + jnp.exp(-jnp.abs(a - b)))


def on_device(samples, gain):
    samples, strip, column, core = lax.optimization_barrier(
        (samples, lax.axis_index(ROWS), lax.axis_index("x"), lax.axis_index("c"))
    )
    packed = pl.pallas_call(
        pack_kernel,
        out_shape=(jax.ShapeDtypeStruct((2, 104, 512), F32),) * 4,
        in_specs=[pl.BlockSpec(memory_space=pltpu.HBM)] * 2,
        out_specs=(pl.BlockSpec(memory_space=pltpu.HBM),) * 4,
        scratch_shapes=[
            pltpu.VMEM((6, 32, 2048), jnp.int32),
            pltpu.SMEM((2,), F32),
            pltpu.VMEM((4, 2, 104, 512), F32),
            pltpu.SemaphoreType.DMA((6,)),
            pltpu.SemaphoreType.DMA,
            pltpu.SemaphoreType.DMA((4,)),
        ],
        compiler_params=pltpu.CompilerParams(vmem_limit_bytes=60 * 1024 * 1024),
        name="pack",
    )(samples, gain)
    mains = [packed[0]] + [
        lax.ppermute(packed[m], "x", [(i, i ^ FLIPS[m]) for i in range(4)]) for m in (1, 2, 3)
    ]
    place = jnp.stack([strip, column, core]).astype(jnp.int32)
    far = [far_rows(pair, core) for pair in (mains[:2], mains[2:])]
    logit_shape = jax.ShapeDtypeStruct((4, 64, W0), F32)

    def energy(step, group, *earlier):
        return pl.pallas_call(
            functools.partial(energy_kernel, step == 1),
            out_shape=(logit_shape,) + (jax.ShapeDtypeStruct((56, W0), F32),) * step,
            in_specs=smem() + vmem(4 + step),
            out_specs=tuple(vmem(1 + step)),
            scratch_shapes=[pltpu.VMEM((64, W0), F32)],
            compiler_params=PARAMS,
            cost_estimate=pl.CostEstimate(flops=2_000_000_000, bytes_accessed=6_000_000, transcendentals=0),
            name="energy",
        )(place, *group, *earlier)

    groups = [(*mains[:2], near_rows(mains[:2], core), far[0])]
    logits = energy(0, groups[0])
    late, _ = lax.optimization_barrier((mains[2:], logits))
    groups.append((*mains[2:], near_rows(late, core), far[1]))
    *more, lse = energy(1, groups[1], *logits)
    logits = [*logits, *more]

    taps = [
        jnp.asarray(t, BF)
        for t in (
            column_taps("down", M0, W0, M1, W1),
            column_taps("down", M1, W1, M2, W2),
            column_taps("up", M2, W2, M1, W1),
            column_taps("up", M1, W1, M0, W0)[:, :M0],
        )
    ]
    details = []
    for step, flips in enumerate(((1, 3), (3, 1))):
        other = crossed(lse, flips)
        detail = pl.pallas_call(
            pyramid_kernel,
            out_shape=(
                jax.ShapeDtypeStruct((384, M0), F32),
                jax.ShapeDtypeStruct((384, W1), F32),
                jax.ShapeDtypeStruct((192, W2), F32),
            ),
            in_specs=smem() + vmem(8),
            out_specs=tuple(vmem(3)),
            scratch_shapes=[
                pltpu.VMEM((64, W0), BF),
                pltpu.VMEM((384, W0), BF),
                pltpu.VMEM((192, W1), F32),
                pltpu.VMEM((192, W1), BF),
                pltpu.VMEM((384, W2), BF),
                pltpu.VMEM((384, W1), BF),
            ],
            compiler_params=PARAMS,
            cost_estimate=pl.CostEstimate(flops=2_000_000_000, bytes_accessed=6_000_000, transcendentals=0),
            name="pyramid",
        )(place, *groups[step], *taps)
        other, *detail = lax.optimization_barrier((other, *detail))
        details += detail
        lse = join_lse(lse, other)

    left, right = pl.pallas_call(
        mix_kernel,
        out_shape=(jax.ShapeDtypeStruct((3, 32, 256), F32),) * 2,
        in_specs=smem() + vmem(13),
        out_specs=tuple(vmem(2)),
        scratch_shapes=[
            pltpu.VMEM((8, 64, W0), F32),
            pltpu.VMEM((512, W0), BF),
            pltpu.VMEM((256, W1), F32),
            pltpu.VMEM((256, W1), BF),
            pltpu.VMEM((192, W2), BF),
            pltpu.VMEM((192, W1), BF),
        ],
        compiler_params=PARAMS,
        name="mix",
    )(place, *logits, lse, *details, *taps)

    for a, b in ((1, 3), (3, 1)):
        left_in, right_in = crossed(left, (a, b)), crossed(right, (b, a))
        left, right = left + left_in, right + right_in
    whole = jnp.concatenate([left, right], axis=-1)
    joined = lax.all_to_all(jnp.broadcast_to(whole, (4, 3, 32, 512)), "x", 0, 0)
    return joined.transpose(1, 2, 0, 3).reshape(3, 32, 2048)


def solution(mesh):
    fine = Mesh(mesh.devices.reshape(4, 4, 2, 4, 4), ROWS + GZ)
    return jax.shard_map(
        on_device,
        mesh=fine,
        in_specs=(P(GZ, None, ROWS, None), P(GZ)),
        out_specs=P(None, ROWS, None),
        check_vma=False,
    )
```

```python
import functools

import jax
import jax.numpy as jnp
import numpy as np
from jax import lax
from jax.experimental import pallas as pl
from jax.experimental.pallas import tpu as pltpu
from jax.sharding import Mesh
from jax.sharding import PartitionSpec as P

ROWS = ("zl", "y", "c")
GZ = ("zh", "x")
BF = jnp.bfloat16
F32 = jnp.float32
GREY = (0.299 / 255.0, 0.587 / 255.0, 0.114 / 255.0)
W0, W1, W2 = 640, 384, 256
M0, M1, M2 = 512, 256, 128
FLIPS = (0, 2, 1, 3)
PARAMS = pltpu.CompilerParams(vmem_limit_bytes=20 * 1024 * 1024)


def lane_of(col, main, wide):
    if 0 <= col < main + 64:
        return col
    if -64 <= col < 0:
        return wide + col
    return None


def column_taps(kind, main_in, wide_in, main_out, wide_out):
    taps = np.zeros((wide_in, wide_out), np.float32)
    for lane in range(wide_out):
        col = lane if lane < main_out + 64 else lane - wide_out
        if kind == "down":
            picks = [(2 * col + d, t / 16.0) for d, t in zip(range(-2, 3), (1, 4, 6, 4, 1))]
        elif col % 2 == 0:
            picks = [(col // 2 - 1, 0.125), (col // 2, 0.75), (col // 2 + 1, 0.125)]
        else:
            picks = [(col // 2, 0.5), (col // 2 + 1, 0.5)]
        for source, tap in picks:
            at = lane_of(source, main_in, wide_in)
            if at is not None:
                taps[at, lane] += tap
    return taps


def pack_kernel(samples_ref, gain_hbm_ref, *refs):
    packed_refs, (held_ref, gain_ref, out_ref, sems, gain_sem, out_sems) = refs[:4], refs[4:]
    copies = []
    for a in range(6):
        p, c = divmod(a, 3)
        copies.append(pltpu.make_async_copy(samples_ref.at[p, c], held_ref.at[a], sems.at[a]))
        copies[a].start()
    gain_copy = pltpu.make_async_copy(gain_hbm_ref, gain_ref, gain_sem)
    gain_copy.start()
    mine = lax.axis_index("x")
    lane = lax.broadcasted_iota(jnp.int32, (16, 128), 1)
    written = []
    for m, flip in enumerate(FLIPS):
        j = mine ^ flip
        base = pl.multiple_of(512 * j, 512)
        before = pl.multiple_of(jnp.maximum(base - 128, 0), 128)
        after = pl.multiple_of(jnp.minimum(base + 512, 1920), 128)
        has_before, has_after = j > 0, j < 3
        for a in range(6):
            if m == 0:
                copies[a].wait()
            for h in range(2):
                out_ref[m, h, 16 * a : 16 * a + 16, :] = held_ref[a, 16 * h : 16 * h + 16, pl.ds(base, 512)].astype(F32)
        if m == 0:
            gain_copy.wait()
        for h in range(2):
            rows = slice(16 * h, 16 * h + 16)
            tiles = [
                jnp.zeros((16, 128), F32),
                jnp.where(lane < 64, 0.0, jnp.where(lane < 96, gain_ref[0], gain_ref[1])),
            ]
            for a in range(6):
                at, t = 32 * (a % 4), a // 4
                piece = pltpu.roll(held_ref[a, rows, pl.ds(before, 128)].astype(F32), (at - 112) % 128, 1)
                piece = jnp.where(has_before, piece, 0.0)
                tiles[t] = jnp.where((lane >= at) & (lane < at + 16), piece, tiles[t])
                piece = pltpu.roll(held_ref[a, rows, pl.ds(after, 128)].astype(F32), (at + 16) % 128, 1)
                piece = jnp.where(has_after, piece, 0.0)
                tiles[t] = jnp.where((lane >= at + 16) & (lane < at + 32), piece, tiles[t])
            out_ref[m, h, 96:104, 0:128] = tiles[0][0:8]
            out_ref[m, h, 96:104, 128:256] = tiles[1][0:8]
            out_ref[m, h, 96:104, 256:384] = tiles[0][8:16]
            out_ref[m, h, 96:104, 384:512] = tiles[1][8:16]
        written.append(pltpu.make_async_copy(out_ref.at[m], packed_refs[m], out_sems.at[m]))
        written[m].start()
    for copy in written:
        copy.wait()


class Strips:
    def __init__(self, place_ref, mains, near_ref, far_ref):
        self.even = place_ref[2] == 0
        self.mains, self.near, self.far = mains, near_ref, far_ref

    def get(self, s, b, rows, cols):
        if b in (1, 2):
            return self.mains[s][b - 1, rows, cols]
        near, far = self.near[s, rows, cols], self.far[s, rows, cols]
        return jnp.where(self.even, far, near) if b == 0 else jnp.where(self.even, near, far)

    def samples(self, s, b, a):
        return self.get(s, b, slice(16 * a, 16 * a + 16), slice(0, M0))

    def halo(self, s, b, a):
        return halo_tile(lambda cols: self.get(s, b, slice(96, 104), cols), a)


def halo_tile(read, a):
    base, at = 128 * (a // 4), 32 * (a % 4)
    tile = jnp.concatenate([read(slice(base, base + 128)), read(slice(256 + base, 384 + base))], axis=0)
    lane = lax.broadcasted_iota(jnp.int32, (16, 128), 1)
    return jnp.where((lane < 16) | (lane >= 112), pltpu.roll(tile, (112 - at) % 128, 1), 0.0)


def column_of(shape, main, wide):
    lane = lax.broadcasted_iota(jnp.int32, shape, len(shape) - 1)
    return jnp.where(lane < main + 64, lane, lane - wide)


def energy_kernel(second, place_ref, main_a_ref, main_b_ref, near_ref, far_ref, *refs):
    earlier_ref, logit_ref, lse_ref, grey_ref = refs if second else (None, refs[0], None, refs[1])
    row = lax.broadcasted_iota(jnp.int32, (64, W0), 0) + (place_ref[0] * 32 - 16)
    col = column_of((64, W0), M0, W0) + place_ref[1] * M0
    keep = (row >= 0) & (row < 1024) & (col >= 0) & (col < 2048)

    mains = (main_a_ref, main_b_ref)
    strips = Strips(place_ref, mains, near_ref, far_ref)
    for s in range(2):
        for p in range(2):
            for b in range(4):
                main = 0.0
                tile = 0.0
                for c in range(3):
                    a = 3 * p + c
                    main = main + strips.samples(s, b, a) * GREY[c]
                    tile = tile + strips.halo(s, b, a) * GREY[c]
                grey_ref[16 * b : 16 * b + 16, 0:M0] = main
                grey_ref[16 * b : 16 * b + 16, M0:W0] = tile
            grey = grey_ref[...]
            lap = (
                4.0 * grey
                - pltpu.roll(grey, 1, 0)
                - pltpu.roll(grey, 63, 0)
                - pltpu.roll(grey, 1, 1)
                - pltpu.roll(grey, W0 - 1, 1)
            )
            field = jnp.where(keep, lap * lap, 0.0)
            for axis, size in ((0, 64), (1, W0)):
                two = field + pltpu.roll(field, size - 1, axis)
                four = two + pltpu.roll(two, size - 2, axis)
                eight = four + pltpu.roll(four, size - 4, axis)
                field = pltpu.roll(eight, 4, axis) + pltpu.roll(field, size - 4, axis)
            gain = mains[s][0, 96:97, 192 + 32 * p : 193 + 32 * p]
            logit_ref[2 * s + p] = gain * field

    if second:
        logits = [ref.at[i] for ref in (earlier_ref, logit_ref) for i in range(4)]
        peak = logits[0][...]
        for ref in logits[1:]:
            peak = jnp.maximum(peak, ref[...])
        total = 0.0
        for ref in logits:
            total = total + jnp.exp(ref[...] - peak)
        lse = pltpu.roll(peak + jnp.log(total), 58, 0)[0:56]
        lane = lax.broadcasted_iota(jnp.int32, (8, 128), 1)
        shared = [jnp.zeros((8, 128), F32)] * 2
        for i in range(7):
            rows = slice(8 * i, 8 * i + 8)
            for j in range(4):
                lse_ref[4 * i + j] = lse[rows, 128 * j : 128 * j + 128]
            at = 32 * (i % 4)
            piece = pltpu.roll(lse[rows, M0:W0], (16 + at) % 128, 1)
            shared[i // 4] = jnp.where((lane >= at) & (lane < at + 32), piece, shared[i // 4])
        lse_ref[28] = shared[0]
        lse_ref[29] = shared[1]


def split2(value):
    high = value.astype(BF)
    low = (value - high.astype(F32)).astype(BF)
    return high, low


def stacked(value):
    return jnp.concatenate(split2(value), axis=0)


def dot(a, b):
    return jnp.dot(a, b, preferred_element_type=F32)


def iota2(shape):
    return lax.broadcasted_iota(jnp.int32, shape, 0), lax.broadcasted_iota(jnp.int32, shape, 1)


def down_rows(count, inputs, copies, first, limit):
    q, e = iota2((count, inputs * copies))
    if copies == 2:
        e = jnp.where(e >= inputs, e - inputs, e)
    gap = jnp.abs(e - 2 * q)
    taps = jnp.where(gap == 0, 0.375, jnp.where(gap == 1, 0.25, jnp.where(gap == 2, 0.0625, 0.0)))
    inside = (q + first >= 0) & (q + first < limit)
    return jnp.where(inside, taps, 0.0).astype(BF)


def up_rows(count, inputs, offset, first, limit):
    r, q = iota2((count, 2 * inputs))
    q = jnp.where(q >= inputs, q - inputs, q)
    gap = jnp.abs(2 * q - (r + offset))
    even = (r & 1) == 0
    taps = jnp.where(
        even,
        jnp.where(gap == 0, 0.75, jnp.where(gap == 2, 0.125, 0.0)),
        jnp.where(gap == 1, 0.5, 0.0),
    )
    inside = (r + first >= 0) & (r + first < limit)
    return jnp.where(inside, taps, 0.0).astype(BF)


def row_matrices(strip):
    v2 = down_rows(16, 32, 2, strip * 8 - 4, 256)
    p2 = up_rows(32, 16, 0, strip * 16 - 8, 512)
    p1 = up_rows(32, 32, 16, 0, 32)
    return v2, p2, p1


def level_masks(rows1, rows2, k):
    col1 = column_of((rows1, W1), M1, W1) + k * M1
    col2 = column_of((rows2, W2), M2, W2) + k * M2
    return (col1 >= 0) & (col1 < 1024), (col2 >= 0) & (col2 < 512)


def put(ref, n, a, count, value):
    high, low = split2(value)
    ref[a * count : (a + 1) * count] = high
    ref[(n + a) * count : (n + a + 1) * count] = low


def resampled(source_ref, taps_ref):
    both = dot(source_ref[...], taps_ref[...])
    half = both.shape[0] // 2
    return both[:half] + both[half:]


def pyramid_kernel(
    place_ref, main_a_ref, main_b_ref, near_ref, far_ref, d1_ref, d2_ref, u2_ref, u1_ref,
    detail0_ref, detail1_ref, l2_ref, x_ref, s1_ref, l1_ref, s2_ref, s3_ref, s4_ref,
):
    strip = place_ref[0]
    v1 = down_rows(32, 64, 1, strip * 16 - 8, 512)
    v2, p2, p1 = row_matrices(strip)
    inside1, inside2 = level_masks(192, 96, place_ref[1])
    mains = (main_a_ref, main_b_ref)
    strips = Strips(place_ref, mains, near_ref, far_ref)
    for i in range(2):
        for a in range(6):
            for b in range(4):
                x_ref[16 * b : 16 * b + 16, 0:M0] = strips.samples(i, b, a).astype(BF)
                x_ref[16 * b : 16 * b + 16, M0:W0] = strips.halo(i, b, a).astype(BF)
            put(s1_ref, 6, a, 32, dot(v1, x_ref[...]))
        l1_ref[...] = jnp.where(inside1, resampled(s1_ref, d1_ref), 0.0)
        for a in range(6):
            both = stacked(l1_ref[a * 32 : a * 32 + 32])
            put(s2_ref, 6, a, 16, dot(v2, both))
            put(s4_ref, 6, a, 32, dot(p1, both))
        l2 = jnp.where(inside2, resampled(s2_ref, d2_ref), 0.0)
        l2_ref[i * 96 : i * 96 + 96] = l2
        for a in range(6):
            put(s3_ref, 6, a, 32, dot(p2, stacked(l2[a * 16 : a * 16 + 16])))
        detail1_ref[i * 192 : i * 192 + 192] = l1_ref[...] - resampled(s3_ref, u2_ref)
        part = resampled(s4_ref, u1_ref)
        for a in range(6):
            for h in range(2):
                at = a * 32 + 16 * h
                detail0_ref[i * 192 + at : i * 192 + at + 16] = (
                    mains[i][h, 16 * a : 16 * a + 16, :] - part[at : at + 16]
                )


def mix_kernel(
    place_ref, logit_a_ref, logit_b_ref, lse_ref,
    fine_a_ref, mid_a_ref, low_a_ref, fine_b_ref, mid_b_ref, low_b_ref,
    d1_ref, d2_ref, u2_ref, u1_ref,
    left_ref, right_ref, tiles_ref, w0_ref, s1_ref, w1_ref, s2_ref, s3_ref, s4_ref,
):
    strip, k = place_ref[0], place_ref[1]
    v1 = down_rows(32, 64, 2, strip * 16 - 8, 512)
    v2, p2, p1 = row_matrices(strip)
    col = column_of((16, W0), M0, W0)
    inside_col = (col >= -10) & (col <= 522) & (col + k * M0 >= 0) & (col + k * M0 < 2048)
    row = lax.broadcasted_iota(jnp.int32, (16, W0), 0)
    for i in range(7):
        rows = slice(8 * i, 8 * i + 8)
        for j in range(4):
            tiles_ref[rows, 128 * j : 128 * j + 128] = lse_ref[4 * i + j]
        tiles_ref[rows, M0:W0] = pltpu.roll(lse_ref[28 + i // 4], (112 - 32 * (i % 4)) % 128, 1)
    tiles_ref[56:64] = jnp.zeros((8, W0), F32)
    lse = pltpu.roll(tiles_ref[...], 6, 0)
    keeps = []
    for b in range(4):
        r = row + (16 * b - 16)
        g = r + strip * 32
        keeps.append(inside_col & (r >= -10) & (r <= 42) & (g >= 0) & (g < 1024))
    for i in range(8):
        logit_ref = (logit_a_ref, logit_b_ref)[i // 4]
        for b in range(4):
            rows = slice(16 * b, 16 * b + 16)
            w0_ref[i, rows] = jnp.where(keeps[b], jnp.exp(logit_ref[i % 4, rows] - lse[rows]), 0.0)
        put(s1_ref, 8, i, 32, dot(v1, stacked(w0_ref[i])))
    inside1, inside2 = level_masks(32, 16, k)
    w1_ref[...] = resampled(s1_ref, d1_ref)
    for i in range(8):
        w1 = jnp.where(inside1, w1_ref[i * 32 : i * 32 + 32], 0.0)
        w1_ref[i * 32 : i * 32 + 32] = w1
        put(s2_ref, 8, i, 16, dot(v2, stacked(w1)))
    w2 = resampled(s2_ref, d2_ref)

    def piece(pair, i, c, rows):
        ref = pair[i // 4]
        at = ((i % 4) * 3 + c) * rows
        return ref[at : at + rows]

    for c in range(3):
        blend2 = 0.0
        for i in range(8):
            blend2 = blend2 + w2[i * 16 : i * 16 + 16] * piece((low_a_ref, low_b_ref), i, c, 16)
        put(s3_ref, 3, c, 32, dot(p2, stacked(blend2)))
    rise = resampled(s3_ref, u2_ref)
    for c in range(3):
        total = jnp.where(inside1, rise[c * 32 : c * 32 + 32], 0.0)
        for i in range(8):
            total = total + w1_ref[i * 32 : i * 32 + 32] * piece((mid_a_ref, mid_b_ref), i, c, 32)
        put(s4_ref, 3, c, 32, dot(p1, stacked(total)))
    rise = resampled(s4_ref, u1_ref)
    for c in range(3):
        total = rise[c * 32 : c * 32 + 32]
        for i in range(8):
            total = total + w0_ref[i, 16:48, 0:M0] * piece((fine_a_ref, fine_b_ref), i, c, 32)
        total = total * (1.0 / 255.0)
        left_ref[c] = total[:, :256]
        right_ref[c] = total[:, 256:]


def vmem(count):
    return [pl.BlockSpec(memory_space=pltpu.VMEM)] * count


def smem():
    return [pl.BlockSpec(memory_space=pltpu.SMEM)]


def half(group, index):
    return jnp.stack([lax.dynamic_index_in_dim(main, index, axis=0, keepdims=False) for main in group])


def near_rows(group, core):
    return lax.ppermute(half(group, 1 - core), "c", [(0, 1), (1, 0)])


def far_rows(group, core):
    count = lax.axis_size(ROWS)
    swaps = [(i, i + 1) for i in range(1, count - 1, 2)]
    swaps += [(b, a) for a, b in swaps]
    return lax.ppermute(half(group, core), ROWS, swaps)


def crossed(value, flips):
    pairs = [(4 * c + i, 4 * c + (i ^ flip)) for c, flip in enumerate(flips) for i in range(4)]
    return lax.ppermute(value, ("c", "zh"), pairs)


def join_lse(a, b):
    return jnp.maximum(a, b) + jnp.log(1.0 + jnp.exp(-jnp.abs(a - b)))


def on_device(samples, gain):
    samples, strip, column, core = lax.optimization_barrier(
        (samples, lax.axis_index(ROWS), lax.axis_index("x"), lax.axis_index("c"))
    )
    packed = pl.pallas_call(
        pack_kernel,
        out_shape=(jax.ShapeDtypeStruct((2, 104, 512), F32),) * 4,
        in_specs=[pl.BlockSpec(memory_space=pltpu.HBM)] * 2,
        out_specs=(pl.BlockSpec(memory_space=pltpu.HBM),) * 4,
        scratch_shapes=[
            pltpu.VMEM((6, 32, 2048), jnp.int32),
            pltpu.SMEM((2,), F32),
            pltpu.VMEM((4, 2, 104, 512), F32),
            pltpu.SemaphoreType.DMA((6,)),
            pltpu.SemaphoreType.DMA,
            pltpu.SemaphoreType.DMA((4,)),
        ],
        compiler_params=pltpu.CompilerParams(vmem_limit_bytes=60 * 1024 * 1024),
        name="pack",
    )(samples, gain)
    mains = [packed[0]] + [
        lax.ppermute(packed[m], "x", [(i, i ^ FLIPS[m]) for i in range(4)]) for m in (1, 2, 3)
    ]
    place = jnp.stack([strip, column, core]).astype(jnp.int32)
    far = [far_rows(pair, core) for pair in (mains[:2], mains[2:])]
    logit_shape = jax.ShapeDtypeStruct((4, 64, W0), F32)

    def energy(step, group, *earlier):
        return pl.pallas_call(
            functools.partial(energy_kernel, step == 1),
            out_shape=(logit_shape,) + (jax.ShapeDtypeStruct((30, 8, 128), F32),) * step,
            in_specs=smem() + vmem(4 + step),
            out_specs=tuple(vmem(1 + step)),
            scratch_shapes=[pltpu.VMEM((64, W0), F32)],
            compiler_params=PARAMS,
            cost_estimate=pl.CostEstimate(flops=2_000_000_000, bytes_accessed=6_000_000, transcendentals=0),
            name="energy",
        )(place, *group, *earlier)

    groups = [(*mains[:2], near_rows(mains[:2], core), far[0])]
    logits = energy(0, groups[0])
    late, _ = lax.optimization_barrier((mains[2:], logits))
    groups.append((*mains[2:], near_rows(late, core), far[1]))
    *more, lse = energy(1, groups[1], *logits)
    logits = [*logits, *more]

    taps = [
        jnp.asarray(t, BF)
        for t in (
            column_taps("down", M0, W0, M1, W1),
            column_taps("down", M1, W1, M2, W2),
            column_taps("up", M2, W2, M1, W1),
            column_taps("up", M1, W1, M0, W0)[:, :M0],
        )
    ]
    details = []
    for step, flips in enumerate(((1, 3), (3, 1))):
        other = crossed(lse, flips)
        detail = pl.pallas_call(
            pyramid_kernel,
            out_shape=(
                jax.ShapeDtypeStruct((384, M0), F32),
                jax.ShapeDtypeStruct((384, W1), F32),
                jax.ShapeDtypeStruct((192, W2), F32),
            ),
            in_specs=smem() + vmem(8),
            out_specs=tuple(vmem(3)),
            scratch_shapes=[
                pltpu.VMEM((64, W0), BF),
                pltpu.VMEM((384, W0), BF),
                pltpu.VMEM((192, W1), F32),
                pltpu.VMEM((192, W1), BF),
                pltpu.VMEM((384, W2), BF),
                pltpu.VMEM((384, W1), BF),
            ],
            compiler_params=PARAMS,
            cost_estimate=pl.CostEstimate(flops=2_000_000_000, bytes_accessed=6_000_000, transcendentals=0),
            name="pyramid",
        )(place, *groups[step], *taps)
        other, *detail = lax.optimization_barrier((other, *detail))
        details += detail
        lse = join_lse(lse, other)

    left, right = pl.pallas_call(
        mix_kernel,
        out_shape=(jax.ShapeDtypeStruct((3, 32, 256), F32),) * 2,
        in_specs=smem() + vmem(13),
        out_specs=tuple(vmem(2)),
        scratch_shapes=[
            pltpu.VMEM((64, W0), F32),
            pltpu.VMEM((8, 64, W0), F32),
            pltpu.VMEM((512, W0), BF),
            pltpu.VMEM((256, W1), F32),
            pltpu.VMEM((256, W1), BF),
            pltpu.VMEM((192, W2), BF),
            pltpu.VMEM((192, W1), BF),
        ],
        compiler_params=PARAMS,
        name="mix",
    )(place, *logits, lse, *details, *taps)

    for a, b in ((1, 3), (3, 1)):
        left_in, right_in = crossed(left, (a, b)), crossed(right, (b, a))
        left, right = left + left_in, right + right_in
    whole = jnp.concatenate([left, right], axis=-1)
    joined = lax.all_to_all(jnp.broadcast_to(whole, (4, 3, 32, 512)), "x", 0, 0)
    return joined.transpose(1, 2, 0, 3).reshape(3, 32, 2048)


def solution(mesh):
    fine = Mesh(mesh.devices.reshape(4, 4, 2, 4, 4), ROWS + GZ)
    return jax.shard_map(
        on_device,
        mesh=fine,
        in_specs=(P(GZ, None, ROWS, None), P(GZ)),
        out_specs=P(None, ROWS, None),
        check_vma=False,
    )
```

```python
import functools

import jax
import jax.numpy as jnp
import numpy as np
from jax import lax
from jax.experimental import pallas as pl
from jax.experimental.pallas import tpu as pltpu
from jax.sharding import Mesh
from jax.sharding import PartitionSpec as P

ROWS = ("zl", "y", "c")
GZ = ("zh", "x")
BF = jnp.bfloat16
F32 = jnp.float32
GREY = (0.299 / 255.0, 0.587 / 255.0, 0.114 / 255.0)
W0, W1, W2 = 640, 384, 256
M0, M1, M2 = 512, 256, 128
FLIPS = (0, 2, 1, 3)
PARAMS = pltpu.CompilerParams(vmem_limit_bytes=20 * 1024 * 1024)


def lane_of(col, main, wide):
    if 0 <= col < main + 64:
        return col
    if -64 <= col < 0:
        return wide + col
    return None


def column_taps(kind, main_in, wide_in, main_out, wide_out):
    taps = np.zeros((wide_in, wide_out), np.float32)
    for lane in range(wide_out):
        col = lane if lane < main_out + 64 else lane - wide_out
        if kind == "down":
            picks = [(2 * col + d, t / 16.0) for d, t in zip(range(-2, 3), (1, 4, 6, 4, 1))]
        elif col % 2 == 0:
            picks = [(col // 2 - 1, 0.125), (col // 2, 0.75), (col // 2 + 1, 0.125)]
        else:
            picks = [(col // 2, 0.5), (col // 2 + 1, 0.5)]
        for source, tap in picks:
            at = lane_of(source, main_in, wide_in)
            if at is not None:
                taps[at, lane] += tap
    return taps


def pack_kernel(samples_ref, gain_hbm_ref, *refs):
    packed_refs, (held_ref, gain_ref, out_ref, sems, gain_sem, out_sems) = refs[:4], refs[4:]
    copies = []
    for a in range(6):
        p, c = divmod(a, 3)
        copies.append(pltpu.make_async_copy(samples_ref.at[p, c], held_ref.at[a], sems.at[a]))
        copies[a].start()
    gain_copy = pltpu.make_async_copy(gain_hbm_ref, gain_ref, gain_sem)
    gain_copy.start()
    mine = lax.axis_index("x")
    lane = lax.broadcasted_iota(jnp.int32, (16, 128), 1)
    written = []
    for m, flip in enumerate(FLIPS):
        j = mine ^ flip
        base = pl.multiple_of(512 * j, 512)
        before = pl.multiple_of(jnp.maximum(base - 128, 0), 128)
        after = pl.multiple_of(jnp.minimum(base + 512, 1920), 128)
        has_before, has_after = j > 0, j < 3
        for a in range(6):
            if m == 0:
                copies[a].wait()
            for h in range(2):
                out_ref[m, h, 16 * a : 16 * a + 16, :] = held_ref[a, 16 * h : 16 * h + 16, pl.ds(base, 512)].astype(F32)
        if m == 0:
            gain_copy.wait()
        for h in range(2):
            rows = slice(16 * h, 16 * h + 16)
            tiles = [
                jnp.zeros((16, 128), F32),
                jnp.where(lane < 64, 0.0, jnp.where(lane < 96, gain_ref[0], gain_ref[1])),
            ]
            for a in range(6):
                at, t = 32 * (a % 4), a // 4
                piece = pltpu.roll(held_ref[a, rows, pl.ds(before, 128)].astype(F32), (at - 112) % 128, 1)
                piece = jnp.where(has_before, piece, 0.0)
                tiles[t] = jnp.where((lane >= at) & (lane < at + 16), piece, tiles[t])
                piece = pltpu.roll(held_ref[a, rows, pl.ds(after, 128)].astype(F32), (at + 16) % 128, 1)
                piece = jnp.where(has_after, piece, 0.0)
                tiles[t] = jnp.where((lane >= at + 16) & (lane < at + 32), piece, tiles[t])
            out_ref[m, h, 96:104, 0:128] = tiles[0][0:8]
            out_ref[m, h, 96:104, 128:256] = tiles[1][0:8]
            out_ref[m, h, 96:104, 256:384] = tiles[0][8:16]
            out_ref[m, h, 96:104, 384:512] = tiles[1][8:16]
        written.append(pltpu.make_async_copy(out_ref.at[m], packed_refs[m], out_sems.at[m]))
        written[m].start()
    for copy in written:
        copy.wait()


class Strips:
    def __init__(self, place_ref, mains, near_ref, far_ref):
        self.even = place_ref[2] == 0
        self.mains, self.near, self.far = mains, near_ref, far_ref

    def get(self, s, b, rows, cols):
        if b in (1, 2):
            return self.mains[s][b - 1, rows, cols]
        near, far = self.near[s, rows, cols], self.far[s, rows, cols]
        return jnp.where(self.even, far, near) if b == 0 else jnp.where(self.even, near, far)

    def samples(self, s, b, a):
        return self.get(s, b, slice(16 * a, 16 * a + 16), slice(0, M0))

    def halo(self, s, b, a):
        return halo_tile(lambda cols: self.get(s, b, slice(96, 104), cols), a)


def halo_tile(read, a):
    base, at = 128 * (a // 4), 32 * (a % 4)
    tile = jnp.concatenate([read(slice(base, base + 128)), read(slice(256 + base, 384 + base))], axis=0)
    lane = lax.broadcasted_iota(jnp.int32, (16, 128), 1)
    return jnp.where((lane < 16) | (lane >= 112), pltpu.roll(tile, (112 - at) % 128, 1), 0.0)


def column_of(shape, main, wide):
    lane = lax.broadcasted_iota(jnp.int32, shape, len(shape) - 1)
    return jnp.where(lane < main + 64, lane, lane - wide)


def energy_kernel(second, place_ref, main_a_ref, main_b_ref, near_ref, far_ref, *refs):
    earlier_ref, logit_ref, lse_ref, grey_ref = refs if second else (None, refs[0], None, refs[1])
    row = lax.broadcasted_iota(jnp.int32, (64, W0), 0) + (place_ref[0] * 32 - 16)
    col = column_of((64, W0), M0, W0) + place_ref[1] * M0
    keep = (row >= 0) & (row < 1024) & (col >= 0) & (col < 2048)

    mains = (main_a_ref, main_b_ref)
    strips = Strips(place_ref, mains, near_ref, far_ref)
    for s in range(2):
        for p in range(2):
            for b in range(4):
                main = 0.0
                tile = 0.0
                for c in range(3):
                    a = 3 * p + c
                    main = main + strips.samples(s, b, a) * GREY[c]
                    tile = tile + strips.halo(s, b, a) * GREY[c]
                grey_ref[16 * b : 16 * b + 16, 0:M0] = main
                grey_ref[16 * b : 16 * b + 16, M0:W0] = tile
            grey = grey_ref[...]
            lap = (
                4.0 * grey
                - pltpu.roll(grey, 1, 0)
                - pltpu.roll(grey, 63, 0)
                - pltpu.roll(grey, 1, 1)
                - pltpu.roll(grey, W0 - 1, 1)
            )
            field = jnp.where(keep, lap * lap, 0.0)
            for axis, size in ((0, 64), (1, W0)):
                two = field + pltpu.roll(field, size - 1, axis)
                four = two + pltpu.roll(two, size - 2, axis)
                eight = four + pltpu.roll(four, size - 4, axis)
                field = pltpu.roll(eight, 4, axis) + pltpu.roll(field, size - 4, axis)
            gain = mains[s][0, 96:97, 192 + 32 * p : 193 + 32 * p]
            logit_ref[2 * s + p] = gain * field

    if second:
        logits = [ref.at[i] for ref in (earlier_ref, logit_ref) for i in range(4)]
        peak = logits[0][...]
        for ref in logits[1:]:
            peak = jnp.maximum(peak, ref[...])
        total = 0.0
        for ref in logits:
            total = total + jnp.exp(ref[...] - peak)
        lse = pltpu.roll(peak + jnp.log(total), 58, 0)[0:56]
        lane = lax.broadcasted_iota(jnp.int32, (8, 128), 1)
        shared = [jnp.zeros((8, 128), F32)] * 2
        for i in range(7):
            rows = slice(8 * i, 8 * i + 8)
            for j in range(4):
                lse_ref[4 * i + j] = lse[rows, 128 * j : 128 * j + 128]
            at = 32 * (i % 4)
            piece = pltpu.roll(lse[rows, M0:W0], (16 + at) % 128, 1)
            shared[i // 4] = jnp.where((lane >= at) & (lane < at + 32), piece, shared[i // 4])
        lse_ref[28] = shared[0]
        lse_ref[29] = shared[1]


def split2(value):
    high = value.astype(BF)
    low = (value - high.astype(F32)).astype(BF)
    return high, low


def stacked(value):
    return jnp.concatenate(split2(value), axis=0)


def dot(a, b):
    return jnp.dot(a, b, preferred_element_type=F32)


def iota2(shape):
    return lax.broadcasted_iota(jnp.int32, shape, 0), lax.broadcasted_iota(jnp.int32, shape, 1)


def down_rows(count, inputs, copies, first, limit):
    q, e = iota2((count, inputs * copies))
    if copies == 2:
        e = jnp.where(e >= inputs, e - inputs, e)
    gap = jnp.abs(e - 2 * q)
    taps = jnp.where(gap == 0, 0.375, jnp.where(gap == 1, 0.25, jnp.where(gap == 2, 0.0625, 0.0)))
    inside = (q + first >= 0) & (q + first < limit)
    return jnp.where(inside, taps, 0.0).astype(BF)


def up_rows(count, inputs, offset, first, limit):
    r, q = iota2((count, 2 * inputs))
    q = jnp.where(q >= inputs, q - inputs, q)
    gap = jnp.abs(2 * q - (r + offset))
    even = (r & 1) == 0
    taps = jnp.where(
        even,
        jnp.where(gap == 0, 0.75, jnp.where(gap == 2, 0.125, 0.0)),
        jnp.where(gap == 1, 0.5, 0.0),
    )
    inside = (r + first >= 0) & (r + first < limit)
    return jnp.where(inside, taps, 0.0).astype(BF)


def row_matrices(strip):
    v2 = down_rows(16, 32, 2, strip * 8 - 4, 256)
    p2 = up_rows(32, 16, 0, strip * 16 - 8, 512)
    p1 = up_rows(32, 32, 16, 0, 32)
    return v2, p2, p1


def level_masks(rows1, rows2, k):
    col1 = column_of((rows1, W1), M1, W1) + k * M1
    col2 = column_of((rows2, W2), M2, W2) + k * M2
    return (col1 >= 0) & (col1 < 1024), (col2 >= 0) & (col2 < 512)


def put(ref, n, a, count, value):
    high, low = split2(value)
    ref[a * count : (a + 1) * count] = high
    ref[(n + a) * count : (n + a + 1) * count] = low


def resampled(source_ref, taps_ref):
    both = dot(source_ref[...], taps_ref[...])
    half = both.shape[0] // 2
    return both[:half] + both[half:]


def pyramid_kernel(
    place_ref, main_a_ref, main_b_ref, near_ref, far_ref, d1_ref, d2_ref, u2_ref, u1_ref,
    detail0_ref, detail1_ref, l2_ref, x_ref, s1_ref, l1_ref, s2_ref, s3_ref, s4_ref,
):
    strip = place_ref[0]
    v1 = down_rows(32, 64, 1, strip * 16 - 8, 512)
    v2, p2, p1 = row_matrices(strip)
    inside1, inside2 = level_masks(192, 96, place_ref[1])
    mains = (main_a_ref, main_b_ref)
    strips = Strips(place_ref, mains, near_ref, far_ref)
    for i in range(2):
        for a in range(6):
            for b in range(4):
                x_ref[16 * b : 16 * b + 16, 0:M0] = strips.samples(i, b, a).astype(BF)
                x_ref[16 * b : 16 * b + 16, M0:W0] = strips.halo(i, b, a).astype(BF)
            put(s1_ref, 6, a, 32, dot(v1, x_ref[...]))
        l1_ref[...] = jnp.where(inside1, resampled(s1_ref, d1_ref), 0.0)
        for a in range(6):
            both = stacked(l1_ref[a * 32 : a * 32 + 32])
            put(s2_ref, 6, a, 16, dot(v2, both))
            put(s4_ref, 6, a, 32, dot(p1, both))
        l2 = jnp.where(inside2, resampled(s2_ref, d2_ref), 0.0)
        l2_ref[i * 96 : i * 96 + 96] = l2
        for a in range(6):
            put(s3_ref, 6, a, 32, dot(p2, stacked(l2[a * 16 : a * 16 + 16])))
        detail1_ref[i * 192 : i * 192 + 192] = l1_ref[...] - resampled(s3_ref, u2_ref)
        part = resampled(s4_ref, u1_ref)
        for a in range(6):
            for h in range(2):
                at = a * 32 + 16 * h
                detail0_ref[i * 192 + at : i * 192 + at + 16] = (
                    mains[i][h, 16 * a : 16 * a + 16, :] - part[at : at + 16]
                )


def mix_kernel(
    place_ref, logit_a_ref, logit_b_ref, lse_ref,
    fine_a_ref, mid_a_ref, low_a_ref, fine_b_ref, mid_b_ref, low_b_ref,
    d1_ref, d2_ref, u2_ref, u1_ref,
    left_ref, right_ref, tiles_ref, w0_ref, s1_ref, w1_ref, s2_ref, s3_ref, s4_ref,
):
    strip, k = place_ref[0], place_ref[1]
    v1 = down_rows(32, 64, 2, strip * 16 - 8, 512)
    v2, p2, p1 = row_matrices(strip)
    col = column_of((16, W0), M0, W0)
    inside_col = (col >= -10) & (col <= 522) & (col + k * M0 >= 0) & (col + k * M0 < 2048)
    row = lax.broadcasted_iota(jnp.int32, (16, W0), 0)
    for i in range(7):
        rows = slice(8 * i, 8 * i + 8)
        for j in range(4):
            tiles_ref[rows, 128 * j : 128 * j + 128] = lse_ref[4 * i + j]
        tiles_ref[rows, M0:W0] = pltpu.roll(lse_ref[28 + i // 4], (112 - 32 * (i % 4)) % 128, 1)
    tiles_ref[56:64] = jnp.zeros((8, W0), F32)
    lse = pltpu.roll(tiles_ref[...], 6, 0)
    keeps = []
    for b in range(4):
        r = row + (16 * b - 16)
        g = r + strip * 32
        keeps.append(inside_col & (r >= -10) & (r <= 42) & (g >= 0) & (g < 1024))
    for i in range(8):
        logit_ref = (logit_a_ref, logit_b_ref)[i // 4]
        for b in range(4):
            rows = slice(16 * b, 16 * b + 16)
            w0_ref[i, rows] = jnp.where(keeps[b], jnp.exp(logit_ref[i % 4, rows] - lse[rows]), 0.0)
        put(s1_ref, 8, i, 32, dot(v1, stacked(w0_ref[i])))
    inside1, inside2 = level_masks(32, 16, k)
    w1_ref[...] = resampled(s1_ref, d1_ref)
    for i in range(8):
        w1 = jnp.where(inside1, w1_ref[i * 32 : i * 32 + 32], 0.0)
        w1_ref[i * 32 : i * 32 + 32] = w1
        put(s2_ref, 8, i, 16, dot(v2, stacked(w1)))
    w2 = resampled(s2_ref, d2_ref)

    def piece(pair, i, c, rows):
        ref = pair[i // 4]
        at = ((i % 4) * 3 + c) * rows
        return ref[at : at + rows]

    for c in range(3):
        blend2 = 0.0
        for i in range(8):
            blend2 = blend2 + w2[i * 16 : i * 16 + 16] * piece((low_a_ref, low_b_ref), i, c, 16)
        put(s3_ref, 3, c, 32, dot(p2, stacked(blend2)))
    rise = resampled(s3_ref, u2_ref)
    for c in range(3):
        total = jnp.where(inside1, rise[c * 32 : c * 32 + 32], 0.0)
        for i in range(8):
            total = total + w1_ref[i * 32 : i * 32 + 32] * piece((mid_a_ref, mid_b_ref), i, c, 32)
        put(s4_ref, 3, c, 32, dot(p1, stacked(total)))
    rise = resampled(s4_ref, u1_ref)
    for c in range(3):
        total = rise[c * 32 : c * 32 + 32]
        for i in range(8):
            total = total + w0_ref[i, 16:48, 0:M0] * piece((fine_a_ref, fine_b_ref), i, c, 32)
        total = total * (1.0 / 255.0)
        left_ref[c] = total[:, :256]
        right_ref[c] = total[:, 256:]


def vmem(count):
    return [pl.BlockSpec(memory_space=pltpu.VMEM)] * count


def smem():
    return [pl.BlockSpec(memory_space=pltpu.SMEM)]


def half(group, index):
    return jnp.stack([lax.dynamic_index_in_dim(main, index, axis=0, keepdims=False) for main in group])


def near_rows(group, core):
    return lax.ppermute(half(group, 1 - core), "c", [(0, 1), (1, 0)])


def far_rows(group, core):
    count = lax.axis_size(ROWS)
    swaps = [(i, i + 1) for i in range(1, count - 1, 2)]
    swaps += [(b, a) for a, b in swaps]
    return lax.ppermute(half(group, core), ROWS, swaps)


def crossed(value, flips):
    pairs = [(4 * c + i, 4 * c + (i ^ flip)) for c, flip in enumerate(flips) for i in range(4)]
    return lax.ppermute(value, ("c", "zh"), pairs)


def join_lse(a, b):
    return jnp.maximum(a, b) + jnp.log(1.0 + jnp.exp(-jnp.abs(a - b)))


def on_device(samples, gain):
    samples, strip, column, core = lax.optimization_barrier(
        (samples, lax.axis_index(ROWS), lax.axis_index("x"), lax.axis_index("c"))
    )
    packed = pl.pallas_call(
        pack_kernel,
        out_shape=(jax.ShapeDtypeStruct((2, 104, 512), F32),) * 4,
        in_specs=[pl.BlockSpec(memory_space=pltpu.HBM)] * 2,
        out_specs=(pl.BlockSpec(memory_space=pltpu.HBM),) * 4,
        scratch_shapes=[
            pltpu.VMEM((6, 32, 2048), jnp.int32),
            pltpu.SMEM((2,), F32),
            pltpu.VMEM((4, 2, 104, 512), F32),
            pltpu.SemaphoreType.DMA((6,)),
            pltpu.SemaphoreType.DMA,
            pltpu.SemaphoreType.DMA((4,)),
        ],
        compiler_params=pltpu.CompilerParams(vmem_limit_bytes=60 * 1024 * 1024),
        name="pack",
    )(samples, gain)
    mains = [packed[0]] + [
        lax.ppermute(packed[m], "x", [(i, i ^ FLIPS[m]) for i in range(4)]) for m in (1, 2, 3)
    ]
    place = jnp.stack([strip, column, core]).astype(jnp.int32)
    far = [far_rows(pair, core) for pair in (mains[:2], mains[2:])]
    logit_shape = jax.ShapeDtypeStruct((4, 64, W0), F32)

    def energy(step, group, *earlier):
        return pl.pallas_call(
            functools.partial(energy_kernel, step == 1),
            out_shape=(logit_shape,) + (jax.ShapeDtypeStruct((30, 8, 128), F32),) * step,
            in_specs=smem() + vmem(4 + step),
            out_specs=tuple(vmem(1 + step)),
            scratch_shapes=[pltpu.VMEM((64, W0), F32)],
            compiler_params=PARAMS,
            cost_estimate=pl.CostEstimate(flops=2_000_000_000, bytes_accessed=6_000_000, transcendentals=0),
            name="energy",
        )(place, *group, *earlier)

    groups = [(*mains[:2], near_rows(mains[:2], core), far[0])]
    logits = energy(0, groups[0])
    late, _ = lax.optimization_barrier((mains[2:], groups[0][3]))
    groups.append((*mains[2:], near_rows(late, core), far[1]))
    *more, lse = energy(1, groups[1], *logits)
    logits = [*logits, *more]

    taps = [
        jnp.asarray(t, BF)
        for t in (
            column_taps("down", M0, W0, M1, W1),
            column_taps("down", M1, W1, M2, W2),
            column_taps("up", M2, W2, M1, W1),
            column_taps("up", M1, W1, M0, W0)[:, :M0],
        )
    ]
    details = []
    for step, flips in enumerate(((1, 3), (3, 1))):
        other = crossed(lse, flips)
        detail = pl.pallas_call(
            pyramid_kernel,
            out_shape=(
                jax.ShapeDtypeStruct((384, M0), F32),
                jax.ShapeDtypeStruct((384, W1), F32),
                jax.ShapeDtypeStruct((192, W2), F32),
            ),
            in_specs=smem() + vmem(8),
            out_specs=tuple(vmem(3)),
            scratch_shapes=[
                pltpu.VMEM((64, W0), BF),
                pltpu.VMEM((384, W0), BF),
                pltpu.VMEM((192, W1), F32),
                pltpu.VMEM((192, W1), BF),
                pltpu.VMEM((384, W2), BF),
                pltpu.VMEM((384, W1), BF),
            ],
            compiler_params=PARAMS,
            cost_estimate=pl.CostEstimate(flops=2_000_000_000, bytes_accessed=6_000_000, transcendentals=0),
            name="pyramid",
        )(place, *groups[step], *taps)
        other, *detail = lax.optimization_barrier((other, *detail))
        details += detail
        lse = join_lse(lse, other)

    left, right = pl.pallas_call(
        mix_kernel,
        out_shape=(jax.ShapeDtypeStruct((3, 32, 256), F32),) * 2,
        in_specs=smem() + vmem(13),
        out_specs=tuple(vmem(2)),
        scratch_shapes=[
            pltpu.VMEM((64, W0), F32),
            pltpu.VMEM((8, 64, W0), F32),
            pltpu.VMEM((512, W0), BF),
            pltpu.VMEM((256, W1), F32),
            pltpu.VMEM((256, W1), BF),
            pltpu.VMEM((192, W2), BF),
            pltpu.VMEM((192, W1), BF),
        ],
        compiler_params=PARAMS,
        name="mix",
    )(place, *logits, lse, *details, *taps)

    for a, b in ((1, 3), (3, 1)):
        left_in, right_in = crossed(left, (a, b)), crossed(right, (b, a))
        left, right = left + left_in, right + right_in
    whole = jnp.concatenate([left, right], axis=-1)
    joined = lax.all_to_all(jnp.broadcast_to(whole, (4, 3, 32, 512)), "x", 0, 0)
    return joined.transpose(1, 2, 0, 3).reshape(3, 32, 2048)


def solution(mesh):
    fine = Mesh(mesh.devices.reshape(4, 4, 2, 4, 4), ROWS + GZ)
    return jax.shard_map(
        on_device,
        mesh=fine,
        in_specs=(P(GZ, None, ROWS, None), P(GZ)),
        out_specs=P(None, ROWS, None),
        check_vma=False,
    )
```

```python
import functools

import jax
import jax.numpy as jnp
import numpy as np
from jax import lax
from jax.experimental import pallas as pl
from jax.experimental.pallas import tpu as pltpu
from jax.sharding import Mesh
from jax.sharding import PartitionSpec as P

ROWS = ("zl", "y", "c")
GZ = ("zh", "x")
BF = jnp.bfloat16
F32 = jnp.float32
GREY = (0.299 / 255.0, 0.587 / 255.0, 0.114 / 255.0)
W0, W1, W2 = 640, 384, 256
M0, M1, M2 = 512, 256, 128
FLIPS = (0, 2, 1, 3)
PARAMS = pltpu.CompilerParams(vmem_limit_bytes=20 * 1024 * 1024)


def lane_of(col, main, wide):
    if 0 <= col < main + 64:
        return col
    if -64 <= col < 0:
        return wide + col
    return None


def column_taps(kind, main_in, wide_in, main_out, wide_out):
    taps = np.zeros((wide_in, wide_out), np.float32)
    for lane in range(wide_out):
        col = lane if lane < main_out + 64 else lane - wide_out
        if kind == "down":
            picks = [(2 * col + d, t / 16.0) for d, t in zip(range(-2, 3), (1, 4, 6, 4, 1))]
        elif col % 2 == 0:
            picks = [(col // 2 - 1, 0.125), (col // 2, 0.75), (col // 2 + 1, 0.125)]
        else:
            picks = [(col // 2, 0.5), (col // 2 + 1, 0.5)]
        for source, tap in picks:
            at = lane_of(source, main_in, wide_in)
            if at is not None:
                taps[at, lane] += tap
    return taps


def pack_kernel(samples_ref, gain_hbm_ref, *refs):
    packed_refs, (held_ref, gain_ref, out_ref, sems, gain_sem, out_sems) = refs[:4], refs[4:]
    copies = []
    for a in range(6):
        p, c = divmod(a, 3)
        copies.append(pltpu.make_async_copy(samples_ref.at[p, c], held_ref.at[a], sems.at[a]))
        copies[a].start()
    gain_copy = pltpu.make_async_copy(gain_hbm_ref, gain_ref, gain_sem)
    gain_copy.start()
    mine = lax.axis_index("x")
    lane = lax.broadcasted_iota(jnp.int32, (16, 128), 1)
    written = []
    for m, flip in enumerate(FLIPS):
        j = mine ^ flip
        base = pl.multiple_of(512 * j, 512)
        before = pl.multiple_of(jnp.maximum(base - 128, 0), 128)
        after = pl.multiple_of(jnp.minimum(base + 512, 1920), 128)
        has_before, has_after = j > 0, j < 3
        for a in range(6):
            if m == 0:
                copies[a].wait()
            for h in range(2):
                out_ref[m, h, 16 * a : 16 * a + 16, :] = held_ref[a, 16 * h : 16 * h + 16, pl.ds(base, 512)].astype(F32)
        if m == 0:
            gain_copy.wait()
        for h in range(2):
            rows = slice(16 * h, 16 * h + 16)
            tiles = [
                jnp.zeros((16, 128), F32),
                jnp.where(lane < 64, 0.0, jnp.where(lane < 96, gain_ref[0], gain_ref[1])),
            ]
            for a in range(6):
                at, t = 32 * (a % 4), a // 4
                piece = pltpu.roll(held_ref[a, rows, pl.ds(before, 128)].astype(F32), (at - 112) % 128, 1)
                piece = jnp.where(has_before, piece, 0.0)
                tiles[t] = jnp.where((lane >= at) & (lane < at + 16), piece, tiles[t])
                piece = pltpu.roll(held_ref[a, rows, pl.ds(after, 128)].astype(F32), (at + 16) % 128, 1)
                piece = jnp.where(has_after, piece, 0.0)
                tiles[t] = jnp.where((lane >= at + 16) & (lane < at + 32), piece, tiles[t])
            out_ref[m, h, 96:104, 0:128] = tiles[0][0:8]
            out_ref[m, h, 96:104, 128:256] = tiles[1][0:8]
            out_ref[m, h, 96:104, 256:384] = tiles[0][8:16]
            out_ref[m, h, 96:104, 384:512] = tiles[1][8:16]
        written.append(pltpu.make_async_copy(out_ref.at[m], packed_refs[m], out_sems.at[m]))
        written[m].start()
    for copy in written:
        copy.wait()


class Strips:
    def __init__(self, place_ref, mains, near_ref, far_ref):
        self.even = place_ref[2] == 0
        self.mains, self.near, self.far = mains, near_ref, far_ref

    def get(self, s, b, rows, cols):
        if b in (1, 2):
            return self.mains[s][b - 1, rows, cols]
        near, far = self.near[s, rows, cols], self.far[s, rows, cols]
        return jnp.where(self.even, far, near) if b == 0 else jnp.where(self.even, near, far)

    def samples(self, s, b, a):
        return self.get(s, b, slice(16 * a, 16 * a + 16), slice(0, M0))

    def halo(self, s, b, a):
        return halo_tile(lambda cols: self.get(s, b, slice(96, 104), cols), a)


def halo_tile(read, a):
    base, at = 128 * (a // 4), 32 * (a % 4)
    tile = jnp.concatenate([read(slice(base, base + 128)), read(slice(256 + base, 384 + base))], axis=0)
    lane = lax.broadcasted_iota(jnp.int32, (16, 128), 1)
    return jnp.where((lane < 16) | (lane >= 112), pltpu.roll(tile, (112 - at) % 128, 1), 0.0)


def column_of(shape, main, wide):
    lane = lax.broadcasted_iota(jnp.int32, shape, len(shape) - 1)
    return jnp.where(lane < main + 64, lane, lane - wide)


def energy_kernel(second, place_ref, main_a_ref, main_b_ref, near_ref, far_ref, *refs):
    if second:
        earlier_ref, logit_ref, lse_ref, grey_ref = refs
    else:
        logit_ref, part_ref, grey_ref = refs
    row = lax.broadcasted_iota(jnp.int32, (64, W0), 0) + (place_ref[0] * 32 - 16)
    col = column_of((64, W0), M0, W0) + place_ref[1] * M0
    keep = (row >= 0) & (row < 1024) & (col >= 0) & (col < 2048)

    mains = (main_a_ref, main_b_ref)
    strips = Strips(place_ref, mains, near_ref, far_ref)
    for s in range(2):
        for p in range(2):
            for b in range(4):
                main = 0.0
                tile = 0.0
                for c in range(3):
                    a = 3 * p + c
                    main = main + strips.samples(s, b, a) * GREY[c]
                    tile = tile + strips.halo(s, b, a) * GREY[c]
                grey_ref[16 * b : 16 * b + 16, 0:M0] = main
                grey_ref[16 * b : 16 * b + 16, M0:W0] = tile
            grey = grey_ref[...]
            lap = (
                4.0 * grey
                - pltpu.roll(grey, 1, 0)
                - pltpu.roll(grey, 63, 0)
                - pltpu.roll(grey, 1, 1)
                - pltpu.roll(grey, W0 - 1, 1)
            )
            field = jnp.where(keep, lap * lap, 0.0)
            for axis, size in ((0, 64), (1, W0)):
                two = field + pltpu.roll(field, size - 1, axis)
                four = two + pltpu.roll(two, size - 2, axis)
                eight = four + pltpu.roll(four, size - 4, axis)
                field = pltpu.roll(eight, 4, axis) + pltpu.roll(field, size - 4, axis)
            gain = mains[s][0, 96:97, 192 + 32 * p : 193 + 32 * p]
            logit_ref[2 * s + p] = gain * field

    peak = logit_ref[0]
    for i in range(1, 4):
        peak = jnp.maximum(peak, logit_ref[i])
    if second:
        peak = jnp.maximum(peak, earlier_ref[0])
    total = 0.0
    for i in range(4):
        total = total + jnp.exp(logit_ref[i] - peak)
    if not second:
        part_ref[0] = peak
        part_ref[1] = total
    else:
        total = total + earlier_ref[1] * jnp.exp(earlier_ref[0] - peak)
        lse = pltpu.roll(peak + jnp.log(total), 58, 0)[0:56]
        lane = lax.broadcasted_iota(jnp.int32, (8, 128), 1)
        shared = [jnp.zeros((8, 128), F32)] * 2
        for i in range(7):
            rows = slice(8 * i, 8 * i + 8)
            for j in range(4):
                lse_ref[4 * i + j] = lse[rows, 128 * j : 128 * j + 128]
            at = 32 * (i % 4)
            piece = pltpu.roll(lse[rows, M0:W0], (16 + at) % 128, 1)
            shared[i // 4] = jnp.where((lane >= at) & (lane < at + 32), piece, shared[i // 4])
        lse_ref[28] = shared[0]
        lse_ref[29] = shared[1]


def split2(value):
    high = value.astype(BF)
    low = (value - high.astype(F32)).astype(BF)
    return high, low


def stacked(value):
    return jnp.concatenate(split2(value), axis=0)


def dot(a, b):
    return jnp.dot(a, b, preferred_element_type=F32)


def iota2(shape):
    return lax.broadcasted_iota(jnp.int32, shape, 0), lax.broadcasted_iota(jnp.int32, shape, 1)


def down_rows(count, inputs, copies, first, limit):
    q, e = iota2((count, inputs * copies))
    if copies == 2:
        e = jnp.where(e >= inputs, e - inputs, e)
    gap = jnp.abs(e - 2 * q)
    taps = jnp.where(gap == 0, 0.375, jnp.where(gap == 1, 0.25, jnp.where(gap == 2, 0.0625, 0.0)))
    inside = (q + first >= 0) & (q + first < limit)
    return jnp.where(inside, taps, 0.0).astype(BF)


def up_rows(count, inputs, offset, first, limit):
    r, q = iota2((count, 2 * inputs))
    q = jnp.where(q >= inputs, q - inputs, q)
    gap = jnp.abs(2 * q - (r + offset))
    even = (r & 1) == 0
    taps = jnp.where(
        even,
        jnp.where(gap == 0, 0.75, jnp.where(gap == 2, 0.125, 0.0)),
        jnp.where(gap == 1, 0.5, 0.0),
    )
    inside = (r + first >= 0) & (r + first < limit)
    return jnp.where(inside, taps, 0.0).astype(BF)


def row_matrices(strip):
    v2 = down_rows(16, 32, 2, strip * 8 - 4, 256)
    p2 = up_rows(32, 16, 0, strip * 16 - 8, 512)
    p1 = up_rows(32, 32, 16, 0, 32)
    return v2, p2, p1


def level_masks(rows1, rows2, k):
    col1 = column_of((rows1, W1), M1, W1) + k * M1
    col2 = column_of((rows2, W2), M2, W2) + k * M2
    return (col1 >= 0) & (col1 < 1024), (col2 >= 0) & (col2 < 512)


def put(ref, n, a, count, value):
    high, low = split2(value)
    ref[a * count : (a + 1) * count] = high
    ref[(n + a) * count : (n + a + 1) * count] = low


def resampled(source_ref, taps_ref):
    both = dot(source_ref[...], taps_ref[...])
    half = both.shape[0] // 2
    return both[:half] + both[half:]


def pyramid_kernel(
    place_ref, main_a_ref, main_b_ref, near_ref, far_ref, d1_ref, d2_ref, u2_ref, u1_ref,
    detail0_ref, detail1_ref, l2_ref, x_ref, s1_ref, l1_ref, s2_ref, s3_ref, s4_ref,
):
    strip = place_ref[0]
    v1 = down_rows(32, 64, 1, strip * 16 - 8, 512)
    v2, p2, p1 = row_matrices(strip)
    inside1, inside2 = level_masks(192, 96, place_ref[1])
    mains = (main_a_ref, main_b_ref)
    strips = Strips(place_ref, mains, near_ref, far_ref)
    for i in range(2):
        for a in range(6):
            for b in range(4):
                x_ref[16 * b : 16 * b + 16, 0:M0] = strips.samples(i, b, a).astype(BF)
                x_ref[16 * b : 16 * b + 16, M0:W0] = strips.halo(i, b, a).astype(BF)
            put(s1_ref, 6, a, 32, dot(v1, x_ref[...]))
        l1_ref[...] = jnp.where(inside1, resampled(s1_ref, d1_ref), 0.0)
        for a in range(6):
            both = stacked(l1_ref[a * 32 : a * 32 + 32])
            put(s2_ref, 6, a, 16, dot(v2, both))
            put(s4_ref, 6, a, 32, dot(p1, both))
        l2 = jnp.where(inside2, resampled(s2_ref, d2_ref), 0.0)
        l2_ref[i * 96 : i * 96 + 96] = l2
        for a in range(6):
            put(s3_ref, 6, a, 32, dot(p2, stacked(l2[a * 16 : a * 16 + 16])))
        detail1_ref[i * 192 : i * 192 + 192] = l1_ref[...] - resampled(s3_ref, u2_ref)
        part = resampled(s4_ref, u1_ref)
        for a in range(6):
            for h in range(2):
                at = a * 32 + 16 * h
                detail0_ref[i * 192 + at : i * 192 + at + 16] = (
                    mains[i][h, 16 * a : 16 * a + 16, :] - part[at : at + 16]
                )


def mix_kernel(
    place_ref, logit_a_ref, logit_b_ref, lse_ref,
    fine_a_ref, mid_a_ref, low_a_ref, fine_b_ref, mid_b_ref, low_b_ref,
    d1_ref, d2_ref, u2_ref, u1_ref,
    left_ref, right_ref, tiles_ref, w0_ref, s1_ref, w1_ref, s2_ref, s3_ref, s4_ref,
):
    strip, k = place_ref[0], place_ref[1]
    v1 = down_rows(32, 64, 2, strip * 16 - 8, 512)
    v2, p2, p1 = row_matrices(strip)
    col = column_of((16, W0), M0, W0)
    inside_col = (col >= -10) & (col <= 522) & (col + k * M0 >= 0) & (col + k * M0 < 2048)
    row = lax.broadcasted_iota(jnp.int32, (16, W0), 0)
    for i in range(7):
        rows = slice(8 * i, 8 * i + 8)
        for j in range(4):
            tiles_ref[rows, 128 * j : 128 * j + 128] = lse_ref[4 * i + j]
        tiles_ref[rows, M0:W0] = pltpu.roll(lse_ref[28 + i // 4], (112 - 32 * (i % 4)) % 128, 1)
    tiles_ref[56:64] = jnp.zeros((8, W0), F32)
    lse = pltpu.roll(tiles_ref[...], 6, 0)
    keeps = []
    for b in range(4):
        r = row + (16 * b - 16)
        g = r + strip * 32
        keeps.append(inside_col & (r >= -10) & (r <= 42) & (g >= 0) & (g < 1024))
    for i in range(8):
        logit_ref = (logit_a_ref, logit_b_ref)[i // 4]
        for b in range(4):
            rows = slice(16 * b, 16 * b + 16)
            w0_ref[i, rows] = jnp.where(keeps[b], jnp.exp(logit_ref[i % 4, rows] - lse[rows]), 0.0)
        put(s1_ref, 8, i, 32, dot(v1, stacked(w0_ref[i])))
    inside1, inside2 = level_masks(32, 16, k)
    w1_ref[...] = resampled(s1_ref, d1_ref)
    for i in range(8):
        w1 = jnp.where(inside1, w1_ref[i * 32 : i * 32 + 32], 0.0)
        w1_ref[i * 32 : i * 32 + 32] = w1
        put(s2_ref, 8, i, 16, dot(v2, stacked(w1)))
    w2 = resampled(s2_ref, d2_ref)

    def piece(pair, i, c, rows):
        ref = pair[i // 4]
        at = ((i % 4) * 3 + c) * rows
        return ref[at : at + rows]

    for c in range(3):
        blend2 = 0.0
        for i in range(8):
            blend2 = blend2 + w2[i * 16 : i * 16 + 16] * piece((low_a_ref, low_b_ref), i, c, 16)
        put(s3_ref, 3, c, 32, dot(p2, stacked(blend2)))
    rise = resampled(s3_ref, u2_ref)
    for c in range(3):
        total = jnp.where(inside1, rise[c * 32 : c * 32 + 32], 0.0)
        for i in range(8):
            total = total + w1_ref[i * 32 : i * 32 + 32] * piece((mid_a_ref, mid_b_ref), i, c, 32)
        put(s4_ref, 3, c, 32, dot(p1, stacked(total)))
    rise = resampled(s4_ref, u1_ref)
    for c in range(3):
        total = rise[c * 32 : c * 32 + 32]
        for i in range(8):
            total = total + w0_ref[i, 16:48, 0:M0] * piece((fine_a_ref, fine_b_ref), i, c, 32)
        total = total * (1.0 / 255.0)
        left_ref[c] = total[:, :256]
        right_ref[c] = total[:, 256:]


def vmem(count):
    return [pl.BlockSpec(memory_space=pltpu.VMEM)] * count


def smem():
    return [pl.BlockSpec(memory_space=pltpu.SMEM)]


def half(group, index):
    return jnp.stack([lax.dynamic_index_in_dim(main, index, axis=0, keepdims=False) for main in group])


def near_rows(group, core):
    return lax.ppermute(half(group, 1 - core), "c", [(0, 1), (1, 0)])


def far_rows(group, core):
    count = lax.axis_size(ROWS)
    swaps = [(i, i + 1) for i in range(1, count - 1, 2)]
    swaps += [(b, a) for a, b in swaps]
    return lax.ppermute(half(group, core), ROWS, swaps)


def crossed(value, flips):
    pairs = [(4 * c + i, 4 * c + (i ^ flip)) for c, flip in enumerate(flips) for i in range(4)]
    return lax.ppermute(value, ("c", "zh"), pairs)


def join_lse(a, b):
    return jnp.maximum(a, b) + jnp.log(1.0 + jnp.exp(-jnp.abs(a - b)))


def on_device(samples, gain):
    samples, strip, column, core = lax.optimization_barrier(
        (samples, lax.axis_index(ROWS), lax.axis_index("x"), lax.axis_index("c"))
    )
    packed = pl.pallas_call(
        pack_kernel,
        out_shape=(jax.ShapeDtypeStruct((2, 104, 512), F32),) * 4,
        in_specs=[pl.BlockSpec(memory_space=pltpu.HBM)] * 2,
        out_specs=(pl.BlockSpec(memory_space=pltpu.HBM),) * 4,
        scratch_shapes=[
            pltpu.VMEM((6, 32, 2048), jnp.int32),
            pltpu.SMEM((2,), F32),
            pltpu.VMEM((4, 2, 104, 512), F32),
            pltpu.SemaphoreType.DMA((6,)),
            pltpu.SemaphoreType.DMA,
            pltpu.SemaphoreType.DMA((4,)),
        ],
        compiler_params=pltpu.CompilerParams(vmem_limit_bytes=60 * 1024 * 1024),
        name="pack",
    )(samples, gain)
    mains = [packed[0]] + [
        lax.ppermute(packed[m], "x", [(i, i ^ FLIPS[m]) for i in range(4)]) for m in (1, 2, 3)
    ]
    place = jnp.stack([strip, column, core]).astype(jnp.int32)
    far = [far_rows(pair, core) for pair in (mains[:2], mains[2:])]
    logit_shape = jax.ShapeDtypeStruct((4, 64, W0), F32)

    def energy(step, group, *earlier):
        return pl.pallas_call(
            functools.partial(energy_kernel, step == 1),
            out_shape=(logit_shape, jax.ShapeDtypeStruct((30, 8, 128) if step else (2, 64, W0), F32)),
            in_specs=smem() + vmem(4 + step),
            out_specs=tuple(vmem(2)),
            scratch_shapes=[pltpu.VMEM((64, W0), F32)],
            compiler_params=PARAMS,
            cost_estimate=pl.CostEstimate(flops=2_000_000_000, bytes_accessed=6_000_000, transcendentals=0),
            name="energy",
        )(place, *group, *earlier)

    groups = [(*mains[:2], near_rows(mains[:2], core), far[0])]
    logits, part = energy(0, groups[0])
    late, _ = lax.optimization_barrier((mains[2:], groups[0][3]))
    groups.append((*mains[2:], near_rows(late, core), far[1]))
    more, lse = energy(1, groups[1], part)
    logits = [logits, more]

    taps = [
        jnp.asarray(t, BF)
        for t in (
            column_taps("down", M0, W0, M1, W1),
            column_taps("down", M1, W1, M2, W2),
            column_taps("up", M2, W2, M1, W1),
            column_taps("up", M1, W1, M0, W0)[:, :M0],
        )
    ]
    details = []
    for step, flips in enumerate(((1, 3), (3, 1))):
        other = crossed(lse, flips)
        detail = pl.pallas_call(
            pyramid_kernel,
            out_shape=(
                jax.ShapeDtypeStruct((384, M0), F32),
                jax.ShapeDtypeStruct((384, W1), F32),
                jax.ShapeDtypeStruct((192, W2), F32),
            ),
            in_specs=smem() + vmem(8),
            out_specs=tuple(vmem(3)),
            scratch_shapes=[
                pltpu.VMEM((64, W0), BF),
                pltpu.VMEM((384, W0), BF),
                pltpu.VMEM((192, W1), F32),
                pltpu.VMEM((192, W1), BF),
                pltpu.VMEM((384, W2), BF),
                pltpu.VMEM((384, W1), BF),
            ],
            compiler_params=PARAMS,
            cost_estimate=pl.CostEstimate(flops=2_000_000_000, bytes_accessed=6_000_000, transcendentals=0),
            name="pyramid",
        )(place, *groups[step], *taps)
        other, *detail = lax.optimization_barrier((other, *detail))
        details += detail
        lse = join_lse(lse, other)

    left, right = pl.pallas_call(
        mix_kernel,
        out_shape=(jax.ShapeDtypeStruct((3, 32, 256), F32),) * 2,
        in_specs=smem() + vmem(13),
        out_specs=tuple(vmem(2)),
        scratch_shapes=[
            pltpu.VMEM((64, W0), F32),
            pltpu.VMEM((8, 64, W0), F32),
            pltpu.VMEM((512, W0), BF),
            pltpu.VMEM((256, W1), F32),
            pltpu.VMEM((256, W1), BF),
            pltpu.VMEM((192, W2), BF),
            pltpu.VMEM((192, W1), BF),
        ],
        compiler_params=PARAMS,
        name="mix",
    )(place, *logits, lse, *details, *taps)

    for a, b in ((1, 3), (3, 1)):
        left_in, right_in = crossed(left, (a, b)), crossed(right, (b, a))
        left, right = left + left_in, right + right_in
    whole = jnp.concatenate([left, right], axis=-1)
    joined = lax.all_to_all(jnp.broadcast_to(whole, (4, 3, 32, 512)), "x", 0, 0)
    return joined.transpose(1, 2, 0, 3).reshape(3, 32, 2048)


def solution(mesh):
    fine = Mesh(mesh.devices.reshape(4, 4, 2, 4, 4), ROWS + GZ)
    return jax.shard_map(
        on_device,
        mesh=fine,
        in_specs=(P(GZ, None, ROWS, None), P(GZ)),
        out_specs=P(None, ROWS, None),
        check_vma=False,
    )
```

```python
import functools

import jax
import jax.numpy as jnp
import numpy as np
from jax import lax
from jax.experimental import pallas as pl
from jax.experimental.pallas import tpu as pltpu
from jax.sharding import Mesh
from jax.sharding import PartitionSpec as P

ROWS = ("zl", "y", "c")
GZ = ("zh", "x")
BF = jnp.bfloat16
F32 = jnp.float32
GREY = (0.299 / 255.0, 0.587 / 255.0, 0.114 / 255.0)
W0, W1, W2 = 640, 384, 256
M0, M1, M2 = 512, 256, 128
FLIPS = (0, 2, 1, 3)
PARAMS = pltpu.CompilerParams(vmem_limit_bytes=20 * 1024 * 1024)


def lane_of(col, main, wide):
    if 0 <= col < main + 64:
        return col
    if -64 <= col < 0:
        return wide + col
    return None


def column_taps(kind, main_in, wide_in, main_out, wide_out):
    taps = np.zeros((wide_in, wide_out), np.float32)
    for lane in range(wide_out):
        col = lane if lane < main_out + 64 else lane - wide_out
        if kind == "down":
            picks = [(2 * col + d, t / 16.0) for d, t in zip(range(-2, 3), (1, 4, 6, 4, 1))]
        elif col % 2 == 0:
            picks = [(col // 2 - 1, 0.125), (col // 2, 0.75), (col // 2 + 1, 0.125)]
        else:
            picks = [(col // 2, 0.5), (col // 2 + 1, 0.5)]
        for source, tap in picks:
            at = lane_of(source, main_in, wide_in)
            if at is not None:
                taps[at, lane] += tap
    return taps


def pack_kernel(samples_ref, gain_hbm_ref, *refs):
    packed_refs, (held_ref, gain_ref, out_ref, sems, gain_sem, out_sems) = refs[:4], refs[4:]
    copies = []
    for a in range(6):
        p, c = divmod(a, 3)
        copies.append(pltpu.make_async_copy(samples_ref.at[p, c], held_ref.at[a], sems.at[a]))
        copies[a].start()
    gain_copy = pltpu.make_async_copy(gain_hbm_ref, gain_ref, gain_sem)
    gain_copy.start()
    mine = lax.axis_index("x")
    lane = lax.broadcasted_iota(jnp.int32, (16, 128), 1)
    written = []
    for m, flip in enumerate(FLIPS):
        j = mine ^ flip
        base = pl.multiple_of(512 * j, 512)
        before = pl.multiple_of(jnp.maximum(base - 128, 0), 128)
        after = pl.multiple_of(jnp.minimum(base + 512, 1920), 128)
        has_before, has_after = j > 0, j < 3
        for a in range(6):
            if m == 0:
                copies[a].wait()
            for h in range(2):
                out_ref[m, h, 16 * a : 16 * a + 16, :] = held_ref[a, 16 * h : 16 * h + 16, pl.ds(base, 512)].astype(F32)
        if m == 0:
            gain_copy.wait()
        for h in range(2):
            rows = slice(16 * h, 16 * h + 16)
            tiles = [
                jnp.zeros((16, 128), F32),
                jnp.where(lane < 64, 0.0, jnp.where(lane < 96, gain_ref[0], gain_ref[1])),
            ]
            for a in range(6):
                at, t = 32 * (a % 4), a // 4
                piece = pltpu.roll(held_ref[a, rows, pl.ds(before, 128)].astype(F32), (at - 112) % 128, 1)
                piece = jnp.where(has_before, piece, 0.0)
                tiles[t] = jnp.where((lane >= at) & (lane < at + 16), piece, tiles[t])
                piece = pltpu.roll(held_ref[a, rows, pl.ds(after, 128)].astype(F32), (at + 16) % 128, 1)
                piece = jnp.where(has_after, piece, 0.0)
                tiles[t] = jnp.where((lane >= at + 16) & (lane < at + 32), piece, tiles[t])
            out_ref[m, h, 96:104, 0:128] = tiles[0][0:8]
            out_ref[m, h, 96:104, 128:256] = tiles[1][0:8]
            out_ref[m, h, 96:104, 256:384] = tiles[0][8:16]
            out_ref[m, h, 96:104, 384:512] = tiles[1][8:16]
        written.append(pltpu.make_async_copy(out_ref.at[m], packed_refs[m], out_sems.at[m]))
        written[m].start()
    for copy in written:
        copy.wait()


class Strips:
    def __init__(self, place_ref, mains, near_ref, far_ref):
        self.even = place_ref[2] == 0
        self.mains, self.near, self.far = mains, near_ref, far_ref

    def get(self, s, b, rows, cols):
        if b in (1, 2):
            return self.mains[s][b - 1, rows, cols]
        near, far = self.near[s, rows, cols], self.far[s, rows, cols]
        return jnp.where(self.even, far, near) if b == 0 else jnp.where(self.even, near, far)

    def samples(self, s, b, a):
        return self.get(s, b, slice(16 * a, 16 * a + 16), slice(0, M0))

    def halo(self, s, b, a):
        return halo_tile(lambda cols: self.get(s, b, slice(96, 104), cols), a)


def halo_tile(read, a):
    base, at = 128 * (a // 4), 32 * (a % 4)
    tile = jnp.concatenate([read(slice(base, base + 128)), read(slice(256 + base, 384 + base))], axis=0)
    lane = lax.broadcasted_iota(jnp.int32, (16, 128), 1)
    return jnp.where((lane < 16) | (lane >= 112), pltpu.roll(tile, (112 - at) % 128, 1), 0.0)


def column_of(shape, main, wide):
    lane = lax.broadcasted_iota(jnp.int32, shape, len(shape) - 1)
    return jnp.where(lane < main + 64, lane, lane - wide)


def energy_kernel(second, place_ref, main_a_ref, main_b_ref, near_ref, far_ref, *refs):
    earlier_ref, logit_ref, lse_ref, grey_ref = refs if second else (None, refs[0], None, refs[1])
    row = lax.broadcasted_iota(jnp.int32, (64, W0), 0) + (place_ref[0] * 32 - 16)
    col = column_of((64, W0), M0, W0) + place_ref[1] * M0
    keep = (row >= 0) & (row < 1024) & (col >= 0) & (col < 2048)

    mains = (main_a_ref, main_b_ref)
    strips = Strips(place_ref, mains, near_ref, far_ref)
    for s in range(2):
        for p in range(2):
            for b in range(4):
                main = 0.0
                tile = 0.0
                for c in range(3):
                    a = 3 * p + c
                    main = main + strips.samples(s, b, a) * GREY[c]
                    tile = tile + strips.halo(s, b, a) * GREY[c]
                grey_ref[16 * b : 16 * b + 16, 0:M0] = main
                grey_ref[16 * b : 16 * b + 16, M0:W0] = tile
            grey = grey_ref[...]
            lap = (
                4.0 * grey
                - pltpu.roll(grey, 1, 0)
                - pltpu.roll(grey, 63, 0)
                - pltpu.roll(grey, 1, 1)
                - pltpu.roll(grey, W0 - 1, 1)
            )
            field = jnp.where(keep, lap * lap, 0.0)
            for axis, size in ((0, 64), (1, W0)):
                two = field + pltpu.roll(field, size - 1, axis)
                four = two + pltpu.roll(two, size - 2, axis)
                eight = four + pltpu.roll(four, size - 4, axis)
                field = pltpu.roll(eight, 4, axis) + pltpu.roll(field, size - 4, axis)
            gain = mains[s][0, 96:97, 192 + 32 * p : 193 + 32 * p]
            logit_ref[2 * s + p] = gain * field

    if second:
        logits = [ref.at[i] for ref in (earlier_ref, logit_ref) for i in range(4)]
        peak = logits[0][...]
        for ref in logits[1:]:
            peak = jnp.maximum(peak, ref[...])
        total = 0.0
        for ref in logits:
            total = total + jnp.exp(ref[...] - peak)
        lse = pltpu.roll(peak + jnp.log(total), 58, 0)[0:56]
        lane = lax.broadcasted_iota(jnp.int32, (8, 128), 1)
        shared = [jnp.zeros((8, 128), F32)] * 2
        for i in range(7):
            rows = slice(8 * i, 8 * i + 8)
            for j in range(4):
                lse_ref[4 * i + j] = lse[rows, 128 * j : 128 * j + 128]
            at = 32 * (i % 4)
            piece = pltpu.roll(lse[rows, M0:W0], (16 + at) % 128, 1)
            shared[i // 4] = jnp.where((lane >= at) & (lane < at + 32), piece, shared[i // 4])
        lse_ref[28] = shared[0]
        lse_ref[29] = shared[1]


def split2(value):
    high = value.astype(BF)
    low = (value - high.astype(F32)).astype(BF)
    return high, low


def stacked(value):
    return jnp.concatenate(split2(value), axis=0)


def dot(a, b):
    return jnp.dot(a, b, preferred_element_type=F32)


def iota2(shape):
    return lax.broadcasted_iota(jnp.int32, shape, 0), lax.broadcasted_iota(jnp.int32, shape, 1)


def down_rows(count, inputs, copies, first, limit):
    q, e = iota2((count, inputs * copies))
    if copies == 2:
        e = jnp.where(e >= inputs, e - inputs, e)
    gap = jnp.abs(e - 2 * q)
    taps = jnp.where(gap == 0, 0.375, jnp.where(gap == 1, 0.25, jnp.where(gap == 2, 0.0625, 0.0)))
    inside = (q + first >= 0) & (q + first < limit)
    return jnp.where(inside, taps, 0.0).astype(BF)


def up_rows(count, inputs, offset, first, limit):
    r, q = iota2((count, 2 * inputs))
    q = jnp.where(q >= inputs, q - inputs, q)
    gap = jnp.abs(2 * q - (r + offset))
    even = (r & 1) == 0
    taps = jnp.where(
        even,
        jnp.where(gap == 0, 0.75, jnp.where(gap == 2, 0.125, 0.0)),
        jnp.where(gap == 1, 0.5, 0.0),
    )
    inside = (r + first >= 0) & (r + first < limit)
    return jnp.where(inside, taps, 0.0).astype(BF)


def row_matrices(strip):
    v2 = down_rows(16, 32, 2, strip * 8 - 4, 256)
    p2 = up_rows(32, 16, 0, strip * 16 - 8, 512)
    p1 = up_rows(32, 32, 16, 0, 32)
    return v2, p2, p1


def level_masks(rows1, rows2, k):
    col1 = column_of((rows1, W1), M1, W1) + k * M1
    col2 = column_of((rows2, W2), M2, W2) + k * M2
    return (col1 >= 0) & (col1 < 1024), (col2 >= 0) & (col2 < 512)


def put(ref, n, a, count, value):
    high, low = split2(value)
    ref[a * count : (a + 1) * count] = high
    ref[(n + a) * count : (n + a + 1) * count] = low


def resampled(source_ref, taps_ref):
    both = dot(source_ref[...], taps_ref[...])
    half = both.shape[0] // 2
    return both[:half] + both[half:]


def pyramid_kernel(
    place_ref, main_a_ref, main_b_ref, near_ref, far_ref, d1_ref, d2_ref, u2_ref, u1_ref,
    detail0_ref, detail1_ref, l2_ref, x_ref, s1_ref, l1_ref, s2_ref, s3_ref, s4_ref,
):
    strip = place_ref[0]
    v1 = down_rows(32, 64, 1, strip * 16 - 8, 512)
    v2, p2, p1 = row_matrices(strip)
    inside1, inside2 = level_masks(192, 96, place_ref[1])
    mains = (main_a_ref, main_b_ref)
    strips = Strips(place_ref, mains, near_ref, far_ref)
    for i in range(2):
        for a in range(6):
            for b in range(4):
                x_ref[16 * b : 16 * b + 16, 0:M0] = strips.samples(i, b, a).astype(BF)
                x_ref[16 * b : 16 * b + 16, M0:W0] = strips.halo(i, b, a).astype(BF)
            put(s1_ref, 6, a, 32, dot(v1, x_ref[...]))
        l1_ref[...] = jnp.where(inside1, resampled(s1_ref, d1_ref), 0.0)
        for a in range(6):
            both = stacked(l1_ref[a * 32 : a * 32 + 32])
            put(s2_ref, 6, a, 16, dot(v2, both))
            put(s4_ref, 6, a, 32, dot(p1, both))
        l2 = jnp.where(inside2, resampled(s2_ref, d2_ref), 0.0)
        l2_ref[i * 96 : i * 96 + 96] = l2
        for a in range(6):
            put(s3_ref, 6, a, 32, dot(p2, stacked(l2[a * 16 : a * 16 + 16])))
        detail1_ref[i * 192 : i * 192 + 192] = l1_ref[...] - resampled(s3_ref, u2_ref)
        part = resampled(s4_ref, u1_ref)
        for a in range(6):
            for h in range(2):
                at = a * 32 + 16 * h
                detail0_ref[i * 192 + at : i * 192 + at + 16] = (
                    mains[i][h, 16 * a : 16 * a + 16, :] - part[at : at + 16]
                )


def mix_kernel(
    place_ref, logit_a_ref, logit_b_ref, lse_ref,
    fine_a_ref, mid_a_ref, low_a_ref, fine_b_ref, mid_b_ref, low_b_ref,
    d1_ref, d2_ref, u2_ref, u1_ref,
    left_ref, right_ref, tiles_ref, w0_ref, s1_ref, w1_ref, s2_ref, s3_ref, s4_ref,
):
    strip, k = place_ref[0], place_ref[1]
    v1 = down_rows(32, 64, 2, strip * 16 - 8, 512)
    v2, p2, p1 = row_matrices(strip)
    col = column_of((16, W0), M0, W0)
    inside_col = (col >= -10) & (col <= 522) & (col + k * M0 >= 0) & (col + k * M0 < 2048)
    row = lax.broadcasted_iota(jnp.int32, (16, W0), 0)
    for i in range(7):
        rows = slice(8 * i, 8 * i + 8)
        for j in range(4):
            tiles_ref[rows, 128 * j : 128 * j + 128] = lse_ref[4 * i + j]
        tiles_ref[rows, M0:W0] = pltpu.roll(lse_ref[28 + i // 4], (112 - 32 * (i % 4)) % 128, 1)
    tiles_ref[56:64] = jnp.zeros((8, W0), F32)
    lse = pltpu.roll(tiles_ref[...], 6, 0)
    keeps = []
    for b in range(4):
        r = row + (16 * b - 16)
        g = r + strip * 32
        keeps.append(inside_col & (r >= -10) & (r <= 42) & (g >= 0) & (g < 1024))
    for i in range(8):
        logit_ref = (logit_a_ref, logit_b_ref)[i // 4]
        for b in range(4):
            rows = slice(16 * b, 16 * b + 16)
            w0_ref[i, rows] = jnp.where(keeps[b], jnp.exp(logit_ref[i % 4, rows] - lse[rows]), 0.0)
        put(s1_ref, 8, i, 32, dot(v1, stacked(w0_ref[i])))
    inside1, inside2 = level_masks(32, 16, k)
    w1_ref[...] = resampled(s1_ref, d1_ref)
    for i in range(8):
        w1 = jnp.where(inside1, w1_ref[i * 32 : i * 32 + 32], 0.0)
        w1_ref[i * 32 : i * 32 + 32] = w1
        put(s2_ref, 8, i, 16, dot(v2, stacked(w1)))
    w2 = resampled(s2_ref, d2_ref)

    def piece(pair, i, c, rows):
        ref = pair[i // 4]
        at = ((i % 4) * 3 + c) * rows
        return ref[at : at + rows]

    for c in range(3):
        blend2 = 0.0
        for i in range(8):
            blend2 = blend2 + w2[i * 16 : i * 16 + 16] * piece((low_a_ref, low_b_ref), i, c, 16)
        put(s3_ref, 3, c, 32, dot(p2, stacked(blend2)))
    rise = resampled(s3_ref, u2_ref)
    for c in range(3):
        total = jnp.where(inside1, rise[c * 32 : c * 32 + 32], 0.0)
        for i in range(8):
            total = total + w1_ref[i * 32 : i * 32 + 32] * piece((mid_a_ref, mid_b_ref), i, c, 32)
        put(s4_ref, 3, c, 32, dot(p1, stacked(total)))
    rise = resampled(s4_ref, u1_ref)
    for c in range(3):
        total = rise[c * 32 : c * 32 + 32]
        for i in range(8):
            total = total + w0_ref[i, 16:48, 0:M0] * piece((fine_a_ref, fine_b_ref), i, c, 32)
        total = total * (1.0 / 255.0)
        left_ref[c] = total[:, :256]
        right_ref[c] = total[:, 256:]


def vmem(count):
    return [pl.BlockSpec(memory_space=pltpu.VMEM)] * count


def smem():
    return [pl.BlockSpec(memory_space=pltpu.SMEM)]


def half(group, index):
    return jnp.stack([lax.dynamic_index_in_dim(main, index, axis=0, keepdims=False) for main in group])


def near_rows(group, core):
    return lax.ppermute(half(group, 1 - core), "c", [(0, 1), (1, 0)])


def far_rows(group, core):
    count = lax.axis_size(ROWS)
    swaps = [(i, i + 1) for i in range(1, count - 1, 2)]
    swaps += [(b, a) for a, b in swaps]
    return lax.ppermute(half(group, core), ROWS, swaps)


def crossed(value, flips):
    pairs = [(4 * c + i, 4 * c + (i ^ flip)) for c, flip in enumerate(flips) for i in range(4)]
    return lax.ppermute(value, ("c", "zh"), pairs)


def woven(value, flips):
    pairs = [
        (8 * low + 4 * c + i, 8 * low + 4 * c + (i ^ flips[(low + c) % 2]))
        for low in range(4) for c in range(2) for i in range(4)
    ]
    return lax.ppermute(value, ("zl", "c", "zh"), pairs)


def join_lse(a, b):
    return jnp.maximum(a, b) + jnp.log(1.0 + jnp.exp(-jnp.abs(a - b)))


def on_device(samples, gain):
    samples, strip, column, core = lax.optimization_barrier(
        (samples, lax.axis_index(ROWS), lax.axis_index("x"), lax.axis_index("c"))
    )
    packed = pl.pallas_call(
        pack_kernel,
        out_shape=(jax.ShapeDtypeStruct((2, 104, 512), F32),) * 4,
        in_specs=[pl.BlockSpec(memory_space=pltpu.HBM)] * 2,
        out_specs=(pl.BlockSpec(memory_space=pltpu.HBM),) * 4,
        scratch_shapes=[
            pltpu.VMEM((6, 32, 2048), jnp.int32),
            pltpu.SMEM((2,), F32),
            pltpu.VMEM((4, 2, 104, 512), F32),
            pltpu.SemaphoreType.DMA((6,)),
            pltpu.SemaphoreType.DMA,
            pltpu.SemaphoreType.DMA((4,)),
        ],
        compiler_params=pltpu.CompilerParams(vmem_limit_bytes=60 * 1024 * 1024),
        name="pack",
    )(samples, gain)
    mains = [packed[0]] + [
        lax.ppermute(packed[m], "x", [(i, i ^ FLIPS[m]) for i in range(4)]) for m in (1, 2, 3)
    ]
    place = jnp.stack([strip, column, core]).astype(jnp.int32)
    far = [far_rows(pair, core) for pair in (mains[:2], mains[2:])]
    logit_shape = jax.ShapeDtypeStruct((4, 64, W0), F32)

    def energy(step, group, *earlier):
        return pl.pallas_call(
            functools.partial(energy_kernel, step == 1),
            out_shape=(logit_shape,) + (jax.ShapeDtypeStruct((30, 8, 128), F32),) * step,
            in_specs=smem() + vmem(4 + step),
            out_specs=tuple(vmem(1 + step)),
            scratch_shapes=[pltpu.VMEM((64, W0), F32)],
            compiler_params=PARAMS,
            cost_estimate=pl.CostEstimate(flops=2_000_000_000, bytes_accessed=6_000_000, transcendentals=0),
            name="energy",
        )(place, *group, *earlier)

    groups = [(*mains[:2], near_rows(mains[:2], core), far[0])]
    logits = energy(0, groups[0])
    late, _ = lax.optimization_barrier((mains[2:], groups[0][3]))
    groups.append((*mains[2:], near_rows(late, core), far[1]))
    *more, lse = energy(1, groups[1], *logits)
    logits = [*logits, *more]

    taps = [
        jnp.asarray(t, BF)
        for t in (
            column_taps("down", M0, W0, M1, W1),
            column_taps("down", M1, W1, M2, W2),
            column_taps("up", M2, W2, M1, W1),
            column_taps("up", M1, W1, M0, W0)[:, :M0],
        )
    ]
    details = []
    for step, flips in enumerate(((1, 3), (3, 1))):
        other = crossed(lse, flips)
        detail = pl.pallas_call(
            pyramid_kernel,
            out_shape=(
                jax.ShapeDtypeStruct((384, M0), F32),
                jax.ShapeDtypeStruct((384, W1), F32),
                jax.ShapeDtypeStruct((192, W2), F32),
            ),
            in_specs=smem() + vmem(8),
            out_specs=tuple(vmem(3)),
            scratch_shapes=[
                pltpu.VMEM((64, W0), BF),
                pltpu.VMEM((384, W0), BF),
                pltpu.VMEM((192, W1), F32),
                pltpu.VMEM((192, W1), BF),
                pltpu.VMEM((384, W2), BF),
                pltpu.VMEM((384, W1), BF),
            ],
            compiler_params=PARAMS,
            cost_estimate=pl.CostEstimate(flops=2_000_000_000, bytes_accessed=6_000_000, transcendentals=0),
            name="pyramid",
        )(place, *groups[step], *taps)
        other, *detail = lax.optimization_barrier((other, *detail))
        details += detail
        lse = join_lse(lse, other)

    left, right = pl.pallas_call(
        mix_kernel,
        out_shape=(jax.ShapeDtypeStruct((3, 32, 256), F32),) * 2,
        in_specs=smem() + vmem(13),
        out_specs=tuple(vmem(2)),
        scratch_shapes=[
            pltpu.VMEM((64, W0), F32),
            pltpu.VMEM((8, 64, W0), F32),
            pltpu.VMEM((512, W0), BF),
            pltpu.VMEM((256, W1), F32),
            pltpu.VMEM((256, W1), BF),
            pltpu.VMEM((192, W2), BF),
            pltpu.VMEM((192, W1), BF),
        ],
        compiler_params=PARAMS,
        name="mix",
    )(place, *logits, lse, *details, *taps)

    for a, b in ((1, 3), (3, 1)):
        left_in, right_in = woven(left, (a, b)), woven(right, (b, a))
        left, right = left + left_in, right + right_in
    whole = jnp.concatenate([left, right], axis=-1)
    joined = lax.all_to_all(jnp.broadcast_to(whole, (4, 3, 32, 512)), "x", 0, 0)
    return joined.transpose(1, 2, 0, 3).reshape(3, 32, 2048)


def solution(mesh):
    fine = Mesh(mesh.devices.reshape(4, 4, 2, 4, 4), ROWS + GZ)
    return jax.shard_map(
        on_device,
        mesh=fine,
        in_specs=(P(GZ, None, ROWS, None), P(GZ)),
        out_specs=P(None, ROWS, None),
        check_vma=False,
    )
```
